128 devices in a mesh: lat: 16 (over z, x_lo, core), lon: 8 (over x_hi, y).
Axes of the slice: x: 4 (x_hi: 2, x_lo: 2; x = x_hi * 2 + x_lo), y: 4, z: 4, core: 2. Of those that a mesh axis runs over, the one named last changes fastest.
Arguments:
- increments: float32 [48, 768, 3072], P(None, 'lat', 'lon'), may hold values from -6 to 6
- lengths: float32 [48, 3], replicated, may hold values from 0.6 to 40, as said below
- weights: float32 [48, 3], replicated, may hold values from 0.3 to 1
Outputs:
- control: float32 [48, 768, 3072], P(None, 'lat', 'lon')
The draws below stay inside these ranges and needn't reach their ends.
Inputs may be any that keep to these rules, and one draw needn't show every extreme that they name: Column 0 of lengths lies in 0.6 to 1.5, column 1 in 4 to 10, column 2 in 16 to 40 grid cells.
All inputs are finite; a program needn't handle non-finite values.
Results may differ from the reference program's by a relative error of at most 0.0001.
Values sent between devices are 32-bit elements; how exact they have to be, the bound alone decides.
No kernel may reach another device: no remote copies, remote signals or barrier semaphores. Data moves between devices by JAX's collectives and lax.ppermute only.
A program may use at most 192 MiB of HBM per device.

```python
import math
import jax
import jax.numpy as jnp
from jax import lax

GLAT = 768
GLON = 3072
LEVELS = 8
SCALES = 3
BLOCK = 256
FIELDS = 48


def draw_increments(key, part):
    key = jax.random.fold_in(key, 11)
    shape = (FIELDS, GLAT, GLON)
    return jax.random.truncated_normal(key, -6.0, 6.0, shape, jnp.float32)


def draw_lengths(key, part):
    key = jax.random.fold_in(key, 23)
    factor = jnp.exp(jax.random.uniform(key, (FIELDS, SCALES), jnp.float32, 0.0, math.log(2.5)))
    base_length = jnp.array([0.6, 4.0, 16.0], jnp.float32)
    return factor * base_length[None, :]


def setup_inputs(seed: int = 0) -> dict:
    key_list = jax.random.split(jax.random.key(seed), 4)
    return {
        "increments": draw_increments(jax.random.fold_in(key_list[3], 71), 0),
        "lengths": draw_lengths(jax.random.fold_in(key_list[3], 71), 0),
        "weights": jnp.clip(jnp.exp(jax.random.uniform(key_list[2], (FIELDS, SCALES), jnp.float32, math.log(0.3), math.log(1.0))), 0.3, 1.0),
    }


precise_mode = lax.Precision.HIGHEST


def line_tables(decay_rate, block_width, block_count):
    offsets = jnp.arange(block_width, dtype=jnp.float32)
    offset_gap = offsets[:, None] - offsets[None, :]
    inside = offset_gap >= 0
    rate_grid = decay_rate[..., None, None]
    leakage = -jnp.expm1(-rate_grid)
    lower_matrix = jnp.where(inside, leakage * jnp.exp(-rate_grid * jnp.where(inside, offset_gap, 0.0)), 0.0)
    block_steps = jnp.arange(block_count, dtype=jnp.float32)
    block_gap = block_steps[:, None] - block_steps[None, :]
    block_inside = block_gap >= 0
    carry_matrix = jnp.where(block_inside, jnp.exp(-rate_grid * block_width * jnp.where(block_inside, block_gap, 0.0)), 0.0)
    rise_powers = jnp.exp(-decay_rate[..., None] * (offsets + 1.0))
    fall_powers = jnp.exp(-decay_rate[..., None] * (block_width - offsets))
    return lower_matrix, carry_matrix, rise_powers, fall_powers


def filter_last(stack, decay_rate, block_width):
    fields, across, length = stack.shape
    block_count = length // block_width
    lower_matrix, carry_matrix, rise_powers, fall_powers = line_tables(decay_rate, block_width, block_count)
    blocks = stack.reshape(fields, across, block_count, block_width)
    block_local = jnp.einsum('fij,fakj->faki', lower_matrix, blocks, precision=precise_mode)
    block_ends = jnp.einsum('fkm,fam->fak', carry_matrix, block_local[..., block_width - 1], precision=precise_mode)
    before = jnp.concatenate([jnp.zeros_like(block_ends[..., :1]), block_ends[..., :-1]], axis=2)
    forward_pass = block_local + before[..., None] * rise_powers[:, None, None, :]
    block_local = jnp.einsum('fji,fakj->faki', lower_matrix, forward_pass, precision=precise_mode)
    block_starts = jnp.einsum('fmk,fam->fak', carry_matrix, block_local[..., 0], precision=precise_mode)
    following = jnp.concatenate([block_starts[..., 1:], jnp.zeros_like(block_starts[..., :1])], axis=2)
    backward_pass = block_local + following[..., None] * fall_powers[:, None, None, :]
    return backward_pass.reshape(fields, across, length)


def filter_mid(stack, decay_rate, block_width):
    fields, length, across = stack.shape
    block_count = length // block_width
    lower_matrix, carry_matrix, rise_powers, fall_powers = line_tables(decay_rate, block_width, block_count)
    blocks = stack.reshape(fields, block_count, block_width, across)
    block_local = jnp.einsum('fij,fkja->fkia', lower_matrix, blocks, precision=precise_mode)
    block_ends = jnp.einsum('fkm,fma->fka', carry_matrix, block_local[:, :, block_width - 1, :], precision=precise_mode)
    before = jnp.concatenate([jnp.zeros_like(block_ends[:, :1]), block_ends[:, :-1]], axis=1)
    forward_pass = block_local + before[:, :, None, :] * rise_powers[:, None, :, None]
    block_local = jnp.einsum('fji,fkja->fkia', lower_matrix, forward_pass, precision=precise_mode)
    block_starts = jnp.einsum('fmk,fma->fka', carry_matrix, block_local[:, :, 0, :], precision=precise_mode)
    following = jnp.concatenate([block_starts[:, 1:], jnp.zeros_like(block_starts[:, :1])], axis=1)
    backward_pass = block_local + following[:, :, None, :] * fall_powers[:, None, :, None]
    return backward_pass.reshape(fields, length, across)


def scale_coefficients(lengths, weights):
    decay_rate = 1.0 / lengths
    decay = jnp.exp(-decay_rate)
    leakage = -jnp.expm1(-decay_rate)
    coefficient = weights * (1.0 + decay) ** 3 / (leakage * (1.0 + decay * decay))
    return decay_rate, coefficient


def wind_adjoint(increments, levels):
    eastward = increments[:levels]
    northward = increments[levels:2 * levels]

    def along_rows(field):
        padded = jnp.pad(field, ((0, 0), (1, 1), (0, 0)))
        return 0.5 * (padded[:, 2:, :] - padded[:, :-2, :])

    def along_columns(field):
        return 0.5 * (jnp.roll(field, -1, axis=2) - jnp.roll(field, 1, axis=2))

    stream = along_rows(eastward) - along_columns(northward)
    potential = -along_columns(eastward) - along_rows(northward)
    return jnp.concatenate([stream, potential, increments[2 * levels:]], axis=0)


def reference(increments, lengths, weights):
    adjoint = wind_adjoint(increments, LEVELS)
    decay_rate, coefficient = scale_coefficients(lengths, weights)

    def one_field(item):
        field, rate_row, coef_row = item
        summed = jnp.zeros_like(field)
        for scale_index in range(SCALES):
            single_rate = rate_row[scale_index][None]
            along = filter_last(field[None], single_rate, BLOCK)
            filtered = filter_mid(along, single_rate, BLOCK)
            summed = summed + coef_row[scale_index] * filtered[0]
        return summed

    return lax.map(one_field, (adjoint, decay_rate, coefficient))
```

```python
import functools

import jax
import jax.numpy as jnp
from jax import lax
from jax.experimental import pallas as pl
from jax.experimental.pallas import tpu as pltpu
from jax.sharding import PartitionSpec as P

LEVELS = 8
SCALES = 3
WINDS = 16
FIELDS = 48
ROWS = 48
COLS = 384
GROUP = 8
GROUPS = FIELDS // GROUP
NLAT = 16
NLON = 8
LANES = 128
PARTS = COLS // LANES
HALF = FIELDS // 2
HALF_ROWS = SCALES * HALF
F32 = jnp.float32
BF16 = jnp.bfloat16

VMEM = pl.BlockSpec(memory_space=pltpu.VMEM)
SMEM = pl.BlockSpec(memory_space=pltpu.SMEM)
BIG = 48 * 1024 * 1024


def params(**kw):
    return pltpu.CompilerParams(vmem_limit_bytes=BIG, **kw)


def iota(shape, dim):
    return lax.broadcasted_iota(jnp.int32, shape, dim)


def fiota(shape, dim):
    return iota(shape, dim).astype(F32)


def split(value):
    high = value.astype(BF16)
    return high, (value - high.astype(F32)).astype(BF16)


def mm(a, b):
    return jnp.dot(a, b, preferred_element_type=F32)


def lane_fields(shape):
    lane = iota(shape, 1)
    virtual = lane & 31
    wind_field = ((virtual >> 4) << 3) + (virtual & 7)
    return lane, lane >> 5, virtual, wind_field, virtual + WINDS


def lane_rates(lengths):
    rate = 1.0 / lengths
    shape = (FIELDS, LANES)
    lane, scale, _, wind_field, rest_field = lane_fields(shape)
    value = jnp.where(scale == 0, rate[:, 0:1], jnp.where(scale == 1, rate[:, 1:2], rate[:, 2:3]))
    field = iota(shape, 0)
    pick = lambda which: jnp.sum(jnp.where(field == which, value, 0.0), axis=0, keepdims=True)
    used = lane[:1] < 96
    return jnp.where(used, pick(wind_field), 1.0), jnp.where(used, pick(rest_field), 1.0)


def lane_kinds(shape):
    _, _, virtual, _, _ = lane_fields(shape)
    second = virtual >= 16
    north = (virtual & 15) >= 8
    zonal = second != north
    sign = jnp.where(second | north, -1.0, 1.0).astype(F32)
    return zonal, sign


def row_sums_kernel(where_ref, len_ref, x_ref, sums_ref, edge_ref, high_ref, low_ref):
    group = pl.program_id(0)
    lon = where_ref[1]

    @pl.when(group == 0)
    def _():
        rate0, rate1 = lane_rates(len_ref[...])
        column = fiota((COLS, LANES), 0)
        for tile, rate in enumerate((rate0, rate1)):
            for side, steps in enumerate((COLS - 1 - column, column)):
                high, low = split(jnp.exp(-rate * steps))
                high_ref[tile, :, side * LANES:(side + 1) * LANES] = high
                low_ref[tile, :, side * LANES:(side + 1) * LANES] = low
        sums_ref[...] = jnp.zeros_like(sums_ref)
        edge_ref[...] = jnp.zeros_like(edge_ref)

    x = x_ref[...].reshape(GROUP * ROWS, COLS)
    xh, xl = split(x)
    tile = jnp.where(group < 2, 0, 1)
    wh = high_ref[tile]
    wl = low_ref[tile]
    res = mm(xh, wh) + mm(xl, wh) + mm(xh, wl)
    lane = iota((ROWS, LANES), 1)
    virtual = lane & 31

    @pl.when(group < 2)
    def _():
        left, right = sums_ref[:, 0:128], sums_ref[:, 128:256]
        first, last = edge_ref[:, 0:128], edge_ref[:, 128:256]
        for i in range(GROUP):
            mine = (virtual & 15) == group * GROUP + i
            rows = slice(i * ROWS, (i + 1) * ROWS)
            left = jnp.where(mine, res[rows, 0:128], left)
            right = jnp.where(mine, res[rows, 128:256], right)
            first = jnp.where(mine, x[rows, 0:1], first)
            last = jnp.where(mine, x[rows, COLS - 1:COLS], last)
        sums_ref[:, 0:128] = left
        sums_ref[:, 128:256] = right
        sums_ref[:, 256:384] = jnp.where(lon == 0, first, jnp.where(lon == NLON - 1, last, 0.0))
        edge_ref[:, 0:128] = first
        edge_ref[:, 128:256] = last

    @pl.when(group >= 2)
    def _():
        left, right = sums_ref[:, 384:512], sums_ref[:, 512:640]
        for i in range(GROUP):
            mine = virtual == (group - 2) * GROUP + i
            rows = slice(i * ROWS, (i + 1) * ROWS)
            left = jnp.where(mine, res[rows, 0:128], left)
            right = jnp.where(mine, res[rows, 128:256], right)
        sums_ref[:, 384:512] = left
        sums_ref[:, 512:640] = right


def row_sums(where, lengths, x):
    return pl.pallas_call(
        row_sums_kernel,
        grid=(GROUPS,),
        in_specs=[SMEM, pl.BlockSpec((FIELDS, SCALES), lambda g: (0, 0)),
                  pl.BlockSpec((GROUP, ROWS, COLS), lambda g: (g, 0, 0))],
        out_specs=[pl.BlockSpec((ROWS, 640), lambda g: (0, 0)), pl.BlockSpec((ROWS, 256), lambda g: (0, 0))],
        out_shape=[jax.ShapeDtypeStruct((ROWS, 640), F32), jax.ShapeDtypeStruct((ROWS, 256), F32)],
        scratch_shapes=[pltpu.VMEM((2, COLS, 256), BF16), pltpu.VMEM((2, COLS, 256), BF16)],
        compiler_params=params(),
        name="row_sums",
    )(where, lengths, x)


def zonal_difference(x):
    shape = x.shape
    axis = len(shape) - 1
    column = iota(shape, axis)
    ahead = jnp.where(column == COLS - 1, 0.0, pltpu.roll(x, COLS - 1, axis))
    behind = jnp.where(column == 0, 0.0, pltpu.roll(x, 1, axis))
    return 0.5 * (ahead - behind)


def local_sums_kernel(where_ref, len_ref, x1_ref, x2_ref, out_ref, acc_ref):
    group = pl.program_id(0)
    top = where_ref[0] == 0
    rate = 1.0 / len_ref[...]
    row_rate = jnp.concatenate([rate[:, s:s + 1] for _ in range(2) for s in range(SCALES)], axis=0)
    shape = (2 * SCALES * GROUP, ROWS)
    out_row = iota(shape, 0)
    member = out_row & 7
    left_side = out_row < SCALES * GROUP
    row = fiota(shape, 1)
    plain = jnp.exp(-row_rate * jnp.where(left_side, ROWS - 1 - row, row))

    def weighted(matrix, x, i):
        mh, ml = split(jnp.where(member == i, matrix, 0.0))
        xh, xl = split(x)
        return mm(mh, xh) + mm(mh, xl) + mm(ml, xh)

    @pl.when(group < 2)
    def _():
        decay = jnp.exp(-row_rate)
        gain = 0.5 * (1.0 - decay * decay) / decay
        start = jnp.where(top & (row == 0.0), 0.5 * jnp.exp(-row_rate * ROWS), 0.0)
        slope = jnp.where(left_side, -gain * plain - start, gain * plain)
        second_sign = jnp.where(group == 0, 1.0, -1.0)
        acc = jnp.zeros((2 * SCALES * GROUP, COLS), F32)
        for i in range(GROUP):
            acc += weighted(plain, -zonal_difference(x2_ref[i]), i)
            acc += weighted(slope, second_sign * x1_ref[i], i)
        acc_ref[...] = acc

    @pl.when(group >= 2)
    def _():
        acc = jnp.zeros((2 * SCALES * GROUP, COLS), F32)
        for i in range(GROUP):
            acc += weighted(plain, x1_ref[i], i)
        acc_ref[...] = acc

    acc = acc_ref[...]
    column = iota(acc.shape, 1)
    forward, backward = acc, acc
    factor = jnp.exp(-row_rate)
    step = 1
    while step < COLS:
        forward = forward + factor * jnp.where(column >= step, pltpu.roll(forward, step, 1), 0.0)
        backward = backward + factor * jnp.where(column < COLS - step, pltpu.roll(backward, COLS - step, 1), 0.0)
        factor = factor * factor
        step *= 2
    acc = forward + backward - acc
    for side in range(2):
        for s in range(SCALES):
            k = side * SCALES + s
            out_ref[0, side, s, 0] = acc[k * GROUP:(k + 1) * GROUP]


def other_wind(g):
    return jnp.where(g < 2, 1 - g, 0)


def local_sums(where, lengths, x):
    out = pl.pallas_call(
        local_sums_kernel,
        grid=(GROUPS,),
        in_specs=[SMEM, pl.BlockSpec((GROUP, SCALES), lambda g: (g, 0)),
                  pl.BlockSpec((GROUP, ROWS, COLS), lambda g: (g, 0, 0)),
                  pl.BlockSpec((GROUP, ROWS, COLS), lambda g: (other_wind(g), 0, 0))],
        out_specs=pl.BlockSpec((1, 2, SCALES, 1, GROUP, COLS), lambda g: (g // 3, 0, 0, g % 3, 0, 0)),
        out_shape=jax.ShapeDtypeStruct((2, 2, SCALES, 3, GROUP, COLS), F32),
        scratch_shapes=[pltpu.VMEM((2 * SCALES * GROUP, COLS), F32)],
        compiler_params=params(),
        name="local_sums",
    )(where, lengths, x, x)
    return out.reshape(2, 2 * HALF_ROWS, COLS)


def lon_merge_kernel(where_ref, len_ref, own_ref, g1_ref, g2_ref, g3_ref, part_ref, mine_ref):
    y = where_ref[1] & 3
    yf = y.astype(F32)
    rates = lane_rates(len_ref[...])
    got = (g1_ref, g2_ref, g3_ref)
    for tile in range(2):
        step = lambda n: jnp.exp(-rates[tile] * (COLS * n))
        base = tile * 384
        lanes_l = slice(base, base + 128)
        lanes_r = slice(base + 128, base + 256)
        left_total = step(3.0 - yf) * own_ref[:, lanes_l]
        right_total = step(yf) * own_ref[:, lanes_r]
        left = jnp.zeros((ROWS, LANES), F32)
        right = jnp.zeros((ROWS, LANES), F32)
        for d, ref in zip((1, 2, 3), got):
            below = y >= d
            lg, rg = ref[:, lanes_l], ref[:, lanes_r]
            left = left + jnp.where(below, step(d - 1.0), 0.0) * lg
            right = right + jnp.where(below, 0.0, step(3.0 - d)) * rg
            other = jnp.where(below, yf - d, yf - d + 4.0)
            left_total = left_total + step(3.0 - other) * lg
            right_total = right_total + step(other) * rg
        part_ref[:, tile * 256:tile * 256 + 128] = left
        part_ref[:, tile * 256 + 128:tile * 256 + 256] = right
        mine_ref[:, lanes_l] = left_total
        mine_ref[:, lanes_r] = right_total
    edge = slice(256, 384)
    mine_ref[:, edge] = own_ref[:, edge] + g1_ref[:, edge] + g2_ref[:, edge] + g3_ref[:, edge]


def lon_merge(where, lengths, own, got):
    return pl.pallas_call(
        lon_merge_kernel,
        in_specs=[SMEM] + [VMEM] * 5,
        out_specs=[VMEM, VMEM],
        out_shape=[jax.ShapeDtypeStruct((ROWS, 512), F32), jax.ShapeDtypeStruct((ROWS, 640), F32)],
        compiler_params=params(),
        name="lon_merge",
    )(where, lengths, own, *got)


def column_sums_kernel(where_ref, len_ref, part_ref, mine_ref, theirs_ref, edge_ref, local_ref,
                       carry_ref, keep_ref, send_ref):
    lat, lon = where_ref[0], where_ref[1]
    y = lon & 3
    yf = y.astype(F32)
    high = lon >= 4
    highf = jnp.where(high, 1.0, 0.0)
    lowf = 1.0 - highf
    lonf = lon.astype(F32)
    top = lat == 0
    rates = lane_rates(len_ref[...])
    zonal, sign = lane_kinds((1, LANES))
    row = fiota((ROWS, LANES), 0)
    weights = []
    for tile in range(2):
        rate = rates[tile]
        step = lambda n: jnp.exp(-rate * (COLS * n))
        decay = jnp.exp(-rate)
        base = tile * 384
        lanes_l = slice(base, base + 128)
        lanes_r = slice(base + 128, base + 256)
        left = part_ref[:, tile * 256:tile * 256 + 128] + (highf * step(yf)) * theirs_ref[:, lanes_l]
        right = part_ref[:, tile * 256 + 128:tile * 256 + 256] + (lowf * step(3.0 - yf)) * theirs_ref[:, lanes_r]
        whole = ((highf + lowf * step(4.0)) * mine_ref[:, lanes_l]
                 + (lowf + highf * step(4.0)) * theirs_ref[:, lanes_l])
        end = step(7.0 - lonf)
        weight_l = jnp.exp(-rate * (ROWS - 1 - row))
        weight_r = jnp.exp(-rate * row)
        carry_l = left
        carry_r = right - (end * decay) * whole
        if tile == 0:
            v0 = lowf * mine_ref[:, 256:384] + highf * theirs_ref[:, 256:384]
            vn = highf * mine_ref[:, 256:384] + lowf * theirs_ref[:, 256:384]
            gain = 0.5 * (1.0 - decay * decay) / decay
            initial = -0.5 * (v0 + vn / decay)
            zonal_l = step(lonf) * initial - gain * left + 0.5 * edge_ref[:, 0:128]
            zonal_r = (gain * right - 0.5 * edge_ref[:, 128:256]
                       + end * (gain * v0 - decay * (step(8.0) * initial - gain * whole)))
            carry_l = sign * jnp.where(zonal, zonal_l, carry_l)
            carry_r = sign * jnp.where(zonal, zonal_r, carry_r)
            start = jnp.where(top & (row == 0.0), 0.5 * jnp.exp(-rate * ROWS), 0.0)
            weight_l = jnp.where(zonal, weight_l, -gain * weight_l - start)
            weight_r = jnp.where(zonal, weight_r, gain * weight_r)
        carry_ref[:, tile * 256:tile * 256 + 128] = carry_l
        carry_ref[:, tile * 256 + 128:tile * 256 + 256] = carry_r
        fold = lambda w, c: jnp.sum(w * c, axis=0, keepdims=True)
        weights.append(((fold(weight_l, carry_l), fold(weight_l, carry_r)),
                        (fold(weight_r, carry_l), fold(weight_r, carry_r))))
    shape = (HALF_ROWS, LANES)
    lane, lane_scale, _, wind_field, rest_field = lane_fields(shape)
    out_row = iota(shape, 0)
    scale = jnp.where(out_row < HALF, 0, jnp.where(out_row < 2 * HALF, 1, 2))
    core = lat & 1
    column = fiota((HALF_ROWS, COLS), 1)
    for ref, half in ((send_ref, 1 - core), (keep_ref, core)):
        field = out_row - scale * HALF + half * HALF
        same = lane_scale == scale
        wind = same & (wind_field == field)
        rest = same & (rest_field == field)
        lengths = len_ref[pl.ds(pl.multiple_of(half * HALF, 8), HALF), :]
        rate = 1.0 / lengths
        rate = jnp.concatenate([rate[:, s:s + 1] for s in range(SCALES)], axis=0)
        fall = jnp.exp(-rate * (column + 1.0))
        rise = jnp.exp(-rate * (COLS - column))
        for side in range(2):
            pick = lambda k: jnp.sum(
                jnp.where(wind, weights[0][side][k], 0.0) + jnp.where(rest, weights[1][side][k], 0.0),
                axis=1, keepdims=True)
            rows = slice(side * HALF_ROWS, (side + 1) * HALF_ROWS)
            ref[rows, :] = local_ref[half, rows, :] + pick(0) * fall + pick(1) * rise


def column_sums(where, lengths, part, mine, theirs, edge, local):
    half = jax.ShapeDtypeStruct((2 * HALF_ROWS, COLS), F32)
    return pl.pallas_call(
        column_sums_kernel,
        in_specs=[SMEM] + [VMEM] * 6,
        out_specs=[VMEM] * 3,
        out_shape=[jax.ShapeDtypeStruct((ROWS, 512), F32), half, half],
        compiler_params=params(),
        name="column_sums",
    )(where, lengths, part, mine, theirs, edge, local)


def half_rates(where_ref, len_ref):
    core = where_ref[0] & 1
    rate = 1.0 / len_ref[pl.ds(pl.multiple_of(core * HALF, 8), HALF), :]
    return jnp.concatenate([rate[:, s:s + 1] for s in range(SCALES)], axis=0)


LEFT = slice(0, HALF_ROWS)
RIGHT = slice(HALF_ROWS, 2 * HALF_ROWS)


def chip_merge_kernel(where_ref, len_ref, keep_ref, got_ref, chip_ref):
    rate = half_rates(where_ref, len_ref)
    odd = (where_ref[0] & 1) == 1
    step = jnp.exp(-rate * ROWS)
    one = jnp.ones_like(step)
    mine_l, got_l = jnp.where(odd, one, step), jnp.where(odd, step, one)
    chip_ref[LEFT, :] = mine_l * keep_ref[LEFT, :] + got_l * got_ref[LEFT, :]
    chip_ref[RIGHT, :] = got_l * keep_ref[RIGHT, :] + mine_l * got_ref[RIGHT, :]


def chip_merge(where, lengths, keep, got):
    return pl.pallas_call(
        chip_merge_kernel,
        in_specs=[SMEM] + [VMEM] * 3,
        out_specs=VMEM,
        out_shape=jax.ShapeDtypeStruct((2 * HALF_ROWS, COLS), F32),
        compiler_params=params(),
        name="chip_merge",
    )(where, lengths, keep, got)


def quad_merge_kernel(where_ref, len_ref, chip_ref, pair_ref, left_ref, s1_ref, s2_ref, s3_ref):
    rate = half_rates(where_ref, len_ref)
    z = where_ref[0] >> 2
    zf = z.astype(F32)
    odd = ((where_ref[0] >> 1) & 1) == 1
    step = jnp.exp(-rate * (2 * ROWS))
    one = jnp.ones_like(step)
    mine_l, got_l = jnp.where(odd, one, step), jnp.where(odd, step, one)
    left = mine_l * chip_ref[LEFT, :] + got_l * pair_ref[LEFT, :]
    right = got_l * chip_ref[RIGHT, :] + mine_l * pair_ref[RIGHT, :]
    image = jnp.exp(-rate * (1.0 + 4 * ROWS * jnp.maximum(7.0 - 2.0 * zf, 1.0)))
    back = right - image * left
    left_ref[...] = left
    for d, ref in ((1, s1_ref), (2, s2_ref), (3, s3_ref)):
        ref[...] = jnp.where(z + d <= 3, left, back)


def quad_merge(where, lengths, chip, pair):
    one = jax.ShapeDtypeStruct((HALF_ROWS, COLS), F32)
    return pl.pallas_call(
        quad_merge_kernel,
        in_specs=[SMEM] + [VMEM] * 3,
        out_specs=[VMEM] * 4,
        out_shape=[one] * 4,
        compiler_params=params(),
        name="quad_merge",
    )(where, lengths, chip, pair)


def lat_carry_kernel(where_ref, len_ref, keep_ref, got_ref, pair_ref, left_ref, g1_ref, g2_ref, g3_ref,
                     own_ref, send_ref):
    rate = half_rates(where_ref, len_ref)
    lat = where_ref[0]
    z = lat >> 2
    zf = z.astype(F32)
    quad = lambda n: jnp.exp(-rate * (4 * ROWS * n))
    left = jnp.zeros((HALF_ROWS, COLS), F32)
    right = jnp.zeros((HALF_ROWS, COLS), F32)
    whole = quad(3.0 - zf) * left_ref[...]
    for d, ref in ((1, g1_ref), (2, g2_ref), (3, g3_ref)):
        below = z >= d
        g = ref[...]
        left = left + jnp.where(below, quad(d - 1.0), 0.0) * g
        right = right + jnp.where(below, 0.0, quad(3.0 - d)) * g
        whole = whole + jnp.where(below, quad(3.0 - zf + d), 0.0) * g
    right = right - (quad(3.0 - zf) * jnp.exp(-rate)) * whole
    odd_chip = ((lat >> 1) & 1) == 1
    pair = jnp.exp(-rate * (2 * ROWS))
    zero = jnp.zeros_like(pair)
    one = jnp.ones_like(pair)
    left = jnp.where(odd_chip, pair, one) * left + jnp.where(odd_chip, one, zero) * pair_ref[LEFT, :]
    right = jnp.where(odd_chip, one, pair) * right + jnp.where(odd_chip, zero, one) * pair_ref[RIGHT, :]
    odd = (lat & 1) == 1
    device = jnp.exp(-rate * ROWS)
    low_left = jnp.where(odd, got_ref[LEFT, :], keep_ref[LEFT, :])
    high_right = jnp.where(odd, keep_ref[RIGHT, :], got_ref[RIGHT, :])
    high_l = low_left + device * left
    low_r = high_right + device * right
    own_ref[LEFT, :] = jnp.where(odd, high_l, left)
    own_ref[RIGHT, :] = jnp.where(odd, right, low_r)
    send_ref[LEFT, :] = jnp.where(odd, left, high_l)
    send_ref[RIGHT, :] = jnp.where(odd, low_r, right)


def lat_carry(where, lengths, keep, got, pair, left, gs):
    half = jax.ShapeDtypeStruct((2 * HALF_ROWS, COLS), F32)
    return pl.pallas_call(
        lat_carry_kernel,
        in_specs=[SMEM] + [VMEM] * 8,
        out_specs=[VMEM] * 2,
        out_shape=[half, half],
        compiler_params=params(),
        name="lat_carry",
    )(where, lengths, keep, got, pair, left, *gs)


def scale_weights(lengths, weights):
    rate = 1.0 / lengths
    decay = jnp.exp(-rate)
    leak = 1.0 - decay
    cube = (1.0 + decay) * (1.0 + decay) * (1.0 + decay)
    coefficient = weights * cube / (leak * (1.0 + decay * decay))
    kappa = leak / (1.0 + decay)
    return rate, coefficient * kappa * kappa


def local_filter_kernel(where_ref, len_ref, weight_ref, carry_ref, x1_ref, x2_ref, out_ref):
    group = pl.program_id(0)
    top = where_ref[0] == 0
    shape = (SCALES * ROWS, LANES)
    r48 = iota(shape, 0)
    scale_of = jnp.where(r48 < ROWS, 0, jnp.where(r48 < 2 * ROWS, 1, 2))
    row = (r48 - scale_of * ROWS).astype(F32)
    lane = iota(shape, 1)
    source = jnp.where(lane >= ROWS, lane - ROWS, lane).astype(F32)
    used = lane < 2 * ROWS
    gap = jnp.abs(row - source)
    gap_low = jnp.abs(source - 1.0 - row)
    gap_high = jnp.abs(source + 1.0 - row)
    first = source == 0.0
    spread = jnp.abs(fiota((LANES, LANES), 0) - fiota((LANES, LANES), 1))
    column = fiota((1, LANES), 1)
    small_lane = iota((ROWS, LANES), 1)
    tag = small_lane & 31
    zeros = jnp.zeros((32, COLS + LANES), BF16)
    corner = jnp.zeros((LANES, LANES), BF16)

    def carry_tile(tile, virtual):
        left = carry_ref[:, tile * 256:tile * 256 + 128]
        right = carry_ref[:, tile * 256 + 128:tile * 256 + 256]
        left = pltpu.roll(left, (LANES - virtual) & (LANES - 1), 1)
        right = pltpu.roll(right, (LANES + 1 - virtual) & (LANES - 1), 1)
        return jnp.where(tag == 0, left, jnp.where(tag == 1, right, 0.0))

    def column_pass(matrix, x, carry):
        mh, ml = split(jnp.where(used, matrix, 0.0))
        lhs = jnp.concatenate([mh, ml[:, :ROWS]], axis=1)
        xh, xl = split(jnp.concatenate([x, carry], axis=1))
        rhs = jnp.concatenate([xh, xl, zeros, xh], axis=0)
        return mm(lhs, rhs)

    def one(i, wind):
        rate, weight = scale_weights(len_ref[pl.ds(i, 1), :], weight_ref[pl.ds(i, 1), :])
        by_row = lambda v: jnp.concatenate([jnp.broadcast_to(v[:, s:s + 1], (ROWS, 1)) for s in range(SCALES)], axis=0)
        rate_row, weight_row = by_row(rate), by_row(weight)
        plain = weight_row * jnp.exp(-rate_row * gap)
        if wind:
            slope = jnp.exp(-rate_row * gap_low) - jnp.exp(-rate_row * gap_high)
            slope = slope - jnp.where(top & first, jnp.exp(-rate_row * (row + 1.0)), 0.0)
            slope = (0.5 * weight_row) * slope
            second_sign = jnp.where(group == 0, 1.0, -1.0)
            meridional = jnp.where(group == 0, i, 24 + i)
            zonal = jnp.where(group == 0, 8 + i, 16 + i)
            w = column_pass(plain, -zonal_difference(x2_ref[i]), carry_tile(0, zonal))
            w = w + column_pass(slope, second_sign * x1_ref[i], carry_tile(0, meridional))
        else:
            w = column_pass(plain, x1_ref[i], carry_tile(1, (group - 2) * GROUP + i))
        parts = [None] * PARTS
        for s in range(SCALES):
            rate_s = rate[:, s:s + 1]
            rows = slice(s * ROWS, (s + 1) * ROWS)
            stack = jnp.concatenate([w[rows, b * LANES:(b + 1) * LANES] for b in range(PARTS)], axis=0)
            wh, wl = split(stack)
            th, tl = split(jnp.exp(-rate_s * spread))
            lhs = jnp.concatenate([wh, wl], axis=1)
            rhs = jnp.concatenate([jnp.concatenate([th, tl], axis=1), jnp.concatenate([th, corner], axis=1)], axis=0)
            out = mm(lhs, rhs)
            out = out[:, :LANES] + out[:, LANES:]
            left, right = out[:, LANES - 1:LANES], out[:, 0:1]
            carry = w[rows, COLS:]
            c0l, c2r = carry[:, 32 * s:32 * s + 1], carry[:, 32 * s + 1:32 * s + 2]
            jump = jnp.exp(-rate_s * LANES)
            c1l = left[0:ROWS] + jump * c0l
            c2l = left[ROWS:2 * ROWS] + jump * c1l
            c1r = right[2 * ROWS:] + jump * c2r
            c0r = right[ROWS:2 * ROWS] + jump * c1r
            fall = jnp.exp(-rate_s * (column + 1.0))
            rise = jnp.exp(-rate_s * (LANES - column))
            for b, (cl, cr) in enumerate(((c0l, c0r), (c1l, c1r), (c2l, c2r))):
                term = out[b * ROWS:(b + 1) * ROWS] + cl * fall + cr * rise
                parts[b] = term if s == 0 else parts[b] + term
        for b in range(PARTS):
            out_ref[i, :, b * LANES:(b + 1) * LANES] = parts[b]

    @pl.when(group < 2)
    def _():
        for i in range(GROUP):
            one(i, True)

    @pl.when(group >= 2)
    def _():
        for i in range(GROUP):
            one(i, False)


def local_filter(where, lengths, weights, carry, x):
    return pl.pallas_call(
        local_filter_kernel,
        grid=(GROUPS,),
        in_specs=[SMEM, pl.BlockSpec((GROUP, SCALES), lambda g: (g, 0)),
                  pl.BlockSpec((GROUP, SCALES), lambda g: (g, 0)),
                  pl.BlockSpec((ROWS, 512), lambda g: (0, 0)),
                  pl.BlockSpec((GROUP, ROWS, COLS), lambda g: (g, 0, 0)),
                  pl.BlockSpec((GROUP, ROWS, COLS), lambda g: (other_wind(g), 0, 0))],
        out_specs=pl.BlockSpec((GROUP, ROWS, COLS), lambda g: (g, 0, 0)),
        out_shape=jax.ShapeDtypeStruct((FIELDS, ROWS, COLS), F32),
        compiler_params=params(),
        name="local_filter",
    )(where, lengths, weights, carry, x, x)


def finish_kernel(where_ref, len_ref, weight_ref, z_ref, own_ref, got_ref, out_ref):
    group = pl.program_id(0)
    core = where_ref[0] & 1
    mine = jnp.where(group < 3, 0, 1) == core
    rate, weight = scale_weights(len_ref[...], weight_ref[...])
    row = fiota((ROWS, 1), 0)
    carry = jnp.where(mine, own_ref[...], got_ref[...])
    for i in range(GROUP):
        total = z_ref[i]
        for s in range(SCALES):
            r, w = rate[i:i + 1, s:s + 1], weight[i:i + 1, s:s + 1]
            up = w * jnp.exp(-r * (row + 1.0))
            down = w * jnp.exp(-r * (ROWS - row))
            total = total + up * carry[0, s, 0, i:i + 1] + down * carry[1, s, 0, i:i + 1]
        out_ref[i] = total


def finish(where, lengths, weights, z, own, got):
    shaped = lambda t: t.reshape(2, SCALES, 3, GROUP, COLS)
    carry_spec = pl.BlockSpec((2, SCALES, 1, GROUP, COLS), lambda g: (0, 0, g % 3, 0, 0))
    return pl.pallas_call(
        finish_kernel,
        grid=(GROUPS,),
        in_specs=[SMEM, pl.BlockSpec((GROUP, SCALES), lambda g: (g, 0)),
                  pl.BlockSpec((GROUP, SCALES), lambda g: (g, 0)),
                  pl.BlockSpec((GROUP, ROWS, COLS), lambda g: (g, 0, 0)), carry_spec, carry_spec],
        out_specs=pl.BlockSpec((GROUP, ROWS, COLS), lambda g: (g, 0, 0)),
        out_shape=jax.ShapeDtypeStruct((FIELDS, ROWS, COLS), F32),
        compiler_params=params(),
        name="finish",
    )(where, lengths, weights, z, shaped(own), shaped(got))


def shards(x, lengths, weights):
    where = jnp.stack([lax.axis_index("lat"), lax.axis_index("lon")]).astype(jnp.int32)
    sums, edge = row_sums(where, lengths, x)
    got = []
    for d in (1, 2, 3):
        perm = [(h * 4 + i, h * 4 + (i + d) % 4) for h in range(2) for i in range(4)]
        got.append(lax.ppermute(sums, "lon", perm))
    local = local_sums(where, lengths, x)
    part, mine = lon_merge(where, lengths, sums, got)
    theirs = lax.ppermute(mine, "lon", [(i, i ^ 4) for i in range(NLON)])
    carry, keep, send = column_sums(where, lengths, part, mine, theirs, edge, local)
    core_pairs = [(i, i ^ 1) for i in range(NLAT)]
    got_core = lax.ppermute(send, "lat", core_pairs)
    chip = chip_merge(where, lengths, keep, got_core)
    pair = lax.ppermute(chip, "lat", [(i, i ^ 2) for i in range(NLAT)])
    left, *sends = quad_merge(where, lengths, chip, pair)
    gs = [lax.ppermute(t, "lat", [(i, (i + 4 * d) % NLAT) for i in range(NLAT)]) for d, t in zip((1, 2, 3), sends)]
    z = local_filter(where, lengths, weights, carry, x)
    own, other = lat_carry(where, lengths, keep, got_core, pair, left, gs)
    got_carry = lax.ppermute(other, "lat", core_pairs)
    return finish(where, lengths, weights, z, own, got_carry)


def solution(mesh):
    in_specs = (P(None, "lat", "lon"), P(), P())
    out_specs = P(None, "lat", "lon")
    return jax.shard_map(shards, mesh=mesh, in_specs=in_specs, out_specs=out_specs, check_vma=False)
```

```python
import functools

import jax
import jax.numpy as jnp
from jax import lax
from jax.experimental import pallas as pl
from jax.experimental.pallas import tpu as pltpu
from jax.sharding import PartitionSpec as P

LEVELS = 8
SCALES = 3
WINDS = 16
FIELDS = 48
ROWS = 48
COLS = 384
GROUP = 8
GROUPS = FIELDS // GROUP
NLAT = 16
NLON = 8
LANES = 128
PARTS = COLS // LANES
HALF = FIELDS // 2
HALF_ROWS = SCALES * HALF
F32 = jnp.float32
BF16 = jnp.bfloat16

VMEM = pl.BlockSpec(memory_space=pltpu.VMEM)
SMEM = pl.BlockSpec(memory_space=pltpu.SMEM)
BIG = 48 * 1024 * 1024
WHOLE = 61 * 1024 * 1024


def params(**kw):
    return pltpu.CompilerParams(vmem_limit_bytes=BIG, **kw)


def iota(shape, dim):
    return lax.broadcasted_iota(jnp.int32, shape, dim)


def fiota(shape, dim):
    return iota(shape, dim).astype(F32)


def split(value):
    high = value.astype(BF16)
    return high, (value - high.astype(F32)).astype(BF16)


def mm(a, b):
    return jnp.dot(a, b, preferred_element_type=F32)


def lane_fields(shape):
    lane = iota(shape, 1)
    virtual = lane & 31
    wind_field = ((virtual >> 4) << 3) + (virtual & 7)
    return lane, lane >> 5, virtual, wind_field, virtual + WINDS


def exact(a, b, dims):
    return lax.dot_general(a, b, (dims, ((), ())), precision=lax.Precision.HIGHEST, preferred_element_type=F32)


def lane_rates(rate):
    shape = (FIELDS, LANES)
    _, _, _, wind_field, rest_field = lane_fields(shape)
    field = iota(shape, 0)
    lane = iota((1, LANES), 1)

    def pick(which):
        every = exact(rate, jnp.where(field == which, 1.0, 0.0).astype(F32), ((1,), (0,)))
        value = jnp.where(lane < 32, every[0:1], jnp.where(lane < 64, every[1:2], every[2:3]))
        return jnp.where(lane < 96, value, 1.0)

    return pick(wind_field), pick(rest_field)


def scale_weights(rate, weights):
    decay = jnp.exp(-rate)
    leak = 1.0 - decay
    cube = (1.0 + decay) * (1.0 + decay) * (1.0 + decay)
    coefficient = weights * cube / (leak * (1.0 + decay * decay))
    kappa = leak / (1.0 + decay)
    return coefficient * kappa * kappa


def lane_kinds(shape):
    _, _, virtual, _, _ = lane_fields(shape)
    second = virtual >= 16
    north = (virtual & 15) >= 8
    zonal = second != north
    sign = jnp.where(second | north, -1.0, 1.0).astype(F32)
    return zonal, sign


def row_sums_kernel(where_ref, len_ref, weight_ref, x_ref, sums_ref, edge_ref, table_ref, lanes_ref, w_ref, buf_ref, sem):
    lon = where_ref[1]
    copies = [pltpu.make_async_copy(x_ref.at[pl.ds(g * GROUP, GROUP)], buf_ref.at[g], sem.at[g]) for g in range(GROUPS)]
    for copy in copies:
        copy.start()
    rate = 1.0 / len_ref[...]
    pair = lane_rates(rate)
    lanes_ref[...] = jnp.concatenate([pair[0], pair[1], jnp.ones((6, LANES), F32)], axis=0)
    column = fiota((COLS, LANES), 0)
    for tile, rates in enumerate(pair):
        for side, steps in enumerate((COLS - 1 - column, column)):
            high, low = split(jnp.exp(-rates * steps))
            lanes = slice(side * LANES, (side + 1) * LANES)
            w_ref[tile, 0:COLS, lanes] = high
            w_ref[tile, COLS:2 * COLS, lanes] = high
            w_ref[tile, 2 * COLS:, lanes] = low
    both = jnp.concatenate([rate, scale_weights(rate, weight_ref[...]), jnp.ones((2, FIELDS), F32)], axis=0)
    eye = jnp.where(iota((8, LANES), 0) == iota((8, LANES), 1), 1.0, 0.0).astype(F32)
    table_ref[...] = exact(both, eye, ((0,), (0,)))
    virtual = iota((ROWS, LANES), 1) & 31
    zero = jnp.zeros((ROWS, LANES), F32)
    left, right, first, last = zero, zero, zero, zero
    for g in range(GROUPS):
        copies[g].wait()
        x = buf_ref[g].reshape(GROUP * ROWS, COLS)
        xh, xl = split(x)
        res = mm(jnp.concatenate([xh, xl, xh], axis=1), w_ref[0 if g < 2 else 1])
        if g == 2:
            left, right = zero, zero
        for i in range(GROUP):
            rows = slice(i * ROWS, (i + 1) * ROWS)
            mine = (virtual & 15) == g * GROUP + i if g < 2 else virtual == (g - 2) * GROUP + i
            left = jnp.where(mine, res[rows, 0:128], left)
            right = jnp.where(mine, res[rows, 128:256], right)
            if g < 2:
                first = jnp.where(mine, x[rows, 0:1], first)
                last = jnp.where(mine, x[rows, COLS - 1:COLS], last)
        if g == 1:
            sums_ref[:, 0:128] = left
            sums_ref[:, 128:256] = right
            sums_ref[:, 256:384] = jnp.where(lon == 0, first, jnp.where(lon == NLON - 1, last, 0.0))
            edge_ref[:, 0:128] = first
            edge_ref[:, 128:256] = last
    sums_ref[:, 384:512] = left
    sums_ref[:, 512:640] = right


HBM = pl.BlockSpec(memory_space=pltpu.HBM)
ANY = pl.BlockSpec(memory_space=pl.ANY)


def row_sums(where, lengths, weights, x):
    return pl.pallas_call(
        row_sums_kernel,
        in_specs=[SMEM, VMEM, VMEM, HBM],
        out_specs=[VMEM] * 4,
        out_shape=[jax.ShapeDtypeStruct((ROWS, 640), F32), jax.ShapeDtypeStruct((ROWS, 256), F32),
                   jax.ShapeDtypeStruct((FIELDS, LANES), F32), jax.ShapeDtypeStruct((8, LANES), F32)],
        scratch_shapes=[pltpu.VMEM((2, 3 * COLS, 256), BF16), pltpu.VMEM((GROUPS, GROUP, ROWS, COLS), F32),
                        pltpu.SemaphoreType.DMA((GROUPS,))],
        compiler_params=pltpu.CompilerParams(vmem_limit_bytes=WHOLE),
        name="row_sums",
    )(where, lengths, weights, x)


def zonal_difference(x):
    shape = x.shape
    axis = len(shape) - 1
    column = iota(shape, axis)
    ahead = jnp.where(column == COLS - 1, 0.0, pltpu.roll(x, COLS - 1, axis))
    behind = jnp.where(column == 0, 0.0, pltpu.roll(x, 1, axis))
    return 0.5 * (ahead - behind)


def local_sums_kernel(where_ref, table_ref, x_ref, out_ref):
    top = where_ref[0] == 0
    count = 2 * SCALES * GROUP
    shape = (count, LANES)
    out_row = iota(shape, 0)
    member = out_row & 7
    left_side = out_row < SCALES * GROUP
    lane = iota(shape, 1)
    source = jnp.where(lane >= ROWS, lane - ROWS, lane).astype(F32)
    used = lane < 2 * ROWS
    steps = jnp.where(left_side, ROWS - 1 - source, source)
    zeros = jnp.zeros((32, COLS), BF16)

    def weighted(matrix, x, i):
        mh, ml = split(jnp.where(used & (member == i), matrix, 0.0))
        xh, xl = split(x)
        return mm(jnp.concatenate([mh, ml[:, :ROWS]], axis=1), jnp.concatenate([xh, xl, zeros, xh], axis=0))

    def group_sums(group, wind):
        rate = table_ref[group * GROUP:(group + 1) * GROUP, :]
        row_rate = jnp.concatenate([rate[:, s:s + 1] for _ in range(2) for s in range(SCALES)], axis=0)
        wide = jnp.broadcast_to(row_rate, shape)
        plain = jnp.exp(-wide * steps)
        acc = jnp.zeros((count, COLS), F32)
        if wind:
            decay = jnp.exp(-wide)
            gain = 0.5 * (1.0 - decay * decay) / decay
            start = jnp.where(top & (source == 0.0), 0.5 * jnp.exp(-wide * ROWS), 0.0)
            slope = jnp.where(left_side, -gain * plain - start, gain * plain)
            second_sign = jnp.where(group == 0, 1.0, -1.0)
            for i in range(GROUP):
                acc += weighted(plain, -zonal_difference(x_ref[(1 - group) * GROUP + i]), i)
                acc += weighted(slope, second_sign * x_ref[group * GROUP + i], i)
        else:
            for i in range(GROUP):
                acc += weighted(plain, x_ref[group * GROUP + i], i)
        return acc, row_rate

    made = [group_sums(group, group < 2) for group in range(GROUPS)]
    acc = jnp.concatenate([m[0] for m in made], axis=0)
    factor = jnp.concatenate([jnp.broadcast_to(jnp.exp(-m[1]), (count, LANES)) for m in made], axis=0)
    factor = jnp.concatenate([factor] * PARTS, axis=1)
    column = iota(acc.shape, 1)
    forward, backward = acc, acc
    step = 1
    while step < COLS:
        forward = forward + factor * jnp.where(column >= step, pltpu.roll(forward, step, 1), 0.0)
        backward = backward + factor * jnp.where(column < COLS - step, pltpu.roll(backward, COLS - step, 1), 0.0)
        factor = factor * factor
        step *= 2
    acc = forward + backward - acc
    for group in range(GROUPS):
        for side in range(2):
            for s in range(SCALES):
                k = group * count + (side * SCALES + s) * GROUP
                out_ref[group // 3, side, s, group % 3] = acc[k:k + GROUP]


def local_sums(where, table, x):
    out = pl.pallas_call(
        local_sums_kernel,
        in_specs=[SMEM, VMEM, VMEM],
        out_specs=VMEM,
        out_shape=jax.ShapeDtypeStruct((2, 2, SCALES, 3, GROUP, COLS), F32),
        compiler_params=params(),
        name="local_sums",
    )(where, table, x)
    return out.reshape(2, 2 * HALF_ROWS, COLS)


def lon_merge_kernel(where_ref, lanes_ref, own_ref, g1_ref, g2_ref, g3_ref, _, part_ref, mine_ref):
    y = where_ref[1] & 3
    yf = y.astype(F32)
    rates = (lanes_ref[0:1, :], lanes_ref[1:2, :])
    got = (g1_ref, g2_ref, g3_ref)
    for tile in range(2):
        step = lambda n: jnp.exp(-rates[tile] * (COLS * n))
        base = tile * 384
        lanes_l = slice(base, base + 128)
        lanes_r = slice(base + 128, base + 256)
        left_total = step(3.0 - yf) * own_ref[:, lanes_l]
        right_total = step(yf) * own_ref[:, lanes_r]
        left = jnp.zeros((ROWS, LANES), F32)
        right = jnp.zeros((ROWS, LANES), F32)
        for d, ref in zip((1, 2, 3), got):
            below = y >= d
            lg, rg = ref[:, lanes_l], ref[:, lanes_r]
            left = left + jnp.where(below, step(d - 1.0), 0.0) * lg
            right = right + jnp.where(below, 0.0, step(3.0 - d)) * rg
            other = jnp.where(below, yf - d, yf - d + 4.0)
            left_total = left_total + step(3.0 - other) * lg
            right_total = right_total + step(other) * rg
        part_ref[:, tile * 256:tile * 256 + 128] = left
        part_ref[:, tile * 256 + 128:tile * 256 + 256] = right
        mine_ref[:, lanes_l] = left_total
        mine_ref[:, lanes_r] = right_total
    edge = slice(256, 384)
    mine_ref[:, edge] = own_ref[:, edge] + g1_ref[:, edge] + g2_ref[:, edge] + g3_ref[:, edge]


def lon_merge(where, lanes, own, got, after):
    return pl.pallas_call(
        lon_merge_kernel,
        in_specs=[SMEM] + [VMEM] * 5 + [ANY],
        out_specs=[VMEM, VMEM],
        out_shape=[jax.ShapeDtypeStruct((ROWS, 512), F32), jax.ShapeDtypeStruct((ROWS, 640), F32)],
        compiler_params=params(),
        name="lon_merge",
    )(where, lanes, own, *got, after)


def column_sums_kernel(where_ref, table_ref, lanes_ref, part_ref, mine_ref, theirs_ref, edge_ref, local_ref,
                       carry_ref, keep_ref, send_ref):
    lat, lon = where_ref[0], where_ref[1]
    y = lon & 3
    yf = y.astype(F32)
    high = lon >= 4
    highf = jnp.where(high, 1.0, 0.0)
    lowf = 1.0 - highf
    lonf = lon.astype(F32)
    top = lat == 0
    rates = (lanes_ref[0:1, :], lanes_ref[1:2, :])
    zonal, sign = lane_kinds((1, LANES))
    row = fiota((ROWS, LANES), 0)
    weights = []
    for tile in range(2):
        rate = rates[tile]
        step = lambda n: jnp.exp(-rate * (COLS * n))
        decay = jnp.exp(-rate)
        base = tile * 384
        lanes_l = slice(base, base + 128)
        lanes_r = slice(base + 128, base + 256)
        left = part_ref[:, tile * 256:tile * 256 + 128] + (highf * step(yf)) * theirs_ref[:, lanes_l]
        right = part_ref[:, tile * 256 + 128:tile * 256 + 256] + (lowf * step(3.0 - yf)) * theirs_ref[:, lanes_r]
        whole = ((highf + lowf * step(4.0)) * mine_ref[:, lanes_l]
                 + (lowf + highf * step(4.0)) * theirs_ref[:, lanes_l])
        end = step(7.0 - lonf)
        weight_l = jnp.exp(-rate * (ROWS - 1 - row))
        weight_r = jnp.exp(-rate * row)
        carry_l = left
        carry_r = right - (end * decay) * whole
        if tile == 0:
            v0 = lowf * mine_ref[:, 256:384] + highf * theirs_ref[:, 256:384]
            vn = highf * mine_ref[:, 256:384] + lowf * theirs_ref[:, 256:384]
            gain = 0.5 * (1.0 - decay * decay) / decay
            initial = -0.5 * (v0 + vn / decay)
            zonal_l = step(lonf) * initial - gain * left + 0.5 * edge_ref[:, 0:128]
            zonal_r = (gain * right - 0.5 * edge_ref[:, 128:256]
                       + end * (gain * v0 - decay * (step(8.0) * initial - gain * whole)))
            carry_l = sign * jnp.where(zonal, zonal_l, carry_l)
            carry_r = sign * jnp.where(zonal, zonal_r, carry_r)
            start = jnp.where(top & (row == 0.0), 0.5 * jnp.exp(-rate * ROWS), 0.0)
            weight_l = jnp.where(zonal, weight_l, -gain * weight_l - start)
            weight_r = jnp.where(zonal, weight_r, gain * weight_r)
        carry_ref[:, tile * 256:tile * 256 + 128] = carry_l
        carry_ref[:, tile * 256 + 128:tile * 256 + 256] = carry_r
        fold = lambda w, c: jnp.sum(w * c, axis=0, keepdims=True)
        weights.append(((fold(weight_l, carry_l), fold(weight_l, carry_r)),
                        (fold(weight_r, carry_l), fold(weight_r, carry_r))))
    shape = (HALF_ROWS, LANES)
    lane, lane_scale, _, wind_field, rest_field = lane_fields(shape)
    out_row = iota(shape, 0)
    scale = jnp.where(out_row < HALF, 0, jnp.where(out_row < 2 * HALF, 1, 2))
    core = lat & 1
    column = fiota((HALF_ROWS, COLS), 1)
    for ref, half in ((send_ref, 1 - core), (keep_ref, core)):
        field = out_row - scale * HALF + half * HALF
        same = lane_scale == scale
        wind = same & (wind_field == field)
        rest = same & (rest_field == field)
        rate = table_ref[pl.ds(pl.multiple_of(half * HALF, 8), HALF), :]
        rate = jnp.concatenate([rate[:, s:s + 1] for s in range(SCALES)], axis=0)
        fall = jnp.exp(-rate * (column + 1.0))
        rise = jnp.exp(-rate * (COLS - column))
        for side in range(2):
            pick = lambda k: jnp.sum(
                jnp.where(wind, weights[0][side][k], 0.0) + jnp.where(rest, weights[1][side][k], 0.0),
                axis=1, keepdims=True)
            rows = slice(side * HALF_ROWS, (side + 1) * HALF_ROWS)
            ref[rows, :] = local_ref[half, rows, :] + pick(0) * fall + pick(1) * rise


def column_sums(where, table, lanes, part, mine, theirs, edge, local):
    half = jax.ShapeDtypeStruct((2 * HALF_ROWS, COLS), F32)
    return pl.pallas_call(
        column_sums_kernel,
        in_specs=[SMEM] + [VMEM] * 7,
        out_specs=[VMEM] * 3,
        out_shape=[jax.ShapeDtypeStruct((ROWS, 512), F32), half, half],
        compiler_params=params(),
        name="column_sums",
    )(where, table, lanes, part, mine, theirs, edge, local)


def half_rates(where_ref, table_ref):
    core = where_ref[0] & 1
    rate = table_ref[pl.ds(pl.multiple_of(core * HALF, 8), HALF), :]
    return jnp.concatenate([rate[:, s:s + 1] for s in range(SCALES)], axis=0)


LEFT = slice(0, HALF_ROWS)
RIGHT = slice(HALF_ROWS, 2 * HALF_ROWS)


def chip_merge_kernel(where_ref, table_ref, keep_ref, got_ref, chip_ref):
    rate = half_rates(where_ref, table_ref)
    odd = (where_ref[0] & 1) == 1
    step = jnp.exp(-rate * ROWS)
    one = jnp.ones_like(step)
    mine_l, got_l = jnp.where(odd, one, step), jnp.where(odd, step, one)
    chip_ref[LEFT, :] = mine_l * keep_ref[LEFT, :] + got_l * got_ref[LEFT, :]
    chip_ref[RIGHT, :] = got_l * keep_ref[RIGHT, :] + mine_l * got_ref[RIGHT, :]


def chip_merge(where, table, keep, got):
    return pl.pallas_call(
        chip_merge_kernel,
        in_specs=[SMEM] + [VMEM] * 3,
        out_specs=VMEM,
        out_shape=jax.ShapeDtypeStruct((2 * HALF_ROWS, COLS), F32),
        compiler_params=params(),
        name="chip_merge",
    )(where, table, keep, got)


def quad_merge_kernel(where_ref, table_ref, chip_ref, pair_ref, _, left_ref, s1_ref, s2_ref, s3_ref):
    rate = half_rates(where_ref, table_ref)
    z = where_ref[0] >> 2
    zf = z.astype(F32)
    odd = ((where_ref[0] >> 1) & 1) == 1
    step = jnp.exp(-rate * (2 * ROWS))
    one = jnp.ones_like(step)
    mine_l, got_l = jnp.where(odd, one, step), jnp.where(odd, step, one)
    left = mine_l * chip_ref[LEFT, :] + got_l * pair_ref[LEFT, :]
    right = got_l * chip_ref[RIGHT, :] + mine_l * pair_ref[RIGHT, :]
    image = jnp.exp(-rate * (1.0 + 4 * ROWS * jnp.maximum(7.0 - 2.0 * zf, 1.0)))
    back = right - image * left
    left_ref[...] = left
    for d, ref in ((1, s1_ref), (2, s2_ref), (3, s3_ref)):
        ref[...] = jnp.where(z + d <= 3, left, back)


def quad_merge(where, table, chip, pair, after):
    one = jax.ShapeDtypeStruct((HALF_ROWS, COLS), F32)
    return pl.pallas_call(
        quad_merge_kernel,
        in_specs=[SMEM] + [VMEM] * 3 + [ANY],
        out_specs=[VMEM] * 4,
        out_shape=[one] * 4,
        compiler_params=params(),
        name="quad_merge",
    )(where, table, chip, pair, after)


def lat_carry_kernel(where_ref, table_ref, keep_ref, got_ref, pair_ref, left_ref, g1_ref, g2_ref, g3_ref, _,
                     own_ref, send_ref):
    rate = half_rates(where_ref, table_ref)
    lat = where_ref[0]
    z = lat >> 2
    zf = z.astype(F32)
    quad = lambda n: jnp.exp(-rate * (4 * ROWS * n))
    left = jnp.zeros((HALF_ROWS, COLS), F32)
    right = jnp.zeros((HALF_ROWS, COLS), F32)
    whole = quad(3.0 - zf) * left_ref[...]
    for d, ref in ((1, g1_ref), (2, g2_ref), (3, g3_ref)):
        below = z >= d
        g = ref[...]
        left = left + jnp.where(below, quad(d - 1.0), 0.0) * g
        right = right + jnp.where(below, 0.0, quad(3.0 - d)) * g
        whole = whole + jnp.where(below, quad(3.0 - zf + d), 0.0) * g
    right = right - (quad(3.0 - zf) * jnp.exp(-rate)) * whole
    odd_chip = ((lat >> 1) & 1) == 1
    pair = jnp.exp(-rate * (2 * ROWS))
    zero = jnp.zeros_like(pair)
    one = jnp.ones_like(pair)
    left = jnp.where(odd_chip, pair, one) * left + jnp.where(odd_chip, one, zero) * pair_ref[LEFT, :]
    right = jnp.where(odd_chip, one, pair) * right + jnp.where(odd_chip, zero, one) * pair_ref[RIGHT, :]
    odd = (lat & 1) == 1
    device = jnp.exp(-rate * ROWS)
    low_left = jnp.where(odd, got_ref[LEFT, :], keep_ref[LEFT, :])
    high_right = jnp.where(odd, keep_ref[RIGHT, :], got_ref[RIGHT, :])
    high_l = low_left + device * left
    low_r = high_right + device * right
    own_ref[LEFT, :] = jnp.where(odd, high_l, left)
    own_ref[RIGHT, :] = jnp.where(odd, right, low_r)
    send_ref[LEFT, :] = jnp.where(odd, left, high_l)
    send_ref[RIGHT, :] = jnp.where(odd, low_r, right)


def lat_carry(where, table, keep, got, pair, left, gs, after):
    half = jax.ShapeDtypeStruct((2 * HALF_ROWS, COLS), F32)
    return pl.pallas_call(
        lat_carry_kernel,
        in_specs=[SMEM] + [VMEM] * 8 + [ANY],
        out_specs=[VMEM] * 2,
        out_shape=[half, half],
        compiler_params=params(),
        name="lat_carry",
    )(where, table, keep, got, pair, left, *gs, after)


def local_filter_kernel(starts, where_ref, table_ref, carry_ref, x_ref, out_ref):
    top = where_ref[0] == 0
    shape = (ROWS, LANES)
    row = fiota(shape, 0)
    lane = iota(shape, 1)
    source = jnp.where(lane >= ROWS, lane - ROWS, lane).astype(F32)
    used = lane < 2 * ROWS
    gap = jnp.abs(row - source)
    gap_low = jnp.abs(source - 1.0 - row)
    gap_high = jnp.abs(source + 1.0 - row)
    first = source == 0.0
    spread = jnp.abs(fiota((LANES, LANES), 0) - fiota((LANES, LANES), 1))
    tag = lane & 31
    zeros = jnp.zeros((32, COLS + LANES), BF16)
    corner = jnp.zeros((LANES, LANES), BF16)
    left_lane = (lane == LANES - 1) | (lane == 1) | (lane == 3)
    lane_scale = lambda v: jnp.where((v == LANES - 1) | (v == 0), 0, jnp.where(v <= 2, 1, 2))
    row_scale = lane_scale(lane[:1])
    base = iota((8, LANES), 0)
    column = fiota((8, LANES), 1)

    def carry_tile(tile, virtual):
        left = carry_ref[:, tile * 256:tile * 256 + 128]
        right = carry_ref[:, tile * 256 + 128:tile * 256 + 256]
        left = pltpu.roll(left, (LANES - virtual) % LANES, 1)
        right = pltpu.roll(right, (LANES + 1 - virtual) % LANES, 1)
        return jnp.where(tag == 0, left, jnp.where(tag == 1, right, 0.0))

    def column_pass(matrices, x, carry):
        parts = [split(jnp.where(used, m, 0.0)) for m in matrices]
        lhs = jnp.concatenate([jnp.concatenate([mh, ml[:, :ROWS]], axis=1) for mh, ml in parts], axis=0)
        xh, xl = split(jnp.concatenate([x, carry], axis=1))
        rhs = jnp.concatenate([xh, xl, zeros, xh], axis=0)
        return mm(lhs, rhs)

    def column_stage(f, wind):
        facts = table_ref[pl.ds(f, 1), :]
        rates = [facts[:, s:s + 1] for s in range(SCALES)]
        gains = [facts[:, SCALES + s:SCALES + s + 1] for s in range(SCALES)]
        plain = [gains[s] * jnp.exp(-rates[s] * gap) for s in range(SCALES)]
        if wind:
            slopes = []
            for s in range(SCALES):
                slope = jnp.exp(-rates[s] * gap_low) - jnp.exp(-rates[s] * gap_high)
                slope = slope - jnp.where(top & first, jnp.exp(-rates[s] * (row + 1.0)), 0.0)
                slopes.append((0.5 * gains[s]) * slope)
            stream = f < GROUP
            second_sign = 1.0 if stream else -1.0
            meridional = f if stream else f + 16
            zonal = f + 8
            pair = f + 8 if stream else f - 8
            w = column_pass(plain, -zonal_difference(x_ref[pair]), carry_tile(0, zonal))
            w = w + column_pass(slopes, second_sign * x_ref[f], carry_tile(0, meridional))
        else:
            w = column_pass(plain, x_ref[f], carry_tile(1, f - WINDS))
        return rates, w

    def row_stage(rates, w):
        outs = []
        for s in range(SCALES):
            rows = slice(s * ROWS, (s + 1) * ROWS)
            stack = jnp.concatenate([w[rows, b * LANES:(b + 1) * LANES] for b in range(PARTS)], axis=0)
            wh, wl = split(stack)
            th, tl = split(jnp.exp(-rates[s] * spread))
            lhs = jnp.concatenate([wh, wl], axis=1)
            rhs = jnp.concatenate([jnp.concatenate([th, tl], axis=1), jnp.concatenate([th, corner], axis=1)], axis=0)
            out = mm(lhs, rhs)
            outs.append(out[:, :LANES] + out[:, LANES:])
        return outs

    def carry_stage(rates, w, outs):
        for s in range(SCALES):
            rows = slice(s * ROWS, (s + 1) * ROWS)
            moved = pltpu.roll(w[rows, COLS:], (LANES - 30 * s - 1) % LANES, 1)
            turned = outs[s] if s == 0 else pltpu.roll(outs[s], 2 * s, 1)
            here = row_scale == s
            outer = moved if s == 0 else jnp.where(here, moved, outer)
            sums = turned if s == 0 else jnp.where(here, turned, sums)
        rate_row = jnp.where(row_scale == 0, rates[0], jnp.where(row_scale == 1, rates[1], rates[2]))
        jump = jnp.exp(-rate_row * LANES)
        block = [sums[b * ROWS:(b + 1) * ROWS] for b in range(PARTS)]
        from_left = [outer]
        for b in range(PARTS - 1):
            from_left.append(block[b] + jump * from_left[-1])
        from_right = [outer]
        for b in range(PARTS - 1, 0, -1):
            from_right.append(block[b] + jump * from_right[-1])
        carries = [jnp.where(left_lane, from_left[b], from_right[PARTS - 1 - b]) for b in range(PARTS)]
        ch, cl = split(jnp.concatenate(carries, axis=0))
        low_rate = jnp.where(base == 0, rates[0], jnp.where(base <= 2, rates[1], rates[2]))
        low_left = (base == 1) | (base == 3)
        low = jnp.where(base <= 4, jnp.exp(-low_rate * jnp.where(low_left, column + 1.0, LANES - column)), 0.0)
        high = jnp.where(base == 7, jnp.exp(-rates[0] * (column + 1.0)), 0.0)
        pad = jnp.zeros((8, LANES), F32)
        lh, ll = split(jnp.concatenate([low, pad], axis=0))
        hh, hl = split(jnp.concatenate([pad, high], axis=0))
        gap_rows = jnp.zeros((96, LANES), BF16)
        bh = jnp.concatenate([lh, gap_rows, hh], axis=0)
        bl = jnp.concatenate([ll, gap_rows, hl], axis=0)
        rhs = jnp.concatenate([jnp.concatenate([bh, bl], axis=1), jnp.concatenate([bh, corner], axis=1)], axis=0)
        return jnp.concatenate([ch, cl], axis=1), rhs

    for start in starts:
        wind = start < WINDS
        fields = [start + i for i in range(GROUP)]
        columns = [column_stage(f, wind) for f in fields]
        outs = [row_stage(*c) for c in columns]
        ranks = [carry_stage(*c, o) for c, o in zip(columns, outs)]
        for f, o, (lhs, rhs) in zip(fields, outs, ranks):
            out = mm(lhs, rhs)
            total = (o[0] + o[1]) + (o[2] + out[:, :LANES]) + out[:, LANES:]
            for b in range(PARTS):
                out_ref[f - starts[0], :, b * LANES:(b + 1) * LANES] = total[b * ROWS:(b + 1) * ROWS]


def local_filter(where, table, carry, x, first, count, before, through=None):
    starts = tuple(range(first, first + count, GROUP))
    operands = [where, table, carry, x, before]
    in_specs = [SMEM] + [VMEM] * 3 + [ANY]
    out_specs = [VMEM]
    out_shape = [jax.ShapeDtypeStruct((count, ROWS, COLS), F32)]
    aliases = {}
    if through is not None:
        operands.append(through)
        in_specs.append(ANY)
        out_specs.append(ANY)
        out_shape.append(jax.ShapeDtypeStruct(through.shape, through.dtype))
        aliases = {5: 1}

    def body(*refs):
        local_filter_kernel(starts, *refs[:4], refs[len(in_specs)])

    return pl.pallas_call(
        body,
        in_specs=in_specs,
        out_specs=out_specs,
        out_shape=out_shape,
        input_output_aliases=aliases,
        compiler_params=params(),
        cost_estimate=pl.CostEstimate(flops=count * 400_000_000, bytes_accessed=count * 150_000, transcendentals=0),
        name="local_filter",
    )(*operands)


def finish_kernel(bounds, where_ref, table_ref, own_ref, got_ref, *refs):
    z_refs, (out_ref, buf_ref, sem) = refs[:len(bounds)], refs[len(bounds):]
    core = where_ref[0] & 1
    row = fiota((8, LANES), 0)
    up_steps, down_steps = row + 1.0, 8.0 - row
    copies = []
    for group in range(GROUPS):
        mine = core == group // 3
        part = group % 3
        k = max(i for i, b in enumerate(bounds) if b <= group * GROUP)
        tables = [jnp.where(mine, own_ref[side, s, part], got_ref[side, s, part]) for side in range(2) for s in range(SCALES)]
        for i in range(GROUP):
            f = group * GROUP + i
            facts = table_ref[f:f + 1, :]
            ups = []
            for s in range(SCALES):
                r = jnp.broadcast_to(facts[:, s:s + 1], (8, LANES))
                w = jnp.broadcast_to(facts[:, SCALES + s:SCALES + s + 1], (8, LANES))
                jump = jnp.exp(-8.0 * r)
                up, down = [w * jnp.exp(-r * up_steps)], [w * jnp.exp(-r * down_steps)]
                for _ in range(ROWS // 8 - 1):
                    up.append(up[-1] * jump)
                    down.insert(0, down[0] * jump)
                ups.append((jnp.concatenate(up, axis=0), jnp.concatenate(down, axis=0)))
            for b in range(PARTS):
                lanes = slice(b * LANES, (b + 1) * LANES)
                total = z_refs[k][f - bounds[k], :, lanes]
                for s in range(SCALES):
                    total = total + ups[s][0] * tables[s][i:i + 1, lanes] + ups[s][1] * tables[SCALES + s][i:i + 1, lanes]
                buf_ref[group, i, :, lanes] = total
        copy = pltpu.make_async_copy(buf_ref.at[group], out_ref.at[pl.ds(group * GROUP, GROUP)], sem.at[group])
        copy.start()
        copies.append(copy)
    for copy in copies:
        copy.wait()


def finish(where, table, own, got, parts):
    shaped = lambda t: t.reshape(2, SCALES, 3, GROUP, COLS)
    bounds = [sum(p.shape[0] for p in parts[:i]) for i in range(len(parts))]
    return pl.pallas_call(
        functools.partial(finish_kernel, bounds),
        in_specs=[SMEM] + [VMEM] * (3 + len(parts)),
        out_specs=HBM,
        out_shape=jax.ShapeDtypeStruct((FIELDS, ROWS, COLS), F32),
        scratch_shapes=[pltpu.VMEM((GROUPS, GROUP, ROWS, COLS), F32), pltpu.SemaphoreType.DMA((GROUPS,))],
        compiler_params=params(),
        name="finish",
    )(where, table, shaped(own), shaped(got), *parts)


def shards(x, lengths, weights):
    where = jnp.stack([lax.axis_index("lat"), lax.axis_index("lon")]).astype(jnp.int32)
    sums, edge, table, lanes = row_sums(where, lengths.T, weights.T, x)
    got = []
    for d in (1, 2, 3):
        perm = [(h * 4 + i, h * 4 + (i + d) % 4) for h in range(2) for i in range(4)]
        got.append(lax.ppermute(sums, "lon", perm))
    local = local_sums(where, table, x)
    part, mine = lon_merge(where, lanes, sums, got, local)
    theirs = lax.ppermute(mine, "lon", [(i, i ^ 4) for i in range(NLON)])
    carry, keep, send = column_sums(where, table, lanes, part, mine, theirs, edge, local)
    core_pairs = [(i, i ^ 1) for i in range(NLAT)]
    got_core = lax.ppermute(send, "lat", core_pairs)
    chip = chip_merge(where, table, keep, got_core)
    pair = lax.ppermute(chip, "lat", [(i, i ^ 2) for i in range(NLAT)])
    (z0,) = local_filter(where, table, carry, x, 0, 16, chip)
    left, s1, s2, s3 = quad_merge(where, table, chip, pair, z0)
    quad = lambda t, d: lax.ppermute(t, "lat", [(i, (i + 4 * d) % NLAT) for i in range(NLAT)])
    g1 = quad(s1, 1)
    z1, s2 = local_filter(where, table, carry, x, 16, 16, left, s2)
    g2 = quad(s2, 2)
    z2, s3 = local_filter(where, table, carry, x, 32, 8, z1, s3)
    g3 = quad(s3, 3)
    (z3,) = local_filter(where, table, carry, x, 40, 8, z2)
    own, other = lat_carry(where, table, keep, got_core, pair, left, (g1, g2, g3), z3)
    got_carry = lax.ppermute(other, "lat", core_pairs)
    return finish(where, table, own, got_carry, (z0, z1, z2, z3))


def solution(mesh):
    in_specs = (P(None, "lat", "lon"), P(), P())
    out_specs = P(None, "lat", "lon")
    return jax.shard_map(shards, mesh=mesh, in_specs=in_specs, out_specs=out_specs, check_vma=False)
```

```python
import functools

import jax
import jax.numpy as jnp
from jax import lax
from jax.experimental import pallas as pl
from jax.experimental.pallas import tpu as pltpu
from jax.sharding import PartitionSpec as P

LEVELS = 8
SCALES = 3
WINDS = 16
FIELDS = 48
ROWS = 48
COLS = 384
GROUP = 8
GROUPS = FIELDS // GROUP
NLAT = 16
NLON = 8
LANES = 128
PARTS = COLS // LANES
HALF = FIELDS // 2
HALF_ROWS = SCALES * HALF
F32 = jnp.float32
BF16 = jnp.bfloat16

VMEM = pl.BlockSpec(memory_space=pltpu.VMEM)
SMEM = pl.BlockSpec(memory_space=pltpu.SMEM)
BIG = 48 * 1024 * 1024


def params(**kw):
    return pltpu.CompilerParams(vmem_limit_bytes=BIG, **kw)


def iota(shape, dim):
    return lax.broadcasted_iota(jnp.int32, shape, dim)


def fiota(shape, dim):
    return iota(shape, dim).astype(F32)


def split(value):
    high = value.astype(BF16)
    return high, (value - high.astype(F32)).astype(BF16)


def mm(a, b):
    return jnp.dot(a, b, preferred_element_type=F32)


def lane_fields(shape):
    lane = iota(shape, 1)
    virtual = lane & 31
    wind_field = ((virtual >> 4) << 3) + (virtual & 7)
    return lane, lane >> 5, virtual, wind_field, virtual + WINDS


def exact(a, b, dims):
    return lax.dot_general(a, b, (dims, ((), ())), precision=lax.Precision.HIGHEST, preferred_element_type=F32)


def lane_rates(rate):
    shape = (FIELDS, LANES)
    _, _, _, wind_field, rest_field = lane_fields(shape)
    field = iota(shape, 0)
    lane = iota((1, LANES), 1)

    def pick(which):
        every = exact(rate, jnp.where(field == which, 1.0, 0.0).astype(F32), ((1,), (0,)))
        value = jnp.where(lane < 32, every[0:1], jnp.where(lane < 64, every[1:2], every[2:3]))
        return jnp.where(lane < 96, value, 0.0)

    return pick(wind_field), pick(rest_field)


def scale_weights(rate, weights):
    decay = jnp.exp(-rate)
    leak = 1.0 - decay
    cube = (1.0 + decay) * (1.0 + decay) * (1.0 + decay)
    coefficient = weights * cube / (leak * (1.0 + decay * decay))
    kappa = leak / (1.0 + decay)
    return coefficient * kappa * kappa


def lane_kinds(shape):
    _, _, virtual, _, _ = lane_fields(shape)
    second = virtual >= 16
    north = (virtual & 15) >= 8
    zonal = second != north
    sign = jnp.where(second | north, -1.0, 1.0).astype(F32)
    return zonal, sign


def tables_kernel(len_ref, weight_ref, table_ref, lanes_ref, w_ref):
    rate = 1.0 / len_ref[...]
    pair = lane_rates(rate)
    lanes_ref[...] = jnp.concatenate([pair[0], pair[1], jnp.ones((6, LANES), F32)], axis=0)
    column = fiota((COLS, LANES), 0)
    for tile, rates in enumerate(pair):
        for side, steps in enumerate((COLS - 1 - column, column)):
            high, low = split(jnp.exp(-rates * steps))
            lanes = slice(side * LANES, (side + 1) * LANES)
            w_ref[tile, 0:COLS, lanes] = high
            w_ref[tile, COLS:2 * COLS, lanes] = high
            w_ref[tile, 2 * COLS:, lanes] = low
    both = jnp.concatenate([rate, scale_weights(rate, weight_ref[...]), jnp.ones((2, FIELDS), F32)], axis=0)
    eye = jnp.where(iota((8, LANES), 0) == iota((8, LANES), 1), 1.0, 0.0).astype(F32)
    table_ref[...] = exact(both, eye, ((0,), (0,)))


def tables(lengths, weights):
    return pl.pallas_call(
        tables_kernel,
        in_specs=[VMEM] * 2,
        out_specs=[VMEM] * 3,
        out_shape=[jax.ShapeDtypeStruct((FIELDS, LANES), F32), jax.ShapeDtypeStruct((8, LANES), F32),
                   jax.ShapeDtypeStruct((2, 3 * COLS, 256), BF16)],
        compiler_params=params(),
        name="tables",
    )(lengths, weights)


def row_sums_kernel(where_ref, w_ref, x_ref, sums_ref, edge_ref):
    lon = where_ref[1]
    lane = iota((ROWS, LANES), 1)
    virtual = lane & 31
    zero = jnp.zeros((ROWS, LANES), F32)
    left, right, first, last = zero, zero, zero, zero
    for g in range(GROUPS):
        x = x_ref[g * GROUP:(g + 1) * GROUP].reshape(GROUP * ROWS, COLS)
        xh, xl = split(x)
        res = mm(jnp.concatenate([xh, xl, xh], axis=1), w_ref[0 if g < 2 else 1])
        if g == 2:
            left, right = zero, zero
        for i in range(GROUP):
            rows = slice(i * ROWS, (i + 1) * ROWS)
            mine = (virtual & 15) == g * GROUP + i if g < 2 else virtual == (g - 2) * GROUP + i
            left = jnp.where(mine, res[rows, 0:128], left)
            right = jnp.where(mine, res[rows, 128:256], right)
            if g < 2:
                first = jnp.where(mine, x[rows, 0:1], first)
                last = jnp.where(mine, x[rows, COLS - 1:COLS], last)
        if g == 1:
            edge = jnp.where(lon == 0, first, jnp.where(lon == NLON - 1, last, 0.0))
            sums_ref[:, 0:128] = jnp.where(lane >= 96, edge, left)
            sums_ref[:, 128:256] = right
            edge_ref[:, 0:128] = first
            edge_ref[:, 128:256] = last
    sums_ref[:, 256:384] = left
    sums_ref[:, 384:512] = right


HBM = pl.BlockSpec(memory_space=pltpu.HBM)
ANY = pl.BlockSpec(memory_space=pl.ANY)


def row_sums(where, w, x):
    return pl.pallas_call(
        row_sums_kernel,
        in_specs=[SMEM, VMEM, VMEM],
        out_specs=[VMEM] * 2,
        out_shape=[jax.ShapeDtypeStruct((ROWS, 512), F32), jax.ShapeDtypeStruct((ROWS, 256), F32)],
        compiler_params=params(),
        name="row_sums",
    )(where, w, x)


def zonal_difference(x):
    shape = x.shape
    axis = len(shape) - 1
    column = iota(shape, axis)
    ahead = jnp.where(column == COLS - 1, 0.0, pltpu.roll(x, COLS - 1, axis))
    behind = jnp.where(column == 0, 0.0, pltpu.roll(x, 1, axis))
    return 0.5 * (ahead - behind)


def local_sums_kernel(where_ref, table_ref, x_ref, _, out_ref):
    top = where_ref[0] == 0
    count = 2 * SCALES * GROUP
    shape = (count, LANES)
    out_row = iota(shape, 0)
    member = out_row & 7
    left_side = out_row < SCALES * GROUP
    lane = iota(shape, 1)
    source = jnp.where(lane >= ROWS, lane - ROWS, lane).astype(F32)
    used = lane < 2 * ROWS
    steps = jnp.where(left_side, ROWS - 1 - source, source)
    zeros = jnp.zeros((32, COLS), BF16)

    def weighted(matrix, x, i):
        mh, ml = split(jnp.where(used & (member == i), matrix, 0.0))
        xh, xl = split(x)
        return mm(jnp.concatenate([mh, ml[:, :ROWS]], axis=1), jnp.concatenate([xh, xl, zeros, xh], axis=0))

    def group_sums(group, wind):
        rate = table_ref[group * GROUP:(group + 1) * GROUP, :]
        row_rate = jnp.concatenate([rate[:, s:s + 1] for _ in range(2) for s in range(SCALES)], axis=0)
        wide = jnp.broadcast_to(row_rate, shape)
        plain = jnp.exp(-wide * steps)
        acc = jnp.zeros((count, COLS), F32)
        if wind:
            decay = jnp.exp(-wide)
            gain = 0.5 * (1.0 - decay * decay) / decay
            start = jnp.where(top & (source == 0.0), 0.5 * jnp.exp(-wide * ROWS), 0.0)
            slope = jnp.where(left_side, -gain * plain - start, gain * plain)
            second_sign = jnp.where(group == 0, 1.0, -1.0)
            for i in range(GROUP):
                acc += weighted(plain, -zonal_difference(x_ref[(1 - group) * GROUP + i]), i)
                acc += weighted(slope, second_sign * x_ref[group * GROUP + i], i)
        else:
            for i in range(GROUP):
                acc += weighted(plain, x_ref[group * GROUP + i], i)
        return acc, row_rate

    made = [group_sums(group, group < 2) for group in range(GROUPS)]
    acc = jnp.concatenate([m[0] for m in made], axis=0)
    factor = jnp.concatenate([jnp.broadcast_to(jnp.exp(-m[1]), (count, LANES)) for m in made], axis=0)
    factor = jnp.concatenate([factor] * PARTS, axis=1)
    column = iota(acc.shape, 1)
    forward, backward = acc, acc
    step = 1
    while step < COLS:
        forward = forward + factor * jnp.where(column >= step, pltpu.roll(forward, step, 1), 0.0)
        backward = backward + factor * jnp.where(column < COLS - step, pltpu.roll(backward, COLS - step, 1), 0.0)
        factor = factor * factor
        step *= 2
    acc = forward + backward - acc
    for group in range(GROUPS):
        for side in range(2):
            for s in range(SCALES):
                k = group * count + (side * SCALES + s) * GROUP
                out_ref[group // 3, side, s, group % 3] = acc[k:k + GROUP]


def local_sums(where, table, x, before):
    out = pl.pallas_call(
        local_sums_kernel,
        in_specs=[SMEM, VMEM, VMEM, ANY],
        out_specs=VMEM,
        out_shape=jax.ShapeDtypeStruct((2, 2, SCALES, 3, GROUP, COLS), F32),
        compiler_params=params(),
        cost_estimate=pl.CostEstimate(flops=6_000_000_000, bytes_accessed=4_000_000, transcendentals=0),
        name="local_sums",
    )(where, table, x, before)
    return out.reshape(2, 2 * HALF_ROWS, COLS)


def lon_merge_kernel(where_ref, lanes_ref, own_ref, g1_ref, g2_ref, g3_ref, _, part_ref, send_ref):
    y = where_ref[1] & 3
    high = where_ref[1] >= 4
    yf = y.astype(F32)
    zonal, _ = lane_kinds((1, LANES))
    lane = iota((1, LANES), 1)
    for tile in range(2):
        rate = lanes_ref[tile:tile + 1, :]
        step = lambda n: jnp.exp(-rate * (COLS * n))
        base = tile * 256
        lanes_l = slice(base, base + 128)
        lanes_r = slice(base + 128, base + 256)
        left_total = step(3.0 - yf) * own_ref[:, lanes_l]
        right_total = step(yf) * own_ref[:, lanes_r]
        left = jnp.zeros((ROWS, LANES), F32)
        right = jnp.zeros((ROWS, LANES), F32)
        for d, ref in ((1, g1_ref), (2, g2_ref), (3, g3_ref)):
            other = y ^ d
            of = other.astype(F32)
            below = other < y
            lg, rg = ref[:, lanes_l], ref[:, lanes_r]
            gap = jnp.abs(yf - of) - 1.0
            left = left + jnp.where(below, step(gap), 0.0) * lg
            right = right + jnp.where(below, 0.0, step(gap)) * rg
            left_total = left_total + step(3.0 - of) * lg
            right_total = right_total + step(of) * rg
        part_ref[:, lanes_l] = left
        part_ref[:, lanes_r] = right
        part_ref[:, 512 + tile * 128:640 + tile * 128] = left_total
        image = jnp.exp(-rate * (4.0 * COLS + 1.0))
        if tile == 0:
            image = jnp.where(zonal, -image, image)
            image = jnp.where(lane >= 96, -1.0, image)
            right_total = jnp.where(lane >= 96, 0.0, right_total)
        send_ref[:, tile * 128:tile * 128 + 128] = jnp.where(high, right_total - image * left_total, left_total)


def lon_merge(where, lanes, own, got, after):
    return pl.pallas_call(
        lon_merge_kernel,
        in_specs=[SMEM] + [VMEM] * 5 + [ANY],
        out_specs=[VMEM, VMEM],
        out_shape=[jax.ShapeDtypeStruct((ROWS, 768), F32), jax.ShapeDtypeStruct((ROWS, 256), F32)],
        compiler_params=params(),
        name="lon_merge",
    )(where, lanes, own, *got, after)


def spread_edges(tile):
    lane = iota(tile.shape, 1)
    out = tile
    for k in range(6):
        out = jnp.where((lane >> 4) == k, pltpu.roll(tile, (k * 16 + 32) % LANES, 1), out)
    return out


def column_sums_kernel(where_ref, table_ref, lanes_ref, part_ref, theirs_ref, edge_ref, local_ref,
                       carry_ref, keep_ref, send_ref):
    lat, lon = where_ref[0], where_ref[1]
    y = lon & 3
    yf = y.astype(F32)
    high = lon >= 4
    highf = jnp.where(high, 1.0, 0.0)
    lowf = 1.0 - highf
    lonf = lon.astype(F32)
    top = lat == 0
    rates = (lanes_ref[0:1, :], lanes_ref[1:2, :])
    zonal, sign = lane_kinds((1, LANES))
    row = fiota((ROWS, LANES), 0)
    weights = []
    for tile in range(2):
        rate = rates[tile]
        step = lambda n: jnp.exp(-rate * (COLS * n))
        decay = jnp.exp(-rate)
        theirs = theirs_ref[:, tile * 128:tile * 128 + 128]
        half = part_ref[:, 512 + tile * 128:640 + tile * 128]
        left = part_ref[:, tile * 256:tile * 256 + 128] + (highf * step(yf)) * theirs
        right = part_ref[:, tile * 256 + 128:tile * 256 + 256] + (lowf * step(3.0 - yf)) * theirs
        whole = (highf + lowf * step(4.0)) * half + (highf * step(4.0)) * theirs
        end = step(7.0 - lonf)
        weight_l = jnp.exp(-rate * (ROWS - 1 - row))
        weight_r = jnp.exp(-rate * row)
        carry_l = left
        carry_r = right - (end * decay) * whole
        if tile == 0:
            v0 = spread_edges(lowf * half + highf * theirs)
            vn = spread_edges(highf * half + lowf * theirs)
            gain = 0.5 * (1.0 - decay * decay) / decay
            initial = -0.5 * (v0 + vn / decay)
            zonal_l = step(lonf) * initial - gain * left + 0.5 * edge_ref[:, 0:128]
            zonal_r = (gain * right - 0.5 * edge_ref[:, 128:256]
                       + end * (gain * v0 - decay * (step(8.0) * initial - gain * whole)))
            carry_l = sign * jnp.where(zonal, zonal_l, carry_l)
            carry_r = sign * jnp.where(zonal, zonal_r, carry_r)
            start = jnp.where(top & (row == 0.0), 0.5 * jnp.exp(-rate * ROWS), 0.0)
            weight_l = jnp.where(zonal, weight_l, -gain * weight_l - start)
            weight_r = jnp.where(zonal, weight_r, gain * weight_r)
        carry_ref[:, tile * 256:tile * 256 + 128] = carry_l
        carry_ref[:, tile * 256 + 128:tile * 256 + 256] = carry_r
        fold = lambda w, c: jnp.sum(w * c, axis=0, keepdims=True)
        weights.append(((fold(weight_l, carry_l), fold(weight_l, carry_r)),
                        (fold(weight_r, carry_l), fold(weight_r, carry_r))))
    shape = (HALF_ROWS, LANES)
    lane, lane_scale, _, wind_field, rest_field = lane_fields(shape)
    out_row = iota(shape, 0)
    scale = jnp.where(out_row < HALF, 0, jnp.where(out_row < 2 * HALF, 1, 2))
    core = lat & 1
    column = fiota((HALF_ROWS, COLS), 1)
    for ref, half in ((send_ref, 1 - core), (keep_ref, core)):
        field = out_row - scale * HALF + half * HALF
        same = lane_scale == scale
        wind = same & (wind_field == field)
        rest = same & (rest_field == field)
        rate = table_ref[pl.ds(pl.multiple_of(half * HALF, 8), HALF), :]
        rate = jnp.concatenate([rate[:, s:s + 1] for s in range(SCALES)], axis=0)
        fall = jnp.exp(-rate * (column + 1.0))
        rise = jnp.exp(-rate * (COLS - column))
        for side in range(2):
            pick = lambda k: jnp.sum(
                jnp.where(wind, weights[0][side][k], 0.0) + jnp.where(rest, weights[1][side][k], 0.0),
                axis=1, keepdims=True)
            rows = slice(side * HALF_ROWS, (side + 1) * HALF_ROWS)
            ref[rows, :] = local_ref[half, rows, :] + pick(0) * fall + pick(1) * rise


def column_sums(where, table, lanes, part, theirs, edge, local):
    half = jax.ShapeDtypeStruct((2 * HALF_ROWS, COLS), F32)
    return pl.pallas_call(
        column_sums_kernel,
        in_specs=[SMEM] + [VMEM] * 6,
        out_specs=[VMEM] * 3,
        out_shape=[jax.ShapeDtypeStruct((ROWS, 512), F32), half, half],
        compiler_params=params(),
        name="column_sums",
    )(where, table, lanes, part, theirs, edge, local)


def half_rates(where_ref, table_ref):
    core = where_ref[0] & 1
    rate = table_ref[pl.ds(pl.multiple_of(core * HALF, 8), HALF), :]
    return jnp.concatenate([rate[:, s:s + 1] for s in range(SCALES)], axis=0)


LEFT = slice(0, HALF_ROWS)
RIGHT = slice(HALF_ROWS, 2 * HALF_ROWS)


def chip_merge_kernel(where_ref, table_ref, keep_ref, got_ref, chip_ref):
    rate = half_rates(where_ref, table_ref)
    odd = (where_ref[0] & 1) == 1
    step = jnp.exp(-rate * ROWS)
    one = jnp.ones_like(step)
    mine_l, got_l = jnp.where(odd, one, step), jnp.where(odd, step, one)
    chip_ref[LEFT, :] = mine_l * keep_ref[LEFT, :] + got_l * got_ref[LEFT, :]
    chip_ref[RIGHT, :] = got_l * keep_ref[RIGHT, :] + mine_l * got_ref[RIGHT, :]


def chip_merge(where, table, keep, got):
    return pl.pallas_call(
        chip_merge_kernel,
        in_specs=[SMEM] + [VMEM] * 3,
        out_specs=VMEM,
        out_shape=jax.ShapeDtypeStruct((2 * HALF_ROWS, COLS), F32),
        compiler_params=params(),
        name="chip_merge",
    )(where, table, keep, got)


def quad_merge_kernel(where_ref, table_ref, chip_ref, pair_ref, _, left_ref, s1_ref, s2_ref, s3_ref):
    rate = half_rates(where_ref, table_ref)
    z = where_ref[0] >> 2
    zf = z.astype(F32)
    odd = ((where_ref[0] >> 1) & 1) == 1
    step = jnp.exp(-rate * (2 * ROWS))
    one = jnp.ones_like(step)
    mine_l, got_l = jnp.where(odd, one, step), jnp.where(odd, step, one)
    left = mine_l * chip_ref[LEFT, :] + got_l * pair_ref[LEFT, :]
    right = got_l * chip_ref[RIGHT, :] + mine_l * pair_ref[RIGHT, :]
    image = jnp.exp(-rate * (1.0 + 4 * ROWS * jnp.maximum(7.0 - 2.0 * zf, 1.0)))
    back = right - image * left
    left_ref[...] = left
    for d, ref in ((1, s1_ref), (2, s2_ref), (3, s3_ref)):
        ref[...] = jnp.where((z ^ d) > z, left, back)


def quad_merge(where, table, chip, pair, after):
    one = jax.ShapeDtypeStruct((HALF_ROWS, COLS), F32)
    return pl.pallas_call(
        quad_merge_kernel,
        in_specs=[SMEM] + [VMEM] * 3 + [ANY],
        out_specs=[VMEM] * 4,
        out_shape=[one] * 4,
        compiler_params=params(),
        name="quad_merge",
    )(where, table, chip, pair, after)


def lat_carry_kernel(where_ref, table_ref, keep_ref, got_ref, pair_ref, left_ref, g1_ref, g2_ref, g3_ref, _,
                     own_ref, send_ref):
    rate = half_rates(where_ref, table_ref)
    lat = where_ref[0]
    z = lat >> 2
    zf = z.astype(F32)
    quad = lambda n: jnp.exp(-rate * (4 * ROWS * n))
    left = jnp.zeros((HALF_ROWS, COLS), F32)
    right = jnp.zeros((HALF_ROWS, COLS), F32)
    whole = quad(3.0 - zf) * left_ref[...]
    for d, ref in ((1, g1_ref), (2, g2_ref), (3, g3_ref)):
        other = z ^ d
        of = other.astype(F32)
        below = other < z
        gap = quad(jnp.abs(zf - of) - 1.0)
        g = ref[...]
        left = left + jnp.where(below, gap, 0.0) * g
        right = right + jnp.where(below, 0.0, gap) * g
        whole = whole + jnp.where(below, quad(3.0 - of), 0.0) * g
    right = right - (quad(3.0 - zf) * jnp.exp(-rate)) * whole
    odd_chip = ((lat >> 1) & 1) == 1
    pair = jnp.exp(-rate * (2 * ROWS))
    zero = jnp.zeros_like(pair)
    one = jnp.ones_like(pair)
    left = jnp.where(odd_chip, pair, one) * left + jnp.where(odd_chip, one, zero) * pair_ref[LEFT, :]
    right = jnp.where(odd_chip, one, pair) * right + jnp.where(odd_chip, zero, one) * pair_ref[RIGHT, :]
    odd = (lat & 1) == 1
    device = jnp.exp(-rate * ROWS)
    low_left = jnp.where(odd, got_ref[LEFT, :], keep_ref[LEFT, :])
    high_right = jnp.where(odd, keep_ref[RIGHT, :], got_ref[RIGHT, :])
    high_l = low_left + device * left
    low_r = high_right + device * right
    own_ref[LEFT, :] = jnp.where(odd, high_l, left)
    own_ref[RIGHT, :] = jnp.where(odd, right, low_r)
    send_ref[LEFT, :] = jnp.where(odd, left, high_l)
    send_ref[RIGHT, :] = jnp.where(odd, low_r, right)


def lat_carry(where, table, keep, got, pair, left, gs, after):
    half = jax.ShapeDtypeStruct((2 * HALF_ROWS, COLS), F32)
    return pl.pallas_call(
        lat_carry_kernel,
        in_specs=[SMEM] + [VMEM] * 8 + [ANY],
        out_specs=[VMEM] * 2,
        out_shape=[half, half],
        compiler_params=params(),
        name="lat_carry",
    )(where, table, keep, got, pair, left, *gs, after)


def local_filter_kernel(starts, use_x, use_carry, where_ref, table_ref, carry_ref, x_ref, base_ref, out_ref):
    top = where_ref[0] == 0
    shape = (ROWS, LANES)
    row = fiota(shape, 0)
    lane = iota(shape, 1)
    source = jnp.where(lane >= ROWS, lane - ROWS, lane).astype(F32)
    used = lane < 2 * ROWS
    gap = jnp.abs(row - source)
    gap_low = jnp.abs(source - 1.0 - row)
    gap_high = jnp.abs(source + 1.0 - row)
    first = source == 0.0
    spread = jnp.abs(fiota((LANES, LANES), 0) - fiota((LANES, LANES), 1))
    tag = lane & 31
    corner = jnp.zeros((LANES, LANES), BF16)
    left_lane = (lane & 1) == 0
    row_scale = jnp.minimum(lane[:1] >> 1, 2)
    base = iota((8, LANES), 0)
    column = fiota((8, LANES), 1)
    tall_lane = iota((PARTS * ROWS, LANES), 1)

    def carry_tile(tile, virtual):
        left = carry_ref[:, tile * 256:tile * 256 + 128]
        right = carry_ref[:, tile * 256 + 128:tile * 256 + 256]
        left = pltpu.roll(left, (LANES - virtual) % LANES, 1)
        right = pltpu.roll(right, (LANES + 1 - virtual) % LANES, 1)
        return jnp.where(tag == 0, left, jnp.where(tag == 1, right, 0.0))

    def column_pass(matrices, x, carry):
        parts = [split(jnp.where(used, m, 0.0)) for m in matrices]
        lhs = jnp.concatenate([jnp.concatenate([mh, ml[:, :ROWS]], axis=1) for mh, ml in parts], axis=0)
        wide = [t for t in (x, carry) if t is not None]
        wide = wide[0] if len(wide) == 1 else jnp.concatenate(wide, axis=1)
        xh, xl = split(wide)
        rhs = jnp.concatenate([xh, xl, jnp.zeros((32, wide.shape[1]), BF16), xh], axis=0)
        return mm(lhs, rhs)

    def column_stage(f, wind):
        facts = table_ref[pl.ds(f, 1), :]
        rates = [facts[:, s:s + 1] for s in range(SCALES)]
        gains = [facts[:, SCALES + s:SCALES + s + 1] for s in range(SCALES)]
        plain = [gains[s] * jnp.exp(-rates[s] * gap) for s in range(SCALES)]
        if wind:
            slopes = []
            for s in range(SCALES):
                slope = jnp.exp(-rates[s] * gap_low) - jnp.exp(-rates[s] * gap_high)
                slope = slope - jnp.where(top & first, jnp.exp(-rates[s] * (row + 1.0)), 0.0)
                slopes.append((0.5 * gains[s]) * slope)
            stream = f < GROUP
            second_sign = 1.0 if stream else -1.0
            meridional = f if stream else f + 16
            zonal = f + 8
            pair = f + 8 if stream else f - 8
            w = column_pass(plain, -zonal_difference(x_ref[pair]), carry_tile(0, zonal))
            w = w + column_pass(slopes, second_sign * x_ref[f], carry_tile(0, meridional))
        else:
            w = column_pass(plain, x_ref[f] if use_x else None, carry_tile(1, f - WINDS) if use_carry else None)
        return rates, w

    def row_stage(rates, w):
        outs = []
        for s in range(SCALES):
            rows = slice(s * ROWS, (s + 1) * ROWS)
            stack = jnp.concatenate([w[rows, b * LANES:(b + 1) * LANES] for b in range(PARTS)], axis=0)
            wh, wl = split(stack)
            th, tl = split(jnp.exp(-rates[s] * spread))
            lhs = jnp.concatenate([wh, wl], axis=1)
            rhs = jnp.concatenate([jnp.concatenate([th, tl], axis=1), jnp.concatenate([th, corner], axis=1)], axis=0)
            out = mm(lhs, rhs)
            outs.append(out[:, :LANES] + out[:, LANES:])
        return outs

    def carry_stage(rates, w, outs):
        sums, outer = None, jnp.zeros((ROWS, LANES), F32)
        for s in range(SCALES):
            here = row_scale == s
            if use_carry:
                moved = w[s * ROWS:(s + 1) * ROWS, w.shape[1] - LANES:]
                moved = moved if s == 0 else pltpu.roll(moved, LANES - 30 * s, 1)
                outer = jnp.where(here, moved, outer)
            if use_x:
                turned = pltpu.roll(outs[s], 2 * s + 1, 1)
                sums = turned if s == 0 else jnp.where(here, turned, sums)
        rate_row = jnp.where(row_scale == 0, rates[0], jnp.where(row_scale == 1, rates[1], rates[2]))
        jump = jnp.exp(-rate_row * LANES)
        from_left, from_right = [outer], [outer]
        for b in range(PARTS - 1):
            ahead, behind = jump * from_left[-1], jump * from_right[-1]
            if use_x:
                ahead = ahead + sums[b * ROWS:(b + 1) * ROWS]
                behind = behind + sums[(PARTS - 1 - b) * ROWS:(PARTS - b) * ROWS]
            from_left.append(ahead)
            from_right.append(behind)
        carries = [jnp.where(left_lane, from_left[b], from_right[PARTS - 1 - b]) for b in range(PARTS)]
        carries = jnp.where(tall_lane < 6, jnp.concatenate(carries, axis=0), 0.0)
        ch = carries.astype(BF16).astype(F32)
        lhs = (ch + pltpu.roll(carries - ch, 8, 1)).astype(BF16)[:, :16]
        base_rate = jnp.where(base < 2, rates[0], jnp.where(base < 4, rates[1], rates[2]))
        powers = jnp.exp(-base_rate * jnp.where((base & 1) == 0, column + 1.0, LANES - column))
        powers = jnp.where(base < 6, powers, 0.0)
        ph = powers.astype(BF16).astype(F32)
        rhs = jnp.concatenate([jnp.concatenate([ph, powers - ph], axis=1),
                               jnp.concatenate([ph, jnp.zeros((8, LANES), F32)], axis=1)], axis=0)
        return lhs, rhs.astype(BF16)

    for start in starts:
        wind = start < WINDS
        fields = [start + i for i in range(GROUP)]
        columns = [column_stage(f, wind) for f in fields]
        outs = [row_stage(*c) if use_x else None for c in columns]
        ranks = [carry_stage(*c, o) for c, o in zip(columns, outs)]
        for f, o, (lhs, rhs) in zip(fields, outs, ranks):
            out = mm(lhs, rhs)
            total = out[:, :LANES] + out[:, LANES:]
            if use_x:
                total = (o[0] + o[1]) + (o[2] + total)
            for b in range(PARTS):
                lanes = slice(b * LANES, (b + 1) * LANES)
                part = total[b * ROWS:(b + 1) * ROWS]
                if base_ref is not None:
                    part = part + base_ref[f - starts[0], :, lanes]
                out_ref[f - starts[0], :, lanes] = part


def local_filter(where, table, carry, x, first, count, before, base=None):
    starts = tuple(range(first, first + count, GROUP))
    use_x, use_carry = base is None, carry is not None
    names = ["where", "table"] + ["carry"] * use_carry + ["x"] * use_x + ["base"] * (base is not None) + ["before"]
    arrays = {"where": where, "table": table, "carry": carry, "x": x, "base": base, "before": before}
    specs = {"where": SMEM, "before": ANY}

    def body(*refs):
        by_name = dict(zip(names, refs))
        local_filter_kernel(starts, use_x, use_carry, by_name["where"], by_name["table"], by_name.get("carry"),
                            by_name.get("x"), by_name.get("base"), refs[len(names)])

    return pl.pallas_call(
        body,
        in_specs=[specs.get(n, VMEM) for n in names],
        out_specs=VMEM,
        out_shape=jax.ShapeDtypeStruct((count, ROWS, COLS), F32),
        compiler_params=params(),
        cost_estimate=pl.CostEstimate(flops=count * 300_000_000, bytes_accessed=count * 150_000, transcendentals=0),
        name="local_filter",
    )(*[arrays[n] for n in names])


def finish_kernel(own_half, where_ref, table_ref, carry_ref, z0_ref, z1_ref, z2_ref, *refs):
    out_ref, buf_ref, sem = refs[-3:]
    core = where_ref[0] & 1
    half = core if own_half else 1 - core
    z_refs = (z0_ref, z0_ref, z1_ref, z1_ref, z2_ref, z2_ref)
    row = fiota((8, LANES), 0)
    up_steps, down_steps = row + 1.0, 8.0 - row
    copies = []
    for part in range(3):
        tables = [carry_ref[side, s, part] for side in range(2) for s in range(SCALES)]
        start = pl.multiple_of((half * 3 + part) * GROUP, GROUP)
        group_facts = table_ref[pl.ds(start, GROUP), :]
        for i in range(GROUP):
            facts = group_facts[i:i + 1, :]
            ups = []
            for s in range(SCALES):
                r = jnp.broadcast_to(facts[:, s:s + 1], (8, LANES))
                w = jnp.broadcast_to(facts[:, SCALES + s:SCALES + s + 1], (8, LANES))
                jump = jnp.exp(-8.0 * r)
                up, down = [w * jnp.exp(-r * up_steps)], [w * jnp.exp(-r * down_steps)]
                for _ in range(ROWS // 8 - 1):
                    up.append(up[-1] * jump)
                    down.insert(0, down[0] * jump)
                ups.append((jnp.concatenate(up, axis=0), jnp.concatenate(down, axis=0)))
            for b in range(PARTS):
                lanes = slice(b * LANES, (b + 1) * LANES)
                total = jnp.where(half == 0, z_refs[part][part % 2 * GROUP + i, :, lanes],
                                  z_refs[3 + part][(3 + part) % 2 * GROUP + i, :, lanes])
                for s in range(SCALES):
                    total = total + ups[s][0] * tables[s][i:i + 1, lanes] + ups[s][1] * tables[SCALES + s][i:i + 1, lanes]
                buf_ref[part, i, :, lanes] = total
        copy = pltpu.make_async_copy(buf_ref.at[part], out_ref.at[pl.ds(start, GROUP)], sem.at[part])
        copy.start()
        copies.append(copy)
    for copy in copies:
        copy.wait()


def finish(own_half, where, table, carry, parts, out=None):
    operands = [where, table, carry.reshape(2, SCALES, 3, GROUP, COLS), *parts]
    in_specs = [SMEM] + [VMEM] * 5
    aliases = {}
    if out is not None:
        operands.append(out)
        in_specs.append(HBM)
        aliases = {6: 0}
    return pl.pallas_call(
        functools.partial(finish_kernel, own_half),
        in_specs=in_specs,
        out_specs=HBM,
        out_shape=jax.ShapeDtypeStruct((FIELDS, ROWS, COLS), F32),
        scratch_shapes=[pltpu.VMEM((3, GROUP, ROWS, COLS), F32), pltpu.SemaphoreType.DMA((3,))],
        input_output_aliases=aliases,
        compiler_params=params(),
        cost_estimate=pl.CostEstimate(flops=1_000_000_000, bytes_accessed=4_000_000, transcendentals=0),
        name="finish",
    )(*operands)


def partner(axis, count, bit):
    return functools.partial(lax.ppermute, axis_name=axis, perm=[(i, i ^ bit) for i in range(count)])


def shards(x, lengths, weights):
    where = jnp.stack([lax.axis_index("lat"), lax.axis_index("lon")]).astype(jnp.int32)
    table, lanes, w = tables(lengths.T, weights.T)
    sums, edge = row_sums(where, w, x)
    got = [partner("lon", NLON, d)(sums) for d in (1, 2, 3)]
    early = local_filter(where, table, None, x, 32, 16, sums)
    part, half = lon_merge(where, lanes, sums, got, early)
    theirs = partner("lon", NLON, 4)(half)
    local = local_sums(where, table, x, part)
    carry, keep, send = column_sums(where, table, lanes, part, theirs, edge, local)
    got_core = partner("lat", NLAT, 1)(send)
    chip = chip_merge(where, table, keep, got_core)
    pair = partner("lat", NLAT, 2)(chip)
    z0 = local_filter(where, table, carry, x, 0, 16, chip)
    left, *sends = quad_merge(where, table, chip, pair, z0)
    gs = [partner("lat", NLAT, 4 * d)(t) for d, t in zip((1, 2, 3), sends)]
    z1 = local_filter(where, table, carry, x, 16, 16, left)
    z2 = local_filter(where, table, carry, x, 32, 16, z1, early)
    own, other = lat_carry(where, table, keep, got_core, pair, left, gs, z2)
    got_carry = partner("lat", NLAT, 1)(other)
    out = finish(True, where, table, own, (z0, z1, z2))
    return finish(False, where, table, got_carry, (z0, z1, z2), out)


def solution(mesh):
    in_specs = (P(None, "lat", "lon"), P(), P())
    out_specs = P(None, "lat", "lon")
    return jax.shard_map(shards, mesh=mesh, in_specs=in_specs, out_specs=out_specs, check_vma=False)
```

```python
import functools

import jax
import jax.numpy as jnp
from jax import lax
from jax.experimental import pallas as pl
from jax.experimental.pallas import tpu as pltpu
from jax.sharding import PartitionSpec as P

LEVELS = 8
SCALES = 3
WINDS = 16
FIELDS = 48
ROWS = 48
COLS = 384
GROUP = 8
GROUPS = FIELDS // GROUP
NLAT = 16
NLON = 8
LANES = 128
PARTS = COLS // LANES
HALF = FIELDS // 2
HALF_ROWS = SCALES * HALF
F32 = jnp.float32
BF16 = jnp.bfloat16

VMEM = pl.BlockSpec(memory_space=pltpu.VMEM)
SMEM = pl.BlockSpec(memory_space=pltpu.SMEM)
BIG = 48 * 1024 * 1024
WHOLE = 50 * 1024 * 1024


def params(**kw):
    return pltpu.CompilerParams(vmem_limit_bytes=BIG, **kw)


def iota(shape, dim):
    return lax.broadcasted_iota(jnp.int32, shape, dim)


def fiota(shape, dim):
    return iota(shape, dim).astype(F32)


def split(value):
    high = value.astype(BF16)
    return high, (value - high.astype(F32)).astype(BF16)


def mm(a, b):
    return jnp.dot(a, b, preferred_element_type=F32)


def lane_fields(shape):
    lane = iota(shape, 1)
    virtual = lane & 31
    wind_field = ((virtual >> 4) << 3) + (virtual & 7)
    return lane, lane >> 5, virtual, wind_field, virtual + WINDS


def exact(a, b, dims):
    return lax.dot_general(a, b, (dims, ((), ())), precision=lax.Precision.HIGHEST, preferred_element_type=F32)


def lane_rates(rate):
    shape = (FIELDS, LANES)
    _, _, _, wind_field, rest_field = lane_fields(shape)
    field = iota(shape, 0)
    lane = iota((1, LANES), 1)

    def pick(which):
        every = exact(rate, jnp.where(field == which, 1.0, 0.0).astype(F32), ((1,), (0,)))
        value = jnp.where(lane < 32, every[0:1], jnp.where(lane < 64, every[1:2], every[2:3]))
        return jnp.where(lane < 96, value, 0.0)

    return pick(wind_field), pick(rest_field)


def scale_weights(rate, weights):
    decay = jnp.exp(-rate)
    leak = 1.0 - decay
    cube = (1.0 + decay) * (1.0 + decay) * (1.0 + decay)
    coefficient = weights * cube / (leak * (1.0 + decay * decay))
    kappa = leak / (1.0 + decay)
    return coefficient * kappa * kappa


def lane_kinds(shape):
    _, _, virtual, _, _ = lane_fields(shape)
    second = virtual >= 16
    north = (virtual & 15) >= 8
    zonal = second != north
    sign = jnp.where(second | north, -1.0, 1.0).astype(F32)
    return zonal, sign


def row_sums_kernel(where_ref, len_ref, x_ref, sums_ref, edge_ref, table_ref, lanes_ref, held_ref, w_ref, sem):
    lon = where_ref[1]
    copies = []
    for g in range(GROUPS):
        here = pl.ds(g * GROUP, GROUP)
        copies.append(pltpu.make_async_copy(x_ref.at[here], held_ref.at[here], sem.at[g]))
        copies[-1].start()
    rate = 1.0 / len_ref[0:SCALES, :]
    pair = lane_rates(rate)
    lanes_ref[...] = jnp.concatenate([pair[0], pair[1], jnp.ones((6, LANES), F32)], axis=0)
    column = fiota((COLS, LANES), 0)
    for tile, rates in enumerate(pair):
        for side, steps in enumerate((COLS - 1 - column, column)):
            high, low = split(jnp.exp(-rates * steps))
            lanes = slice(side * LANES, (side + 1) * LANES)
            w_ref[tile, 0:COLS, lanes] = high
            w_ref[tile, COLS:2 * COLS, lanes] = high
            w_ref[tile, 2 * COLS:, lanes] = low
    both = jnp.concatenate([rate, scale_weights(rate, len_ref[SCALES:, :]), jnp.ones((2, FIELDS), F32)], axis=0)
    eye = jnp.where(iota((8, LANES), 0) == iota((8, LANES), 1), 1.0, 0.0).astype(F32)
    table_ref[...] = exact(both, eye, ((0,), (0,)))
    lane = iota((ROWS, LANES), 1)
    virtual = lane & 31
    zero = jnp.zeros((ROWS, LANES), F32)
    left, right, first, last = zero, zero, zero, zero
    for g in range(GROUPS):
        copies[g].wait()
        x = held_ref[g * GROUP:(g + 1) * GROUP].reshape(GROUP * ROWS, COLS)
        xh, xl = split(x)
        res = mm(jnp.concatenate([xh, xl, xh], axis=1), w_ref[0 if g < 2 else 1])
        if g == 2:
            left, right = zero, zero
        for i in range(GROUP):
            rows = slice(i * ROWS, (i + 1) * ROWS)
            mine = (virtual & 15) == g * GROUP + i if g < 2 else virtual == (g - 2) * GROUP + i
            left = jnp.where(mine, res[rows, 0:128], left)
            right = jnp.where(mine, res[rows, 128:256], right)
            if g < 2:
                first = jnp.where(mine, x[rows, 0:1], first)
                last = jnp.where(mine, x[rows, COLS - 1:COLS], last)
        if g == 1:
            edge = jnp.where(lon == 0, first, jnp.where(lon == NLON - 1, last, 0.0))
            sums_ref[:, 0:128] = jnp.where(lane >= 96, edge, left)
            sums_ref[:, 128:256] = right
            edge_ref[:, 0:128] = first
            edge_ref[:, 128:256] = last
    sums_ref[:, 256:384] = left
    sums_ref[:, 384:512] = right


HBM = pl.BlockSpec(memory_space=pltpu.HBM)
ANY = pl.BlockSpec(memory_space=pl.ANY)


def row_sums(where, facts, x):
    return pl.pallas_call(
        row_sums_kernel,
        in_specs=[SMEM, VMEM, HBM],
        out_specs=[VMEM] * 5,
        out_shape=[jax.ShapeDtypeStruct((ROWS, 512), F32), jax.ShapeDtypeStruct((ROWS, 256), F32),
                   jax.ShapeDtypeStruct((FIELDS, LANES), F32), jax.ShapeDtypeStruct((8, LANES), F32),
                   jax.ShapeDtypeStruct((FIELDS, ROWS, COLS), F32)],
        scratch_shapes=[pltpu.VMEM((2, 3 * COLS, 256), BF16), pltpu.SemaphoreType.DMA((GROUPS,))],
        compiler_params=pltpu.CompilerParams(vmem_limit_bytes=WHOLE),
        name="row_sums",
    )(where, facts, x)


def zonal_difference(x):
    shape = x.shape
    axis = len(shape) - 1
    column = iota(shape, axis)
    ahead = jnp.where(column == COLS - 1, 0.0, pltpu.roll(x, COLS - 1, axis))
    behind = jnp.where(column == 0, 0.0, pltpu.roll(x, 1, axis))
    return 0.5 * (ahead - behind)


def local_sums_kernel(where_ref, table_ref, x_ref, _, out_ref):
    top = where_ref[0] == 0
    count = 2 * SCALES * GROUP
    shape = (count, LANES)
    out_row = iota(shape, 0)
    member = out_row & 7
    left_side = out_row < SCALES * GROUP
    lane = iota(shape, 1)
    source = jnp.where(lane >= ROWS, lane - ROWS, lane).astype(F32)
    used = lane < 2 * ROWS
    steps = jnp.where(left_side, ROWS - 1 - source, source)
    zeros = jnp.zeros((32, COLS), BF16)

    def weighted(matrix, x, i):
        mh, ml = split(jnp.where(used & (member == i), matrix, 0.0))
        xh, xl = split(x)
        return mm(jnp.concatenate([mh, ml[:, :ROWS]], axis=1), jnp.concatenate([xh, xl, zeros, xh], axis=0))

    def group_sums(group, wind):
        rate = table_ref[group * GROUP:(group + 1) * GROUP, :]
        row_rate = jnp.concatenate([rate[:, s:s + 1] for _ in range(2) for s in range(SCALES)], axis=0)
        wide = jnp.broadcast_to(row_rate, shape)
        plain = jnp.exp(-wide * steps)
        acc = jnp.zeros((count, COLS), F32)
        if wind:
            decay = jnp.exp(-wide)
            gain = 0.5 * (1.0 - decay * decay) / decay
            start = jnp.where(top & (source == 0.0), 0.5 * jnp.exp(-wide * ROWS), 0.0)
            slope = jnp.where(left_side, -gain * plain - start, gain * plain)
            second_sign = jnp.where(group == 0, 1.0, -1.0)
            for i in range(GROUP):
                acc += weighted(plain, -zonal_difference(x_ref[(1 - group) * GROUP + i]), i)
                acc += weighted(slope, second_sign * x_ref[group * GROUP + i], i)
        else:
            for i in range(GROUP):
                acc += weighted(plain, x_ref[group * GROUP + i], i)
        return acc, row_rate

    made = [group_sums(group, group < 2) for group in range(GROUPS)]
    acc = jnp.concatenate([m[0] for m in made], axis=0)
    factor = jnp.concatenate([jnp.broadcast_to(jnp.exp(-m[1]), (count, LANES)) for m in made], axis=0)
    factor = jnp.concatenate([factor] * PARTS, axis=1)
    column = iota(acc.shape, 1)
    forward, backward = acc, acc
    step = 1
    while step < COLS:
        forward = forward + factor * jnp.where(column >= step, pltpu.roll(forward, step, 1), 0.0)
        backward = backward + factor * jnp.where(column < COLS - step, pltpu.roll(backward, COLS - step, 1), 0.0)
        factor = factor * factor
        step *= 2
    acc = forward + backward - acc
    for group in range(GROUPS):
        for side in range(2):
            for s in range(SCALES):
                k = group * count + (side * SCALES + s) * GROUP
                out_ref[group // 3, side, s, group % 3] = acc[k:k + GROUP]


def local_sums(where, table, x, before):
    out = pl.pallas_call(
        local_sums_kernel,
        in_specs=[SMEM, VMEM, VMEM, ANY],
        out_specs=VMEM,
        out_shape=jax.ShapeDtypeStruct((2, 2, SCALES, 3, GROUP, COLS), F32),
        compiler_params=params(),
        cost_estimate=pl.CostEstimate(flops=6_000_000_000, bytes_accessed=4_000_000, transcendentals=0),
        name="local_sums",
    )(where, table, x, before)
    return out.reshape(2, 2 * HALF_ROWS, COLS)


def lon_merge_kernel(where_ref, lanes_ref, own_ref, g1_ref, g2_ref, g3_ref, _, part_ref, send_ref):
    y = where_ref[1] & 3
    high = where_ref[1] >= 4
    yf = y.astype(F32)
    zonal, _ = lane_kinds((1, LANES))
    lane = iota((1, LANES), 1)
    for tile in range(2):
        rate = lanes_ref[tile:tile + 1, :]
        step = lambda n: jnp.exp(-rate * (COLS * n))
        base = tile * 256
        lanes_l = slice(base, base + 128)
        lanes_r = slice(base + 128, base + 256)
        left_total = step(3.0 - yf) * own_ref[:, lanes_l]
        right_total = step(yf) * own_ref[:, lanes_r]
        left = jnp.zeros((ROWS, LANES), F32)
        right = jnp.zeros((ROWS, LANES), F32)
        for d, ref in ((1, g1_ref), (2, g2_ref), (3, g3_ref)):
            other = y ^ d
            of = other.astype(F32)
            below = other < y
            lg, rg = ref[:, lanes_l], ref[:, lanes_r]
            gap = jnp.abs(yf - of) - 1.0
            left = left + jnp.where(below, step(gap), 0.0) * lg
            right = right + jnp.where(below, 0.0, step(gap)) * rg
            left_total = left_total + step(3.0 - of) * lg
            right_total = right_total + step(of) * rg
        part_ref[:, lanes_l] = left
        part_ref[:, lanes_r] = right
        part_ref[:, 512 + tile * 128:640 + tile * 128] = left_total
        image = jnp.exp(-rate * (4.0 * COLS + 1.0))
        if tile == 0:
            image = jnp.where(zonal, -image, image)
            image = jnp.where(lane >= 96, -1.0, image)
            right_total = jnp.where(lane >= 96, 0.0, right_total)
        send_ref[:, tile * 128:tile * 128 + 128] = jnp.where(high, right_total - image * left_total, left_total)


def lon_merge(where, lanes, own, got, after):
    return pl.pallas_call(
        lon_merge_kernel,
        in_specs=[SMEM] + [VMEM] * 5 + [ANY],
        out_specs=[VMEM, VMEM],
        out_shape=[jax.ShapeDtypeStruct((ROWS, 768), F32), jax.ShapeDtypeStruct((ROWS, 256), F32)],
        compiler_params=params(),
        name="lon_merge",
    )(where, lanes, own, *got, after)


def spread_edges(tile):
    lane = iota(tile.shape, 1)
    out = tile
    for k in range(6):
        out = jnp.where((lane >> 4) == k, pltpu.roll(tile, (k * 16 + 32) % LANES, 1), out)
    return out


def column_sums_kernel(where_ref, table_ref, lanes_ref, part_ref, theirs_ref, edge_ref, local_ref,
                       carry_ref, keep_ref, send_ref):
    lat, lon = where_ref[0], where_ref[1]
    y = lon & 3
    yf = y.astype(F32)
    high = lon >= 4
    highf = jnp.where(high, 1.0, 0.0)
    lowf = 1.0 - highf
    lonf = lon.astype(F32)
    top = lat == 0
    rates = (lanes_ref[0:1, :], lanes_ref[1:2, :])
    zonal, sign = lane_kinds((1, LANES))
    row = fiota((ROWS, LANES), 0)
    weights = []
    for tile in range(2):
        rate = rates[tile]
        step = lambda n: jnp.exp(-rate * (COLS * n))
        decay = jnp.exp(-rate)
        theirs = theirs_ref[:, tile * 128:tile * 128 + 128]
        half = part_ref[:, 512 + tile * 128:640 + tile * 128]
        left = part_ref[:, tile * 256:tile * 256 + 128] + (highf * step(yf)) * theirs
        right = part_ref[:, tile * 256 + 128:tile * 256 + 256] + (lowf * step(3.0 - yf)) * theirs
        whole = (highf + lowf * step(4.0)) * half + (highf * step(4.0)) * theirs
        end = step(7.0 - lonf)
        weight_l = jnp.exp(-rate * (ROWS - 1 - row))
        weight_r = jnp.exp(-rate * row)
        carry_l = left
        carry_r = right - (end * decay) * whole
        if tile == 0:
            v0 = spread_edges(lowf * half + highf * theirs)
            vn = spread_edges(highf * half + lowf * theirs)
            gain = 0.5 * (1.0 - decay * decay) / decay
            initial = -0.5 * (v0 + vn / decay)
            zonal_l = step(lonf) * initial - gain * left + 0.5 * edge_ref[:, 0:128]
            zonal_r = (gain * right - 0.5 * edge_ref[:, 128:256]
                       + end * (gain * v0 - decay * (step(8.0) * initial - gain * whole)))
            carry_l = sign * jnp.where(zonal, zonal_l, carry_l)
            carry_r = sign * jnp.where(zonal, zonal_r, carry_r)
            start = jnp.where(top & (row == 0.0), 0.5 * jnp.exp(-rate * ROWS), 0.0)
            weight_l = jnp.where(zonal, weight_l, -gain * weight_l - start)
            weight_r = jnp.where(zonal, weight_r, gain * weight_r)
        carry_ref[:, tile * 256:tile * 256 + 128] = carry_l
        carry_ref[:, tile * 256 + 128:tile * 256 + 256] = carry_r
        fold = lambda w, c: jnp.sum(w * c, axis=0, keepdims=True)
        weights.append(((fold(weight_l, carry_l), fold(weight_l, carry_r)),
                        (fold(weight_r, carry_l), fold(weight_r, carry_r))))
    shape = (HALF_ROWS, LANES)
    lane, lane_scale, _, wind_field, rest_field = lane_fields(shape)
    out_row = iota(shape, 0)
    scale = jnp.where(out_row < HALF, 0, jnp.where(out_row < 2 * HALF, 1, 2))
    core = lat & 1
    column = fiota((HALF_ROWS, COLS), 1)
    for ref, half in ((send_ref, 1 - core), (keep_ref, core)):
        field = out_row - scale * HALF + half * HALF
        same = lane_scale == scale
        wind = same & (wind_field == field)
        rest = same & (rest_field == field)
        rate = table_ref[pl.ds(pl.multiple_of(half * HALF, 8), HALF), :]
        rate = jnp.concatenate([rate[:, s:s + 1] for s in range(SCALES)], axis=0)
        fall = jnp.exp(-rate * (column + 1.0))
        rise = jnp.exp(-rate * (COLS - column))
        for side in range(2):
            pick = lambda k: jnp.sum(
                jnp.where(wind, weights[0][side][k], 0.0) + jnp.where(rest, weights[1][side][k], 0.0),
                axis=1, keepdims=True)
            rows = slice(side * HALF_ROWS, (side + 1) * HALF_ROWS)
            ref[rows, :] = local_ref[half, rows, :] + pick(0) * fall + pick(1) * rise


def column_sums(where, table, lanes, part, theirs, edge, local):
    half = jax.ShapeDtypeStruct((2 * HALF_ROWS, COLS), F32)
    return pl.pallas_call(
        column_sums_kernel,
        in_specs=[SMEM] + [VMEM] * 6,
        out_specs=[VMEM] * 3,
        out_shape=[jax.ShapeDtypeStruct((ROWS, 512), F32), half, half],
        compiler_params=params(),
        name="column_sums",
    )(where, table, lanes, part, theirs, edge, local)


LEFT = slice(0, HALF_ROWS)
RIGHT = slice(HALF_ROWS, 2 * HALF_ROWS)
STEPS = 21


def steps_kernel(where_ref, table_ref, _, out_ref):
    lat = where_ref[0]
    odd = (lat & 1) == 1
    odd_chip = ((lat >> 1) & 1) == 1
    z = lat >> 2
    zf = z.astype(F32)
    rate = table_ref[pl.ds(pl.multiple_of((lat & 1) * HALF, 8), HALF), :]
    rate = jnp.concatenate([rate[:, s:s + 1] for s in range(SCALES)], axis=0)
    rate = jnp.broadcast_to(rate, (HALF_ROWS, LANES))
    power = lambda n: jnp.exp(-rate * n)
    quad = lambda n: power(4.0 * ROWS * n)
    one, zero = jnp.ones_like(rate), jnp.zeros_like(rate)
    device, chip = power(1.0 * ROWS), power(2.0 * ROWS)
    out = [jnp.where(odd, one, device), jnp.where(odd, device, one)]
    out += [jnp.where(odd_chip, one, chip), jnp.where(odd_chip, chip, one)]
    out += [power(1.0 + 4 * ROWS * jnp.maximum(7.0 - 2.0 * zf, 1.0))]
    for d in (1, 2, 3):
        other = z ^ d
        of = other.astype(F32)
        below = other < z
        gap = quad(jnp.abs(zf - of) - 1.0)
        out += [jnp.where(below, gap, zero), jnp.where(below, zero, gap), jnp.where(below, quad(3.0 - of), zero)]
    out += [quad(3.0 - zf), quad(3.0 - zf) * power(1.0)]
    out += [jnp.where(odd_chip, chip, one), jnp.where(odd_chip, one, zero)]
    out += [jnp.where(odd_chip, one, chip), jnp.where(odd_chip, zero, one)]
    out += [device]
    for k, value in enumerate(out):
        out_ref[k] = value


def lat_steps(where, table, before):
    return pl.pallas_call(
        steps_kernel,
        in_specs=[SMEM, VMEM, ANY],
        out_specs=VMEM,
        out_shape=jax.ShapeDtypeStruct((STEPS, HALF_ROWS, LANES), F32),
        compiler_params=params(),
        name="lat_steps",
    )(where, table, before)


def by_tile(body):
    for b in range(PARTS):
        body(slice(b * LANES, (b + 1) * LANES))


def chip_merge_kernel(steps_ref, keep_ref, got_ref, chip_ref):
    def body(lanes):
        mine, other = steps_ref[0], steps_ref[1]
        chip_ref[LEFT, lanes] = mine * keep_ref[LEFT, lanes] + other * got_ref[LEFT, lanes]
        chip_ref[RIGHT, lanes] = other * keep_ref[RIGHT, lanes] + mine * got_ref[RIGHT, lanes]

    by_tile(body)


def chip_merge(steps, keep, got):
    return pl.pallas_call(
        chip_merge_kernel,
        in_specs=[VMEM] * 3,
        out_specs=VMEM,
        out_shape=jax.ShapeDtypeStruct((2 * HALF_ROWS, COLS), F32),
        compiler_params=params(),
        name="chip_merge",
    )(steps, keep, got)


def quad_merge_kernel(where_ref, steps_ref, chip_ref, pair_ref, _, left_ref, s1_ref, s2_ref, s3_ref):
    z = where_ref[0] >> 2

    def body(lanes):
        mine, other, image = steps_ref[2], steps_ref[3], steps_ref[4]
        left = mine * chip_ref[LEFT, lanes] + other * pair_ref[LEFT, lanes]
        right = other * chip_ref[RIGHT, lanes] + mine * pair_ref[RIGHT, lanes]
        back = right - image * left
        left_ref[:, lanes] = left
        for d, ref in ((1, s1_ref), (2, s2_ref), (3, s3_ref)):
            ref[:, lanes] = jnp.where((z ^ d) > z, left, back)

    by_tile(body)


def quad_merge(where, steps, chip, pair, after):
    one = jax.ShapeDtypeStruct((HALF_ROWS, COLS), F32)
    return pl.pallas_call(
        quad_merge_kernel,
        in_specs=[SMEM] + [VMEM] * 3 + [ANY],
        out_specs=[VMEM] * 4,
        out_shape=[one] * 4,
        compiler_params=params(),
        name="quad_merge",
    )(where, steps, chip, pair, after)


def lat_carry_kernel(where_ref, steps_ref, keep_ref, got_ref, pair_ref, left_ref, g1_ref, g2_ref, g3_ref, _,
                     own_ref, send_ref):
    odd = (where_ref[0] & 1) == 1

    def body(lanes):
        left, right, whole = 0.0, 0.0, steps_ref[14] * left_ref[:, lanes]
        for k, ref in ((5, g1_ref), (8, g2_ref), (11, g3_ref)):
            g = ref[:, lanes]
            left = left + steps_ref[k] * g
            right = right + steps_ref[k + 1] * g
            whole = whole + steps_ref[k + 2] * g
        right = right - steps_ref[15] * whole
        left = steps_ref[16] * left + steps_ref[17] * pair_ref[LEFT, lanes]
        right = steps_ref[18] * right + steps_ref[19] * pair_ref[RIGHT, lanes]
        low_left = jnp.where(odd, got_ref[LEFT, lanes], keep_ref[LEFT, lanes])
        high_right = jnp.where(odd, keep_ref[RIGHT, lanes], got_ref[RIGHT, lanes])
        high_l = low_left + steps_ref[20] * left
        low_r = high_right + steps_ref[20] * right
        own_ref[LEFT, lanes] = jnp.where(odd, high_l, left)
        own_ref[RIGHT, lanes] = jnp.where(odd, right, low_r)
        send_ref[LEFT, lanes] = jnp.where(odd, left, high_l)
        send_ref[RIGHT, lanes] = jnp.where(odd, low_r, right)

    by_tile(body)


def lat_carry(where, steps, keep, got, pair, left, gs, after):
    half = jax.ShapeDtypeStruct((2 * HALF_ROWS, COLS), F32)
    return pl.pallas_call(
        lat_carry_kernel,
        in_specs=[SMEM] + [VMEM] * 8 + [ANY],
        out_specs=[VMEM] * 2,
        out_shape=[half, half],
        compiler_params=params(),
        name="lat_carry",
    )(where, steps, keep, got, pair, left, *gs, after)


def local_filter_kernel(starts, use_x, use_carry, where_ref, table_ref, carry_ref, x_ref, base_ref, out_ref):
    top = where_ref[0] == 0
    shape = (ROWS, LANES)
    row = fiota(shape, 0)
    lane = iota(shape, 1)
    source = jnp.where(lane >= ROWS, lane - ROWS, lane).astype(F32)
    used = lane < 2 * ROWS
    gap = jnp.abs(row - source)
    gap_low = jnp.abs(source - 1.0 - row)
    gap_high = jnp.abs(source + 1.0 - row)
    first = source == 0.0
    spread = jnp.abs(fiota((LANES, LANES), 0) - fiota((LANES, LANES), 1))
    tag = lane & 31
    corner = jnp.zeros((LANES, LANES), BF16)
    left_lane = (lane == LANES - 1) | (lane == 1) | (lane == 3)
    flat = lane[:1]
    row_scale = jnp.where((flat == LANES - 1) | (flat == 0), 0, jnp.where(flat <= 2, 1, 2))
    base = iota((8, LANES), 0)
    column = fiota((8, LANES), 1)

    def carry_tile(tile, virtual):
        left = carry_ref[:, tile * 256:tile * 256 + 128]
        right = carry_ref[:, tile * 256 + 128:tile * 256 + 256]
        left = pltpu.roll(left, (LANES - virtual) % LANES, 1)
        right = pltpu.roll(right, (LANES + 1 - virtual) % LANES, 1)
        return jnp.where(tag == 0, left, jnp.where(tag == 1, right, 0.0))

    def column_pass(matrices, x, carry):
        parts = [split(jnp.where(used, m, 0.0)) for m in matrices]
        lhs = jnp.concatenate([jnp.concatenate([mh, ml[:, :ROWS]], axis=1) for mh, ml in parts], axis=0)
        wide = [t for t in (x, carry) if t is not None]
        wide = wide[0] if len(wide) == 1 else jnp.concatenate(wide, axis=1)
        xh, xl = split(wide)
        rhs = jnp.concatenate([xh, xl, jnp.zeros((32, wide.shape[1]), BF16), xh], axis=0)
        return mm(lhs, rhs)

    def column_stage(f, wind):
        facts = table_ref[pl.ds(f, 1), :]
        rates = [facts[:, s:s + 1] for s in range(SCALES)]
        gains = [facts[:, SCALES + s:SCALES + s + 1] for s in range(SCALES)]
        plain = [gains[s] * jnp.exp(-rates[s] * gap) for s in range(SCALES)]
        if wind:
            slopes = []
            for s in range(SCALES):
                slope = jnp.exp(-rates[s] * gap_low) - jnp.exp(-rates[s] * gap_high)
                slope = slope - jnp.where(top & first, jnp.exp(-rates[s] * (row + 1.0)), 0.0)
                slopes.append((0.5 * gains[s]) * slope)
            stream = f < GROUP
            second_sign = 1.0 if stream else -1.0
            meridional = f if stream else f + 16
            zonal = f + 8
            pair = f + 8 if stream else f - 8
            w = column_pass(plain, -zonal_difference(x_ref[pair]), carry_tile(0, zonal))
            w = w + column_pass(slopes, second_sign * x_ref[f], carry_tile(0, meridional))
        else:
            w = column_pass(plain, x_ref[f] if use_x else None, carry_tile(1, f - WINDS) if use_carry else None)
        return rates, w

    def row_stage(rates, w):
        outs = []
        for s in range(SCALES):
            rows = slice(s * ROWS, (s + 1) * ROWS)
            stack = jnp.concatenate([w[rows, b * LANES:(b + 1) * LANES] for b in range(PARTS)], axis=0)
            wh, wl = split(stack)
            th, tl = split(jnp.exp(-rates[s] * spread))
            lhs = jnp.concatenate([wh, wl], axis=1)
            rhs = jnp.concatenate([jnp.concatenate([th, tl], axis=1), jnp.concatenate([th, corner], axis=1)], axis=0)
            out = mm(lhs, rhs)
            outs.append(out[:, :LANES] + out[:, LANES:])
        return outs

    def carry_stage(rates, w, outs):
        sums, outer = None, jnp.zeros((ROWS, LANES), F32)
        for s in range(SCALES):
            here = row_scale == s
            if use_carry:
                moved = pltpu.roll(w[s * ROWS:(s + 1) * ROWS, w.shape[1] - LANES:], LANES - 30 * s - 1, 1)
                outer = moved if s == 0 else jnp.where(here, moved, outer)
            if use_x:
                turned = outs[s] if s == 0 else pltpu.roll(outs[s], 2 * s, 1)
                sums = turned if s == 0 else jnp.where(here, turned, sums)
        rate_row = jnp.where(row_scale == 0, rates[0], jnp.where(row_scale == 1, rates[1], rates[2]))
        jump = jnp.exp(-rate_row * LANES)
        from_left, from_right = [outer], [outer]
        for b in range(PARTS - 1):
            ahead, behind = jump * from_left[-1], jump * from_right[-1]
            if use_x:
                ahead = ahead + sums[b * ROWS:(b + 1) * ROWS]
                behind = behind + sums[(PARTS - 1 - b) * ROWS:(PARTS - b) * ROWS]
            from_left.append(ahead)
            from_right.append(behind)
        carries = [jnp.where(left_lane, from_left[b], from_right[PARTS - 1 - b]) for b in range(PARTS)]
        ch, cl = split(jnp.concatenate(carries, axis=0))
        low_rate = jnp.where(base == 0, rates[0], jnp.where(base <= 2, rates[1], rates[2]))
        low_left = (base == 1) | (base == 3)
        low = jnp.where(base <= 4, jnp.exp(-low_rate * jnp.where(low_left, column + 1.0, LANES - column)), 0.0)
        high = jnp.where(base == 7, jnp.exp(-rates[0] * (column + 1.0)), 0.0)
        pad = jnp.zeros((8, LANES), F32)
        lh, ll = split(jnp.concatenate([low, pad], axis=0))
        hh, hl = split(jnp.concatenate([pad, high], axis=0))
        gap_rows = jnp.zeros((96, LANES), BF16)
        bh = jnp.concatenate([lh, gap_rows, hh], axis=0)
        bl = jnp.concatenate([ll, gap_rows, hl], axis=0)
        rhs = jnp.concatenate([jnp.concatenate([bh, bl], axis=1), jnp.concatenate([bh, corner], axis=1)], axis=0)
        return jnp.concatenate([ch, cl], axis=1), rhs

    for start in starts:
        wind = start < WINDS
        fields = [start + i for i in range(GROUP)]
        columns = [column_stage(f, wind) for f in fields]
        outs = [row_stage(*c) if use_x else None for c in columns]
        ranks = [carry_stage(*c, o) for c, o in zip(columns, outs)]
        for f, o, (lhs, rhs) in zip(fields, outs, ranks):
            out = mm(lhs, rhs)
            total = out[:, :LANES] + out[:, LANES:]
            if use_x:
                total = (o[0] + o[1]) + (o[2] + total)
            for b in range(PARTS):
                lanes = slice(b * LANES, (b + 1) * LANES)
                part = total[b * ROWS:(b + 1) * ROWS]
                if base_ref is not None:
                    part = part + base_ref[f - starts[0], :, lanes]
                out_ref[f - starts[0], :, lanes] = part


def local_filter(where, table, carry, x, first, count, before, base=None):
    starts = tuple(range(first, first + count, GROUP))
    use_x, use_carry = base is None, carry is not None
    names = ["where", "table"] + ["carry"] * use_carry + ["x"] * use_x + ["base"] * (base is not None) + ["before"]
    arrays = {"where": where, "table": table, "carry": carry, "x": x, "base": base, "before": before}
    specs = {"where": SMEM, "before": ANY}

    def body(*refs):
        by_name = dict(zip(names, refs))
        local_filter_kernel(starts, use_x, use_carry, by_name["where"], by_name["table"], by_name.get("carry"),
                            by_name.get("x"), by_name.get("base"), refs[len(names)])

    return pl.pallas_call(
        body,
        in_specs=[specs.get(n, VMEM) for n in names],
        out_specs=VMEM,
        out_shape=jax.ShapeDtypeStruct((count, ROWS, COLS), F32),
        compiler_params=params(),
        cost_estimate=pl.CostEstimate(flops=count * 300_000_000, bytes_accessed=count * 150_000, transcendentals=0),
        name="local_filter",
    )(*[arrays[n] for n in names])


def add_carries(half, table_ref, carry_ref, z_refs, part, store):
    row = fiota((8, LANES), 0)
    up_steps, down_steps = row + 1.0, 8.0 - row
    tables = [carry_ref[side, s, part] for side in range(2) for s in range(SCALES)]
    start = pl.multiple_of((half * 3 + part) * GROUP, GROUP)
    group_facts = table_ref[pl.ds(start, GROUP), :]
    for i in range(GROUP):
        facts = group_facts[i:i + 1, :]
        ups = []
        for s in range(SCALES):
            r = jnp.broadcast_to(facts[:, s:s + 1], (8, LANES))
            w = jnp.broadcast_to(facts[:, SCALES + s:SCALES + s + 1], (8, LANES))
            jump = jnp.exp(-8.0 * r)
            up, down = [w * jnp.exp(-r * up_steps)], [w * jnp.exp(-r * down_steps)]
            for _ in range(ROWS // 8 - 1):
                up.append(up[-1] * jump)
                down.insert(0, down[0] * jump)
            ups.append((jnp.concatenate(up, axis=0), jnp.concatenate(down, axis=0)))
        for b in range(PARTS):
            lanes = slice(b * LANES, (b + 1) * LANES)
            total = jnp.where(half == 0, z_refs[part // 2][part % 2 * GROUP + i, :, lanes],
                              z_refs[(3 + part) // 2][(3 + part) % 2 * GROUP + i, :, lanes])
            for s in range(SCALES):
                total = total + ups[s][0] * tables[s][i:i + 1, lanes] + ups[s][1] * tables[SCALES + s][i:i + 1, lanes]
            store(i, lanes, total)


def finish_own_kernel(where_ref, table_ref, carry_ref, z0_ref, z1_ref, z2_ref, out_ref):
    for part in range(3):
        def store(i, lanes, value):
            out_ref[part * GROUP + i, :, lanes] = value

        add_carries(where_ref[0] & 1, table_ref, carry_ref, (z0_ref, z1_ref, z2_ref), part, store)


def finish_own(where, table, carry, parts):
    return pl.pallas_call(
        finish_own_kernel,
        in_specs=[SMEM] + [VMEM] * 5,
        out_specs=VMEM,
        out_shape=jax.ShapeDtypeStruct((HALF, ROWS, COLS), F32),
        compiler_params=params(),
        cost_estimate=pl.CostEstimate(flops=1_000_000_000, bytes_accessed=2_000_000, transcendentals=0),
        name="finish_own",
    )(where, table, carry.reshape(2, SCALES, 3, GROUP, COLS), *parts)


def finish_kernel(where_ref, table_ref, carry_ref, z0_ref, z1_ref, z2_ref, own_ref, out_ref, buf_ref, sem):
    half = 1 - (where_ref[0] & 1)
    ready = pltpu.make_async_copy(own_ref, out_ref.at[pl.ds((1 - half) * HALF, HALF)], sem.at[3])
    ready.start()
    copies = [ready]
    for part in range(3):
        def store(i, lanes, value):
            buf_ref[part, i, :, lanes] = value

        add_carries(half, table_ref, carry_ref, (z0_ref, z1_ref, z2_ref), part, store)
        there = out_ref.at[pl.ds((half * 3 + part) * GROUP, GROUP)]
        copies.append(pltpu.make_async_copy(buf_ref.at[part], there, sem.at[part]))
        copies[-1].start()
    for copy in copies:
        copy.wait()


def finish(where, table, carry, parts, own):
    return pl.pallas_call(
        finish_kernel,
        in_specs=[SMEM] + [VMEM] * 6,
        out_specs=HBM,
        out_shape=jax.ShapeDtypeStruct((FIELDS, ROWS, COLS), F32),
        scratch_shapes=[pltpu.VMEM((3, GROUP, ROWS, COLS), F32), pltpu.SemaphoreType.DMA((4,))],
        compiler_params=params(),
        name="finish",
    )(where, table, carry.reshape(2, SCALES, 3, GROUP, COLS), *parts, own)


def partner(axis, count, bit):
    return functools.partial(lax.ppermute, axis_name=axis, perm=[(i, i ^ bit) for i in range(count)])


def shards(x, lengths, weights):
    where = jnp.stack([lax.axis_index("lat"), lax.axis_index("lon")]).astype(jnp.int32)
    facts = jnp.concatenate([lengths.T, weights.T], axis=0)
    sums, edge, table, lanes, held = row_sums(where, facts, x)
    got = [partner("lon", NLON, d)(sums) for d in (1, 2, 3)]
    early = local_filter(where, table, None, held, 32, 16, sums)
    part, half = lon_merge(where, lanes, sums, got, early)
    theirs = partner("lon", NLON, 4)(half)
    local = local_sums(where, table, held, part)
    steps = lat_steps(where, table, part)
    carry, keep, send = column_sums(where, table, lanes, part, theirs, edge, local)
    got_core = partner("lat", NLAT, 1)(send)
    chip = chip_merge(steps, keep, got_core)
    pair = partner("lat", NLAT, 2)(chip)
    z0 = local_filter(where, table, carry, held, 0, 16, chip)
    left, *sends = quad_merge(where, steps, chip, pair, z0)
    gs = [partner("lat", NLAT, 4 * d)(t) for d, t in zip((1, 2, 3), sends)]
    z1 = local_filter(where, table, carry, held, 16, 16, left)
    z2 = local_filter(where, table, carry, held, 32, 16, z1, early)
    own, other = lat_carry(where, steps, keep, got_core, pair, left, gs, z2)
    got_carry = partner("lat", NLAT, 1)(other)
    done = finish_own(where, table, own, (z0, z1, z2))
    return finish(where, table, got_carry, (z0, z1, z2), done)


def solution(mesh):
    in_specs = (P(None, "lat", "lon"), P(), P())
    out_specs = P(None, "lat", "lon")
    return jax.shard_map(shards, mesh=mesh, in_specs=in_specs, out_specs=out_specs, check_vma=False)
```

```python
import functools

import jax
import jax.numpy as jnp
from jax import lax
from jax.experimental import pallas as pl
from jax.experimental.pallas import tpu as pltpu
from jax.sharding import PartitionSpec as P

LEVELS = 8
SCALES = 3
WINDS = 16
FIELDS = 48
ROWS = 48
COLS = 384
GROUP = 8
GROUPS = FIELDS // GROUP
NLAT = 16
NLON = 8
LANES = 128
PARTS = COLS // LANES
HALF = FIELDS // 2
HALF_ROWS = SCALES * HALF
F32 = jnp.float32
BF16 = jnp.bfloat16

VMEM = pl.BlockSpec(memory_space=pltpu.VMEM)
SMEM = pl.BlockSpec(memory_space=pltpu.SMEM)
BIG = 48 * 1024 * 1024
WHOLE = 50 * 1024 * 1024


def params(**kw):
    return pltpu.CompilerParams(vmem_limit_bytes=BIG, **kw)


def iota(shape, dim):
    return lax.broadcasted_iota(jnp.int32, shape, dim)


def fiota(shape, dim):
    return iota(shape, dim).astype(F32)


def split(value):
    high = value.astype(BF16)
    return high, (value - high.astype(F32)).astype(BF16)


def mm(a, b):
    return jnp.dot(a, b, preferred_element_type=F32)


def lane_fields(shape):
    lane = iota(shape, 1)
    virtual = lane & 31
    wind_field = ((virtual >> 4) << 3) + (virtual & 7)
    return lane, lane >> 5, virtual, wind_field, virtual + WINDS


def exact(a, b, dims):
    return lax.dot_general(a, b, (dims, ((), ())), precision=lax.Precision.HIGHEST, preferred_element_type=F32)


def lane_rates(rate):
    shape = (FIELDS, LANES)
    _, _, _, wind_field, rest_field = lane_fields(shape)
    field = iota(shape, 0)
    lane = iota((1, LANES), 1)

    def pick(which):
        every = exact(rate, jnp.where(field == which, 1.0, 0.0).astype(F32), ((1,), (0,)))
        value = jnp.where(lane < 32, every[0:1], jnp.where(lane < 64, every[1:2], every[2:3]))
        return jnp.where(lane < 96, value, 0.0)

    return pick(wind_field), pick(rest_field)


def scale_weights(rate, weights):
    decay = jnp.exp(-rate)
    leak = 1.0 - decay
    cube = (1.0 + decay) * (1.0 + decay) * (1.0 + decay)
    coefficient = weights * cube / (leak * (1.0 + decay * decay))
    kappa = leak / (1.0 + decay)
    return coefficient * kappa * kappa


def lane_kinds(shape):
    _, _, virtual, _, _ = lane_fields(shape)
    second = virtual >= 16
    north = (virtual & 15) >= 8
    zonal = second != north
    sign = jnp.where(second | north, -1.0, 1.0).astype(F32)
    return zonal, sign


def row_sums_kernel(where_ref, len_ref, x_ref, sums_ref, edge_ref, table_ref, lanes_ref, held_ref, w_ref, sem):
    lon = where_ref[1]
    copies = []
    for k, (start, stop) in enumerate(((0, WINDS), (WINDS, FIELDS))):
        here = pl.ds(start, stop - start)
        copies.append(pltpu.make_async_copy(x_ref.at[here], held_ref.at[here], sem.at[k]))
        copies[-1].start()
    rate = 1.0 / len_ref[0:SCALES, :]
    pair = lane_rates(rate)
    lanes_ref[...] = jnp.concatenate([pair[0], pair[1], jnp.ones((6, LANES), F32)], axis=0)
    column = fiota((COLS, LANES), 0)
    for tile, rates in enumerate(pair):
        for side, steps in enumerate((COLS - 1 - column, column)):
            high, low = split(jnp.exp(-rates * steps))
            lanes = slice(side * LANES, (side + 1) * LANES)
            w_ref[tile, 0:COLS, lanes] = high
            w_ref[tile, COLS:2 * COLS, lanes] = high
            w_ref[tile, 2 * COLS:, lanes] = low
    both = jnp.concatenate([rate, scale_weights(rate, len_ref[SCALES:, :]), jnp.ones((2, FIELDS), F32)], axis=0)
    eye = jnp.where(iota((8, LANES), 0) == iota((8, LANES), 1), 1.0, 0.0).astype(F32)
    table_ref[...] = exact(both, eye, ((0,), (0,)))
    lane = iota((ROWS, LANES), 1)
    virtual = lane & 31
    zero = jnp.zeros((ROWS, LANES), F32)
    left, right, first, last = zero, zero, zero, zero
    for g in range(GROUPS):
        if g in (0, 2):
            copies[g // 2].wait()
        x = held_ref[g * GROUP:(g + 1) * GROUP].reshape(GROUP * ROWS, COLS)
        xh, xl = split(x)
        res = mm(jnp.concatenate([xh, xl, xh], axis=1), w_ref[0 if g < 2 else 1])
        if g == 2:
            left, right = zero, zero
        for i in range(GROUP):
            rows = slice(i * ROWS, (i + 1) * ROWS)
            mine = (virtual & 15) == g * GROUP + i if g < 2 else virtual == (g - 2) * GROUP + i
            left = jnp.where(mine, res[rows, 0:128], left)
            right = jnp.where(mine, res[rows, 128:256], right)
            if g < 2:
                first = jnp.where(mine, x[rows, 0:1], first)
                last = jnp.where(mine, x[rows, COLS - 1:COLS], last)
        if g == 1:
            edge = jnp.where(lon == 0, first, jnp.where(lon == NLON - 1, last, 0.0))
            sums_ref[:, 0:128] = jnp.where(lane >= 96, edge, left)
            sums_ref[:, 128:256] = right
            edge_ref[:, 0:128] = first
            edge_ref[:, 128:256] = last
    sums_ref[:, 256:384] = left
    sums_ref[:, 384:512] = right


HBM = pl.BlockSpec(memory_space=pltpu.HBM)
ANY = pl.BlockSpec(memory_space=pl.ANY)


def row_sums(where, facts, x):
    return pl.pallas_call(
        row_sums_kernel,
        in_specs=[SMEM, VMEM, HBM],
        out_specs=[VMEM] * 5,
        out_shape=[jax.ShapeDtypeStruct((ROWS, 512), F32), jax.ShapeDtypeStruct((ROWS, 256), F32),
                   jax.ShapeDtypeStruct((FIELDS, LANES), F32), jax.ShapeDtypeStruct((8, LANES), F32),
                   jax.ShapeDtypeStruct((FIELDS, ROWS, COLS), F32)],
        scratch_shapes=[pltpu.VMEM((2, 3 * COLS, 256), BF16), pltpu.SemaphoreType.DMA((2,))],
        compiler_params=pltpu.CompilerParams(vmem_limit_bytes=WHOLE),
        name="row_sums",
    )(where, facts, x)


def zonal_difference(x):
    shape = x.shape
    axis = len(shape) - 1
    column = iota(shape, axis)
    ahead = jnp.where(column == COLS - 1, 0.0, pltpu.roll(x, COLS - 1, axis))
    behind = jnp.where(column == 0, 0.0, pltpu.roll(x, 1, axis))
    return 0.5 * (ahead - behind)


def local_sums_kernel(where_ref, table_ref, x_ref, _, out_ref):
    top = where_ref[0] == 0
    count = 2 * SCALES * GROUP
    shape = (count, LANES)
    out_row = iota(shape, 0)
    member = out_row & 7
    left_side = out_row < SCALES * GROUP
    lane = iota(shape, 1)
    source = jnp.where(lane >= ROWS, lane - ROWS, lane).astype(F32)
    used = lane < 2 * ROWS
    steps = jnp.where(left_side, ROWS - 1 - source, source)
    zeros = jnp.zeros((32, COLS), BF16)

    def weighted(matrix, x, i):
        mh, ml = split(jnp.where(used & (member == i), matrix, 0.0))
        xh, xl = split(x)
        return mm(jnp.concatenate([mh, ml[:, :ROWS]], axis=1), jnp.concatenate([xh, xl, zeros, xh], axis=0))

    def group_sums(group, wind):
        rate = table_ref[group * GROUP:(group + 1) * GROUP, :]
        row_rate = jnp.concatenate([rate[:, s:s + 1] for _ in range(2) for s in range(SCALES)], axis=0)
        wide = jnp.broadcast_to(row_rate, shape)
        plain = jnp.exp(-wide * steps)
        acc = jnp.zeros((count, COLS), F32)
        if wind:
            decay = jnp.exp(-wide)
            gain = 0.5 * (1.0 - decay * decay) / decay
            start = jnp.where(top & (source == 0.0), 0.5 * jnp.exp(-wide * ROWS), 0.0)
            slope = jnp.where(left_side, -gain * plain - start, gain * plain)
            second_sign = jnp.where(group == 0, 1.0, -1.0)
            for i in range(GROUP):
                acc += weighted(plain, -zonal_difference(x_ref[(1 - group) * GROUP + i]), i)
                acc += weighted(slope, second_sign * x_ref[group * GROUP + i], i)
        else:
            for i in range(GROUP):
                acc += weighted(plain, x_ref[group * GROUP + i], i)
        return acc, row_rate

    made = [group_sums(group, group < 2) for group in range(GROUPS)]
    acc = jnp.concatenate([m[0] for m in made], axis=0)
    factor = jnp.concatenate([jnp.broadcast_to(jnp.exp(-m[1]), (count, LANES)) for m in made], axis=0)
    factor = jnp.concatenate([factor] * PARTS, axis=1)
    column = iota(acc.shape, 1)
    forward, backward = acc, acc
    step = 1
    while step < COLS:
        forward = forward + factor * jnp.where(column >= step, pltpu.roll(forward, step, 1), 0.0)
        backward = backward + factor * jnp.where(column < COLS - step, pltpu.roll(backward, COLS - step, 1), 0.0)
        factor = factor * factor
        step *= 2
    acc = forward + backward - acc
    for group in range(GROUPS):
        for side in range(2):
            for s in range(SCALES):
                k = group * count + (side * SCALES + s) * GROUP
                out_ref[group // 3, side, s, group % 3] = acc[k:k + GROUP]


def local_sums(where, table, x, before):
    out = pl.pallas_call(
        local_sums_kernel,
        in_specs=[SMEM, VMEM, VMEM, ANY],
        out_specs=VMEM,
        out_shape=jax.ShapeDtypeStruct((2, 2, SCALES, 3, GROUP, COLS), F32),
        compiler_params=params(),
        cost_estimate=pl.CostEstimate(flops=600000000, bytes_accessed=4_000_000, transcendentals=0),
        name="local_sums",
    )(where, table, x, before)
    return out.reshape(2, 2 * HALF_ROWS, COLS)


def lon_merge_kernel(where_ref, lanes_ref, own_ref, g1_ref, g2_ref, g3_ref, _, part_ref, send_ref):
    y = where_ref[1] & 3
    high = where_ref[1] >= 4
    yf = y.astype(F32)
    zonal, _ = lane_kinds((1, LANES))
    lane = iota((1, LANES), 1)
    for tile in range(2):
        rate = lanes_ref[tile:tile + 1, :]
        step = lambda n: jnp.exp(-rate * (COLS * n))
        base = tile * 256
        lanes_l = slice(base, base + 128)
        lanes_r = slice(base + 128, base + 256)
        left_total = step(3.0 - yf) * own_ref[:, lanes_l]
        right_total = step(yf) * own_ref[:, lanes_r]
        left = jnp.zeros((ROWS, LANES), F32)
        right = jnp.zeros((ROWS, LANES), F32)
        for d, ref in ((1, g1_ref), (2, g2_ref), (3, g3_ref)):
            other = y ^ d
            of = other.astype(F32)
            below = other < y
            lg, rg = ref[:, lanes_l], ref[:, lanes_r]
            gap = jnp.abs(yf - of) - 1.0
            left = left + jnp.where(below, step(gap), 0.0) * lg
            right = right + jnp.where(below, 0.0, step(gap)) * rg
            left_total = left_total + step(3.0 - of) * lg
            right_total = right_total + step(of) * rg
        part_ref[:, lanes_l] = left
        part_ref[:, lanes_r] = right
        part_ref[:, 512 + tile * 128:640 + tile * 128] = left_total
        image = jnp.exp(-rate * (4.0 * COLS + 1.0))
        if tile == 0:
            image = jnp.where(zonal, -image, image)
            image = jnp.where(lane >= 96, -1.0, image)
            right_total = jnp.where(lane >= 96, 0.0, right_total)
        send_ref[:, tile * 128:tile * 128 + 128] = jnp.where(high, right_total - image * left_total, left_total)


def lon_merge(where, lanes, own, got, after):
    return pl.pallas_call(
        lon_merge_kernel,
        in_specs=[SMEM] + [VMEM] * 5 + [ANY],
        out_specs=[VMEM, VMEM],
        out_shape=[jax.ShapeDtypeStruct((ROWS, 768), F32), jax.ShapeDtypeStruct((ROWS, 256), F32)],
        compiler_params=params(),
        name="lon_merge",
    )(where, lanes, own, *got, after)


def spread_edges(tile):
    lane = iota(tile.shape, 1)
    out = tile
    for k in range(6):
        out = jnp.where((lane >> 4) == k, pltpu.roll(tile, (k * 16 + 32) % LANES, 1), out)
    return out


def column_sums_kernel(where_ref, table_ref, lanes_ref, part_ref, theirs_ref, edge_ref, local_ref,
                       carry_ref, keep_ref, send_ref):
    lat, lon = where_ref[0], where_ref[1]
    y = lon & 3
    yf = y.astype(F32)
    high = lon >= 4
    highf = jnp.where(high, 1.0, 0.0)
    lowf = 1.0 - highf
    lonf = lon.astype(F32)
    top = lat == 0
    rates = (lanes_ref[0:1, :], lanes_ref[1:2, :])
    zonal, sign = lane_kinds((1, LANES))
    row = fiota((ROWS, LANES), 0)
    weights = []
    for tile in range(2):
        rate = rates[tile]
        step = lambda n: jnp.exp(-rate * (COLS * n))
        decay = jnp.exp(-rate)
        theirs = theirs_ref[:, tile * 128:tile * 128 + 128]
        half = part_ref[:, 512 + tile * 128:640 + tile * 128]
        left = part_ref[:, tile * 256:tile * 256 + 128] + (highf * step(yf)) * theirs
        right = part_ref[:, tile * 256 + 128:tile * 256 + 256] + (lowf * step(3.0 - yf)) * theirs
        whole = (highf + lowf * step(4.0)) * half + (highf * step(4.0)) * theirs
        end = step(7.0 - lonf)
        weight_l = jnp.exp(-rate * (ROWS - 1 - row))
        weight_r = jnp.exp(-rate * row)
        carry_l = left
        carry_r = right - (end * decay) * whole
        if tile == 0:
            v0 = spread_edges(lowf * half + highf * theirs)
            vn = spread_edges(highf * half + lowf * theirs)
            gain = 0.5 * (1.0 - decay * decay) / decay
            initial = -0.5 * (v0 + vn / decay)
            zonal_l = step(lonf) * initial - gain * left + 0.5 * edge_ref[:, 0:128]
            zonal_r = (gain * right - 0.5 * edge_ref[:, 128:256]
                       + end * (gain * v0 - decay * (step(8.0) * initial - gain * whole)))
            carry_l = sign * jnp.where(zonal, zonal_l, carry_l)
            carry_r = sign * jnp.where(zonal, zonal_r, carry_r)
            start = jnp.where(top & (row == 0.0), 0.5 * jnp.exp(-rate * ROWS), 0.0)
            weight_l = jnp.where(zonal, weight_l, -gain * weight_l - start)
            weight_r = jnp.where(zonal, weight_r, gain * weight_r)
        carry_ref[:, tile * 256:tile * 256 + 128] = carry_l
        carry_ref[:, tile * 256 + 128:tile * 256 + 256] = carry_r
        fold = lambda w, c: jnp.sum(w * c, axis=0, keepdims=True)
        weights.append(((fold(weight_l, carry_l), fold(weight_l, carry_r)),
                        (fold(weight_r, carry_l), fold(weight_r, carry_r))))
    shape = (HALF_ROWS, LANES)
    lane, lane_scale, _, wind_field, rest_field = lane_fields(shape)
    out_row = iota(shape, 0)
    scale = jnp.where(out_row < HALF, 0, jnp.where(out_row < 2 * HALF, 1, 2))
    core = lat & 1
    column = fiota((HALF_ROWS, COLS), 1)
    for ref, half in ((send_ref, 1 - core), (keep_ref, core)):
        field = out_row - scale * HALF + half * HALF
        same = lane_scale == scale
        wind = same & (wind_field == field)
        rest = same & (rest_field == field)
        rate = table_ref[pl.ds(pl.multiple_of(half * HALF, 8), HALF), :]
        rate = jnp.concatenate([rate[:, s:s + 1] for s in range(SCALES)], axis=0)
        fall = jnp.exp(-rate * (column + 1.0))
        rise = jnp.exp(-rate * (COLS - column))
        for side in range(2):
            pick = lambda k: jnp.sum(
                jnp.where(wind, weights[0][side][k], 0.0) + jnp.where(rest, weights[1][side][k], 0.0),
                axis=1, keepdims=True)
            rows = slice(side * HALF_ROWS, (side + 1) * HALF_ROWS)
            ref[rows, :] = local_ref[half, rows, :] + pick(0) * fall + pick(1) * rise


def column_sums(where, table, lanes, part, theirs, edge, local):
    half = jax.ShapeDtypeStruct((2 * HALF_ROWS, COLS), F32)
    return pl.pallas_call(
        column_sums_kernel,
        in_specs=[SMEM] + [VMEM] * 6,
        out_specs=[VMEM] * 3,
        out_shape=[jax.ShapeDtypeStruct((ROWS, 512), F32), half, half],
        compiler_params=params(),
        name="column_sums",
    )(where, table, lanes, part, theirs, edge, local)


LEFT = slice(0, HALF_ROWS)
RIGHT = slice(HALF_ROWS, 2 * HALF_ROWS)
STEPS = 21


def steps_kernel(where_ref, table_ref, _, out_ref):
    lat = where_ref[0]
    odd = (lat & 1) == 1
    odd_chip = ((lat >> 1) & 1) == 1
    z = lat >> 2
    zf = z.astype(F32)
    rate = table_ref[pl.ds(pl.multiple_of((lat & 1) * HALF, 8), HALF), :]
    rate = jnp.concatenate([rate[:, s:s + 1] for s in range(SCALES)], axis=0)
    rate = jnp.broadcast_to(rate, (HALF_ROWS, LANES))
    power = lambda n: jnp.exp(-rate * n)
    quad = lambda n: power(4.0 * ROWS * n)
    one, zero = jnp.ones_like(rate), jnp.zeros_like(rate)
    device, chip = power(1.0 * ROWS), power(2.0 * ROWS)
    out = [jnp.where(odd, one, device), jnp.where(odd, device, one)]
    out += [jnp.where(odd_chip, one, chip), jnp.where(odd_chip, chip, one)]
    out += [power(1.0 + 4 * ROWS * jnp.maximum(7.0 - 2.0 * zf, 1.0))]
    for d in (1, 2, 3):
        other = z ^ d
        of = other.astype(F32)
        below = other < z
        gap = quad(jnp.abs(zf - of) - 1.0)
        out += [jnp.where(below, gap, zero), jnp.where(below, zero, gap), jnp.where(below, quad(3.0 - of), zero)]
    out += [quad(3.0 - zf), quad(3.0 - zf) * power(1.0)]
    out += [jnp.where(odd_chip, chip, one), jnp.where(odd_chip, one, zero)]
    out += [jnp.where(odd_chip, one, chip), jnp.where(odd_chip, zero, one)]
    out += [device]
    for k, value in enumerate(out):
        out_ref[k] = value


def lat_steps(where, table, before):
    return pl.pallas_call(
        steps_kernel,
        in_specs=[SMEM, VMEM, ANY],
        out_specs=VMEM,
        out_shape=jax.ShapeDtypeStruct((STEPS, HALF_ROWS, LANES), F32),
        compiler_params=params(),
        name="lat_steps",
    )(where, table, before)


def by_tile(body):
    for b in range(PARTS):
        body(slice(b * LANES, (b + 1) * LANES))


def chip_merge_kernel(steps_ref, keep_ref, got_ref, chip_ref):
    def body(lanes):
        mine, other = steps_ref[0], steps_ref[1]
        chip_ref[LEFT, lanes] = mine * keep_ref[LEFT, lanes] + other * got_ref[LEFT, lanes]
        chip_ref[RIGHT, lanes] = other * keep_ref[RIGHT, lanes] + mine * got_ref[RIGHT, lanes]

    by_tile(body)


def chip_merge(steps, keep, got):
    return pl.pallas_call(
        chip_merge_kernel,
        in_specs=[VMEM] * 3,
        out_specs=VMEM,
        out_shape=jax.ShapeDtypeStruct((2 * HALF_ROWS, COLS), F32),
        compiler_params=params(),
        name="chip_merge",
    )(steps, keep, got)


def quad_merge_kernel(where_ref, steps_ref, chip_ref, pair_ref, _, left_ref, s1_ref, s2_ref, s3_ref):
    z = where_ref[0] >> 2

    def body(lanes):
        mine, other, image = steps_ref[2], steps_ref[3], steps_ref[4]
        left = mine * chip_ref[LEFT, lanes] + other * pair_ref[LEFT, lanes]
        right = other * chip_ref[RIGHT, lanes] + mine * pair_ref[RIGHT, lanes]
        back = right - image * left
        left_ref[:, lanes] = left
        for d, ref in ((1, s1_ref), (2, s2_ref), (3, s3_ref)):
            ref[:, lanes] = jnp.where((z ^ d) > z, left, back)

    by_tile(body)


def quad_merge(where, steps, chip, pair, after):
    one = jax.ShapeDtypeStruct((HALF_ROWS, COLS), F32)
    return pl.pallas_call(
        quad_merge_kernel,
        in_specs=[SMEM] + [VMEM] * 3 + [ANY],
        out_specs=[VMEM] * 4,
        out_shape=[one] * 4,
        compiler_params=params(),
        name="quad_merge",
    )(where, steps, chip, pair, after)


def lat_carry_kernel(where_ref, steps_ref, keep_ref, got_ref, pair_ref, left_ref, g1_ref, g2_ref, g3_ref, _,
                     own_ref, send_ref):
    odd = (where_ref[0] & 1) == 1

    def body(lanes):
        left, right, whole = 0.0, 0.0, steps_ref[14] * left_ref[:, lanes]
        for k, ref in ((5, g1_ref), (8, g2_ref), (11, g3_ref)):
            g = ref[:, lanes]
            left = left + steps_ref[k] * g
            right = right + steps_ref[k + 1] * g
            whole = whole + steps_ref[k + 2] * g
        right = right - steps_ref[15] * whole
        left = steps_ref[16] * left + steps_ref[17] * pair_ref[LEFT, lanes]
        right = steps_ref[18] * right + steps_ref[19] * pair_ref[RIGHT, lanes]
        low_left = jnp.where(odd, got_ref[LEFT, lanes], keep_ref[LEFT, lanes])
        high_right = jnp.where(odd, keep_ref[RIGHT, lanes], got_ref[RIGHT, lanes])
        high_l = low_left + steps_ref[20] * left
        low_r = high_right + steps_ref[20] * right
        own_ref[LEFT, lanes] = jnp.where(odd, high_l, left)
        own_ref[RIGHT, lanes] = jnp.where(odd, right, low_r)
        send_ref[LEFT, lanes] = jnp.where(odd, left, high_l)
        send_ref[RIGHT, lanes] = jnp.where(odd, low_r, right)

    by_tile(body)


def lat_carry(where, steps, keep, got, pair, left, gs, after):
    half = jax.ShapeDtypeStruct((2 * HALF_ROWS, COLS), F32)
    return pl.pallas_call(
        lat_carry_kernel,
        in_specs=[SMEM] + [VMEM] * 8 + [ANY],
        out_specs=[VMEM] * 2,
        out_shape=[half, half],
        compiler_params=params(),
        name="lat_carry",
    )(where, steps, keep, got, pair, left, *gs, after)


def local_filter_kernel(starts, use_x, use_carry, where_ref, table_ref, carry_ref, x_ref, base_ref, out_ref):
    top = where_ref[0] == 0
    shape = (ROWS, LANES)
    row = fiota(shape, 0)
    lane = iota(shape, 1)
    source = jnp.where(lane >= ROWS, lane - ROWS, lane).astype(F32)
    used = lane < 2 * ROWS
    gap = jnp.abs(row - source)
    gap_low = jnp.abs(source - 1.0 - row)
    gap_high = jnp.abs(source + 1.0 - row)
    first = source == 0.0
    spread = jnp.abs(fiota((LANES, LANES), 0) - fiota((LANES, LANES), 1))
    tag = lane & 31
    corner = jnp.zeros((LANES, LANES), BF16)
    left_lane = (lane == LANES - 1) | (lane == 1) | (lane == 3)
    flat = lane[:1]
    row_scale = jnp.where((flat == LANES - 1) | (flat == 0), 0, jnp.where(flat <= 2, 1, 2))
    base = iota((8, LANES), 0)
    column = fiota((8, LANES), 1)

    def carry_tile(tile, virtual):
        left = carry_ref[:, tile * 256:tile * 256 + 128]
        right = carry_ref[:, tile * 256 + 128:tile * 256 + 256]
        left = pltpu.roll(left, (LANES - virtual) % LANES, 1)
        right = pltpu.roll(right, (LANES + 1 - virtual) % LANES, 1)
        return jnp.where(tag == 0, left, jnp.where(tag == 1, right, 0.0))

    def column_pass(matrices, x, carry):
        parts = [split(jnp.where(used, m, 0.0)) for m in matrices]
        lhs = jnp.concatenate([jnp.concatenate([mh, ml[:, :ROWS]], axis=1) for mh, ml in parts], axis=0)
        wide = [t for t in (x, carry) if t is not None]
        wide = wide[0] if len(wide) == 1 else jnp.concatenate(wide, axis=1)
        xh, xl = split(wide)
        rhs = jnp.concatenate([xh, xl, jnp.zeros((32, wide.shape[1]), BF16), xh], axis=0)
        return mm(lhs, rhs)

    def column_stage(f, wind):
        facts = table_ref[pl.ds(f, 1), :]
        rates = [facts[:, s:s + 1] for s in range(SCALES)]
        gains = [facts[:, SCALES + s:SCALES + s + 1] for s in range(SCALES)]
        plain = [gains[s] * jnp.exp(-rates[s] * gap) for s in range(SCALES)]
        if wind:
            slopes = []
            for s in range(SCALES):
                slope = jnp.exp(-rates[s] * gap_low) - jnp.exp(-rates[s] * gap_high)
                slope = slope - jnp.where(top & first, jnp.exp(-rates[s] * (row + 1.0)), 0.0)
                slopes.append((0.5 * gains[s]) * slope)
            stream = f < GROUP
            second_sign = 1.0 if stream else -1.0
            meridional = f if stream else f + 16
            zonal = f + 8
            pair = f + 8 if stream else f - 8
            w = column_pass(plain, -zonal_difference(x_ref[pair]), carry_tile(0, zonal))
            w = w + column_pass(slopes, second_sign * x_ref[f], carry_tile(0, meridional))
        else:
            w = column_pass(plain, x_ref[f] if use_x else None, carry_tile(1, f - WINDS) if use_carry else None)
        return rates, w

    def row_stage(rates, w):
        outs = []
        for s in range(SCALES):
            rows = slice(s * ROWS, (s + 1) * ROWS)
            stack = jnp.concatenate([w[rows, b * LANES:(b + 1) * LANES] for b in range(PARTS)], axis=0)
            wh, wl = split(stack)
            th, tl = split(jnp.exp(-rates[s] * spread))
            lhs = jnp.concatenate([wh, wl], axis=1)
            rhs = jnp.concatenate([jnp.concatenate([th, tl], axis=1), jnp.concatenate([th, corner], axis=1)], axis=0)
            out = mm(lhs, rhs)
            outs.append(out[:, :LANES] + out[:, LANES:])
        return outs

    def carry_stage(rates, w, outs):
        sums, outer = None, jnp.zeros((ROWS, LANES), F32)
        for s in range(SCALES):
            here = row_scale == s
            if use_carry:
                moved = pltpu.roll(w[s * ROWS:(s + 1) * ROWS, w.shape[1] - LANES:], LANES - 30 * s - 1, 1)
                outer = moved if s == 0 else jnp.where(here, moved, outer)
            if use_x:
                turned = outs[s] if s == 0 else pltpu.roll(outs[s], 2 * s, 1)
                sums = turned if s == 0 else jnp.where(here, turned, sums)
        rate_row = jnp.where(row_scale == 0, rates[0], jnp.where(row_scale == 1, rates[1], rates[2]))
        jump = jnp.exp(-rate_row * LANES)
        from_left, from_right = [outer], [outer]
        for b in range(PARTS - 1):
            ahead, behind = jump * from_left[-1], jump * from_right[-1]
            if use_x:
                ahead = ahead + sums[b * ROWS:(b + 1) * ROWS]
                behind = behind + sums[(PARTS - 1 - b) * ROWS:(PARTS - b) * ROWS]
            from_left.append(ahead)
            from_right.append(behind)
        carries = [jnp.where(left_lane, from_left[b], from_right[PARTS - 1 - b]) for b in range(PARTS)]
        ch, cl = split(jnp.concatenate(carries, axis=0))
        low_rate = jnp.where(base == 0, rates[0], jnp.where(base <= 2, rates[1], rates[2]))
        low_left = (base == 1) | (base == 3)
        low = jnp.where(base <= 4, jnp.exp(-low_rate * jnp.where(low_left, column + 1.0, LANES - column)), 0.0)
        high = jnp.where(base == 7, jnp.exp(-rates[0] * (column + 1.0)), 0.0)
        pad = jnp.zeros((8, LANES), F32)
        lh, ll = split(jnp.concatenate([low, pad], axis=0))
        hh, hl = split(jnp.concatenate([pad, high], axis=0))
        gap_rows = jnp.zeros((96, LANES), BF16)
        bh = jnp.concatenate([lh, gap_rows, hh], axis=0)
        bl = jnp.concatenate([ll, gap_rows, hl], axis=0)
        rhs = jnp.concatenate([jnp.concatenate([bh, bl], axis=1), jnp.concatenate([bh, corner], axis=1)], axis=0)
        return jnp.concatenate([ch, cl], axis=1), rhs

    for start in starts:
        wind = start < WINDS
        fields = [start + i for i in range(GROUP)]
        columns = [column_stage(f, wind) for f in fields]
        outs = [row_stage(*c) if use_x else None for c in columns]
        ranks = [carry_stage(*c, o) for c, o in zip(columns, outs)]
        for f, o, (lhs, rhs) in zip(fields, outs, ranks):
            out = mm(lhs, rhs)
            total = out[:, :LANES] + out[:, LANES:]
            if use_x:
                total = (o[0] + o[1]) + (o[2] + total)
            for b in range(PARTS):
                lanes = slice(b * LANES, (b + 1) * LANES)
                part = total[b * ROWS:(b + 1) * ROWS]
                if base_ref is not None:
                    part = part + base_ref[f - starts[0], :, lanes]
                out_ref[f - starts[0], :, lanes] = part


def local_filter(where, table, carry, x, first, count, before, base=None):
    starts = tuple(range(first, first + count, GROUP))
    use_x, use_carry = base is None, carry is not None
    names = ["where", "table"] + ["carry"] * use_carry + ["x"] * use_x + ["base"] * (base is not None) + ["before"]
    arrays = {"where": where, "table": table, "carry": carry, "x": x, "base": base, "before": before}
    specs = {"where": SMEM, "before": ANY}

    def body(*refs):
        by_name = dict(zip(names, refs))
        local_filter_kernel(starts, use_x, use_carry, by_name["where"], by_name["table"], by_name.get("carry"),
                            by_name.get("x"), by_name.get("base"), refs[len(names)])

    return pl.pallas_call(
        body,
        in_specs=[specs.get(n, VMEM) for n in names],
        out_specs=VMEM,
        out_shape=jax.ShapeDtypeStruct((count, ROWS, COLS), F32),
        compiler_params=params(),
        cost_estimate=pl.CostEstimate(flops=int(count * 30000000), bytes_accessed=count * 150_000, transcendentals=0),
        name="local_filter",
    )(*[arrays[n] for n in names])


def add_carries(half, table_ref, carry_ref, z_refs, part, store):
    row = fiota((8, LANES), 0)
    up_steps, down_steps = row + 1.0, 8.0 - row
    tables = [carry_ref[side, s, part] for side in range(2) for s in range(SCALES)]
    start = pl.multiple_of((half * 3 + part) * GROUP, GROUP)
    group_facts = table_ref[pl.ds(start, GROUP), :]
    for i in range(GROUP):
        facts = group_facts[i:i + 1, :]
        ups = []
        for s in range(SCALES):
            r = jnp.broadcast_to(facts[:, s:s + 1], (8, LANES))
            w = jnp.broadcast_to(facts[:, SCALES + s:SCALES + s + 1], (8, LANES))
            jump = jnp.exp(-8.0 * r)
            up, down = [w * jnp.exp(-r * up_steps)], [w * jnp.exp(-r * down_steps)]
            for _ in range(ROWS // 8 - 1):
                up.append(up[-1] * jump)
                down.insert(0, down[0] * jump)
            ups.append((jnp.concatenate(up, axis=0), jnp.concatenate(down, axis=0)))
        for b in range(PARTS):
            lanes = slice(b * LANES, (b + 1) * LANES)
            total = jnp.where(half == 0, z_refs[part // 2][part % 2 * GROUP + i, :, lanes],
                              z_refs[(3 + part) // 2][(3 + part) % 2 * GROUP + i, :, lanes])
            for s in range(SCALES):
                total = total + ups[s][0] * tables[s][i:i + 1, lanes] + ups[s][1] * tables[SCALES + s][i:i + 1, lanes]
            store(i, lanes, total)


def finish_own_kernel(where_ref, table_ref, carry_ref, z0_ref, z1_ref, z2_ref, out_ref):
    for part in range(3):
        def store(i, lanes, value):
            out_ref[part * GROUP + i, :, lanes] = value

        add_carries(where_ref[0] & 1, table_ref, carry_ref, (z0_ref, z1_ref, z2_ref), part, store)


def finish_own(where, table, carry, parts):
    return pl.pallas_call(
        finish_own_kernel,
        in_specs=[SMEM] + [VMEM] * 5,
        out_specs=VMEM,
        out_shape=jax.ShapeDtypeStruct((HALF, ROWS, COLS), F32),
        compiler_params=params(),
        cost_estimate=pl.CostEstimate(flops=1_000_000_000, bytes_accessed=2_000_000, transcendentals=0),
        name="finish_own",
    )(where, table, carry.reshape(2, SCALES, 3, GROUP, COLS), *parts)


def finish_kernel(where_ref, table_ref, carry_ref, z0_ref, z1_ref, z2_ref, own_ref, out_ref, buf_ref, sem):
    half = 1 - (where_ref[0] & 1)
    ready = pltpu.make_async_copy(own_ref, out_ref.at[pl.ds((1 - half) * HALF, HALF)], sem.at[3])
    ready.start()
    copies = [ready]
    for part in range(3):
        def store(i, lanes, value):
            buf_ref[part, i, :, lanes] = value

        add_carries(half, table_ref, carry_ref, (z0_ref, z1_ref, z2_ref), part, store)
        there = out_ref.at[pl.ds((half * 3 + part) * GROUP, GROUP)]
        copies.append(pltpu.make_async_copy(buf_ref.at[part], there, sem.at[part]))
        copies[-1].start()
    for copy in copies:
        copy.wait()


def finish(where, table, carry, parts, own):
    return pl.pallas_call(
        finish_kernel,
        in_specs=[SMEM] + [VMEM] * 6,
        out_specs=HBM,
        out_shape=jax.ShapeDtypeStruct((FIELDS, ROWS, COLS), F32),
        scratch_shapes=[pltpu.VMEM((3, GROUP, ROWS, COLS), F32), pltpu.SemaphoreType.DMA((4,))],
        compiler_params=params(),
        name="finish",
    )(where, table, carry.reshape(2, SCALES, 3, GROUP, COLS), *parts, own)


def partner(axis, count, bit):
    return functools.partial(lax.ppermute, axis_name=axis, perm=[(i, i ^ bit) for i in range(count)])


def shards(x, lengths, weights):
    where = jnp.stack([lax.axis_index("lat"), lax.axis_index("lon")]).astype(jnp.int32)
    facts = jnp.concatenate([lengths.T, weights.T], axis=0)
    sums, edge, table, lanes, held = row_sums(where, facts, x)
    got = [partner("lon", NLON, d)(sums) for d in (1, 2, 3)]
    early = local_filter(where, table, None, held, 32, 16, sums)
    part, half = lon_merge(where, lanes, sums, got, early)
    theirs = partner("lon", NLON, 4)(half)
    local = local_sums(where, table, held, part)
    steps = lat_steps(where, table, part)
    carry, keep, send = column_sums(where, table, lanes, part, theirs, edge, local)
    got_core = partner("lat", NLAT, 1)(send)
    chip = chip_merge(steps, keep, got_core)
    pair = partner("lat", NLAT, 2)(chip)
    z0 = local_filter(where, table, carry, held, 0, 16, chip)
    left, *sends = quad_merge(where, steps, chip, pair, z0)
    gs = [partner("lat", NLAT, 4 * d)(t) for d, t in zip((1, 2, 3), sends)]
    z1 = local_filter(where, table, carry, held, 16, 16, left)
    z2 = local_filter(where, table, carry, held, 32, 16, z1, early)
    own, other = lat_carry(where, steps, keep, got_core, pair, left, gs, z2)
    got_carry = partner("lat", NLAT, 1)(other)
    done = finish_own(where, table, own, (z0, z1, z2))
    return finish(where, table, got_carry, (z0, z1, z2), done)


def solution(mesh):
    in_specs = (P(None, "lat", "lon"), P(), P())
    out_specs = P(None, "lat", "lon")
    return jax.shard_map(shards, mesh=mesh, in_specs=in_specs, out_specs=out_specs, check_vma=False)
```

```python
import functools

import jax
import jax.numpy as jnp
from jax import lax
from jax.experimental import pallas as pl
from jax.experimental.pallas import tpu as pltpu
from jax.sharding import PartitionSpec as P

LEVELS = 8
SCALES = 3
WINDS = 16
FIELDS = 48
ROWS = 48
COLS = 384
GROUP = 8
GROUPS = FIELDS // GROUP
NLAT = 16
NLON = 8
LANES = 128
PARTS = COLS // LANES
HALF = FIELDS // 2
HALF_ROWS = SCALES * HALF
F32 = jnp.float32
BF16 = jnp.bfloat16

VMEM = pl.BlockSpec(memory_space=pltpu.VMEM)
BIG = 48 * 1024 * 1024
WHOLE = 50 * 1024 * 1024


def lat_index():
    return lax.axis_index("lat")


def lon_index():
    return lax.axis_index("lon")


def params(**kw):
    return pltpu.CompilerParams(vmem_limit_bytes=BIG, **kw)


def iota(shape, dim):
    return lax.broadcasted_iota(jnp.int32, shape, dim)


def fiota(shape, dim):
    return iota(shape, dim).astype(F32)


def split(value):
    high = value.astype(BF16)
    return high, (value - high.astype(F32)).astype(BF16)


def mm(a, b):
    return jnp.dot(a, b, preferred_element_type=F32)


def lane_fields(shape):
    lane = iota(shape, 1)
    virtual = lane & 31
    wind_field = ((virtual >> 4) << 3) + (virtual & 7)
    return lane, lane >> 5, virtual, wind_field, virtual + WINDS


def exact(a, b, dims):
    return lax.dot_general(a, b, (dims, ((), ())), precision=lax.Precision.HIGHEST, preferred_element_type=F32)


def lane_rates(rate):
    shape = (FIELDS, LANES)
    _, _, _, wind_field, rest_field = lane_fields(shape)
    field = iota(shape, 0)
    lane = iota((1, LANES), 1)

    def pick(which):
        every = exact(rate, jnp.where(field == which, 1.0, 0.0).astype(F32), ((1,), (0,)))
        value = jnp.where(lane < 32, every[0:1], jnp.where(lane < 64, every[1:2], every[2:3]))
        return jnp.where(lane < 96, value, 0.0)

    return pick(wind_field), pick(rest_field)


def scale_weights(rate, weights):
    decay = jnp.exp(-rate)
    leak = 1.0 - decay
    cube = (1.0 + decay) * (1.0 + decay) * (1.0 + decay)
    coefficient = weights * cube / (leak * (1.0 + decay * decay))
    kappa = leak / (1.0 + decay)
    return coefficient * kappa * kappa


def lane_kinds(shape):
    _, _, virtual, _, _ = lane_fields(shape)
    second = virtual >= 16
    north = (virtual & 15) >= 8
    zonal = second != north
    sign = jnp.where(second | north, -1.0, 1.0).astype(F32)
    return zonal, sign


def row_sums_kernel(len_ref, x_ref, sums_ref, edge_ref, table_ref, lanes_ref, held_ref, w_ref, sem):
    lon = lon_index()
    copies = []
    for k, (start, stop) in enumerate(((0, WINDS), (WINDS, FIELDS))):
        here = pl.ds(start, stop - start)
        copies.append(pltpu.make_async_copy(x_ref.at[here], held_ref.at[here], sem.at[k]))
        copies[-1].start()
    rate = 1.0 / len_ref[0:SCALES, :]
    pair = lane_rates(rate)
    lanes_ref[...] = jnp.concatenate([pair[0], pair[1], jnp.ones((6, LANES), F32)], axis=0)
    column = fiota((COLS, LANES), 0)
    for tile, rates in enumerate(pair):
        for side, steps in enumerate((COLS - 1 - column, column)):
            high, low = split(jnp.exp(-rates * steps))
            lanes = slice(side * LANES, (side + 1) * LANES)
            w_ref[tile, 0:COLS, lanes] = high
            w_ref[tile, COLS:2 * COLS, lanes] = high
            w_ref[tile, 2 * COLS:, lanes] = low
    both = jnp.concatenate([rate, scale_weights(rate, len_ref[SCALES:, :]), jnp.ones((2, FIELDS), F32)], axis=0)
    eye = jnp.where(iota((8, LANES), 0) == iota((8, LANES), 1), 1.0, 0.0).astype(F32)
    table_ref[...] = exact(both, eye, ((0,), (0,)))
    lane = iota((ROWS, LANES), 1)
    virtual = lane & 31
    zero = jnp.zeros((ROWS, LANES), F32)
    left, right, first, last = zero, zero, zero, zero
    for g in range(GROUPS):
        if g in (0, 2):
            copies[g // 2].wait()
        x = held_ref[g * GROUP:(g + 1) * GROUP].reshape(GROUP * ROWS, COLS)
        xh, xl = split(x)
        res = mm(jnp.concatenate([xh, xl, xh], axis=1), w_ref[0 if g < 2 else 1])
        if g == 2:
            left, right = zero, zero
        for i in range(GROUP):
            rows = slice(i * ROWS, (i + 1) * ROWS)
            mine = (virtual & 15) == g * GROUP + i if g < 2 else virtual == (g - 2) * GROUP + i
            left = jnp.where(mine, res[rows, 0:128], left)
            right = jnp.where(mine, res[rows, 128:256], right)
            if g < 2:
                first = jnp.where(mine, x[rows, 0:1], first)
                last = jnp.where(mine, x[rows, COLS - 1:COLS], last)
        if g == 1:
            edge = jnp.where(lon == 0, first, jnp.where(lon == NLON - 1, last, 0.0))
            sums_ref[:, 0:128] = jnp.where(lane >= 96, edge, left)
            sums_ref[:, 128:256] = right
            edge_ref[:, 0:128] = first
            edge_ref[:, 128:256] = last
    sums_ref[:, 256:384] = left
    sums_ref[:, 384:512] = right


HBM = pl.BlockSpec(memory_space=pltpu.HBM)
ANY = pl.BlockSpec(memory_space=pl.ANY)


def row_sums(facts, x):
    return pl.pallas_call(
        row_sums_kernel,
        in_specs=[VMEM, HBM],
        out_specs=[VMEM] * 5,
        out_shape=[jax.ShapeDtypeStruct((ROWS, 512), F32), jax.ShapeDtypeStruct((ROWS, 256), F32),
                   jax.ShapeDtypeStruct((FIELDS, LANES), F32), jax.ShapeDtypeStruct((8, LANES), F32),
                   jax.ShapeDtypeStruct((FIELDS, ROWS, COLS), F32)],
        scratch_shapes=[pltpu.VMEM((2, 3 * COLS, 256), BF16), pltpu.SemaphoreType.DMA((2,))],
        compiler_params=pltpu.CompilerParams(vmem_limit_bytes=WHOLE),
        name="row_sums",
    )(facts, x)


def zonal_difference(x):
    shape = x.shape
    axis = len(shape) - 1
    column = iota(shape, axis)
    ahead = jnp.where(column == COLS - 1, 0.0, pltpu.roll(x, COLS - 1, axis))
    behind = jnp.where(column == 0, 0.0, pltpu.roll(x, 1, axis))
    return 0.5 * (ahead - behind)


def local_sums_kernel(table_ref, x_ref, _, out_ref):
    top = lat_index() == 0
    count = 2 * SCALES * GROUP
    shape = (count, LANES)
    out_row = iota(shape, 0)
    member = out_row & 7
    left_side = out_row < SCALES * GROUP
    lane = iota(shape, 1)
    source = jnp.where(lane >= ROWS, lane - ROWS, lane).astype(F32)
    used = lane < 2 * ROWS
    steps = jnp.where(left_side, ROWS - 1 - source, source)
    zeros = jnp.zeros((32, COLS), BF16)

    def weighted(matrix, x, i):
        mh, ml = split(jnp.where(used & (member == i), matrix, 0.0))
        xh, xl = split(x)
        return mm(jnp.concatenate([mh, ml[:, :ROWS]], axis=1), jnp.concatenate([xh, xl, zeros, xh], axis=0))

    def group_sums(group, wind):
        rate = table_ref[group * GROUP:(group + 1) * GROUP, :]
        row_rate = jnp.concatenate([rate[:, s:s + 1] for _ in range(2) for s in range(SCALES)], axis=0)
        wide = jnp.broadcast_to(row_rate, shape)
        plain = jnp.exp(-wide * steps)
        acc = jnp.zeros((count, COLS), F32)
        if wind:
            decay = jnp.exp(-wide)
            gain = 0.5 * (1.0 - decay * decay) / decay
            start = jnp.where(top & (source == 0.0), 0.5 * jnp.exp(-wide * ROWS), 0.0)
            slope = jnp.where(left_side, -gain * plain - start, gain * plain)
            second_sign = jnp.where(group == 0, 1.0, -1.0)
            for i in range(GROUP):
                acc += weighted(plain, -zonal_difference(x_ref[(1 - group) * GROUP + i]), i)
                acc += weighted(slope, second_sign * x_ref[group * GROUP + i], i)
        else:
            for i in range(GROUP):
                acc += weighted(plain, x_ref[group * GROUP + i], i)
        return acc, row_rate

    made = [group_sums(group, group < 2) for group in range(GROUPS)]
    acc = jnp.concatenate([m[0] for m in made], axis=0)
    factor = jnp.concatenate([jnp.broadcast_to(jnp.exp(-m[1]), (count, LANES)) for m in made], axis=0)
    factor = jnp.concatenate([factor] * PARTS, axis=1)
    column = iota(acc.shape, 1)
    forward, backward = acc, acc
    step = 1
    while step < COLS:
        forward = forward + factor * jnp.where(column >= step, pltpu.roll(forward, step, 1), 0.0)
        backward = backward + factor * jnp.where(column < COLS - step, pltpu.roll(backward, COLS - step, 1), 0.0)
        factor = factor * factor
        step *= 2
    acc = forward + backward - acc
    for group in range(GROUPS):
        for side in range(2):
            for s in range(SCALES):
                k = group * count + (side * SCALES + s) * GROUP
                out_ref[group // 3, side, s, group % 3] = acc[k:k + GROUP]


def local_sums(table, x, before):
    out = pl.pallas_call(
        local_sums_kernel,
        in_specs=[VMEM, VMEM, ANY],
        out_specs=VMEM,
        out_shape=jax.ShapeDtypeStruct((2, 2, SCALES, 3, GROUP, COLS), F32),
        compiler_params=params(),
        cost_estimate=pl.CostEstimate(flops=600000000, bytes_accessed=4_000_000, transcendentals=0),
        name="local_sums",
    )(table, x, before)
    return out.reshape(2, 2 * HALF_ROWS, COLS)


def lon_merge_kernel(lanes_ref, own_ref, g1_ref, g2_ref, g3_ref, _, part_ref, send_ref):
    y = lon_index() & 3
    high = lon_index() >= 4
    yf = y.astype(F32)
    zonal, _ = lane_kinds((1, LANES))
    lane = iota((1, LANES), 1)
    for tile in range(2):
        rate = lanes_ref[tile:tile + 1, :]
        step = lambda n: jnp.exp(-rate * (COLS * n))
        base = tile * 256
        lanes_l = slice(base, base + 128)
        lanes_r = slice(base + 128, base + 256)
        left_total = step(3.0 - yf) * own_ref[:, lanes_l]
        right_total = step(yf) * own_ref[:, lanes_r]
        left = jnp.zeros((ROWS, LANES), F32)
        right = jnp.zeros((ROWS, LANES), F32)
        for d, ref in ((1, g1_ref), (2, g2_ref), (3, g3_ref)):
            other = y ^ d
            of = other.astype(F32)
            below = other < y
            lg, rg = ref[:, lanes_l], ref[:, lanes_r]
            gap = jnp.abs(yf - of) - 1.0
            left = left + jnp.where(below, step(gap), 0.0) * lg
            right = right + jnp.where(below, 0.0, step(gap)) * rg
            left_total = left_total + step(3.0 - of) * lg
            right_total = right_total + step(of) * rg
        part_ref[:, lanes_l] = left
        part_ref[:, lanes_r] = right
        part_ref[:, 512 + tile * 128:640 + tile * 128] = left_total
        image = jnp.exp(-rate * (4.0 * COLS + 1.0))
        if tile == 0:
            image = jnp.where(zonal, -image, image)
            image = jnp.where(lane >= 96, -1.0, image)
            right_total = jnp.where(lane >= 96, 0.0, right_total)
        send_ref[:, tile * 128:tile * 128 + 128] = jnp.where(high, right_total - image * left_total, left_total)


def lon_merge(lanes, own, got, after):
    return pl.pallas_call(
        lon_merge_kernel,
        in_specs=[VMEM] * 5 + [ANY],
        out_specs=[VMEM, VMEM],
        out_shape=[jax.ShapeDtypeStruct((ROWS, 768), F32), jax.ShapeDtypeStruct((ROWS, 256), F32)],
        compiler_params=params(),
        name="lon_merge",
    )(lanes, own, *got, after)


def spread_edges(tile):
    lane = iota(tile.shape, 1)
    out = tile
    for k in range(6):
        out = jnp.where((lane >> 4) == k, pltpu.roll(tile, (k * 16 + 32) % LANES, 1), out)
    return out


def column_sums_kernel(table_ref, lanes_ref, part_ref, theirs_ref, edge_ref, local_ref,
                       carry_ref, keep_ref, send_ref):
    lat, lon = lat_index(), lon_index()
    y = lon & 3
    yf = y.astype(F32)
    high = lon >= 4
    highf = jnp.where(high, 1.0, 0.0)
    lowf = 1.0 - highf
    lonf = lon.astype(F32)
    top = lat == 0
    rates = (lanes_ref[0:1, :], lanes_ref[1:2, :])
    zonal, sign = lane_kinds((1, LANES))
    row = fiota((ROWS, LANES), 0)
    weights = []
    for tile in range(2):
        rate = rates[tile]
        step = lambda n: jnp.exp(-rate * (COLS * n))
        decay = jnp.exp(-rate)
        theirs = theirs_ref[:, tile * 128:tile * 128 + 128]
        half = part_ref[:, 512 + tile * 128:640 + tile * 128]
        left = part_ref[:, tile * 256:tile * 256 + 128] + (highf * step(yf)) * theirs
        right = part_ref[:, tile * 256 + 128:tile * 256 + 256] + (lowf * step(3.0 - yf)) * theirs
        whole = (highf + lowf * step(4.0)) * half + (highf * step(4.0)) * theirs
        end = step(7.0 - lonf)
        weight_l = jnp.exp(-rate * (ROWS - 1 - row))
        weight_r = jnp.exp(-rate * row)
        carry_l = left
        carry_r = right - (end * decay) * whole
        if tile == 0:
            v0 = spread_edges(lowf * half + highf * theirs)
            vn = spread_edges(highf * half + lowf * theirs)
            gain = 0.5 * (1.0 - decay * decay) / decay
            initial = -0.5 * (v0 + vn / decay)
            zonal_l = step(lonf) * initial - gain * left + 0.5 * edge_ref[:, 0:128]
            zonal_r = (gain * right - 0.5 * edge_ref[:, 128:256]
                       + end * (gain * v0 - decay * (step(8.0) * initial - gain * whole)))
            carry_l = sign * jnp.where(zonal, zonal_l, carry_l)
            carry_r = sign * jnp.where(zonal, zonal_r, carry_r)
            start = jnp.where(top & (row == 0.0), 0.5 * jnp.exp(-rate * ROWS), 0.0)
            weight_l = jnp.where(zonal, weight_l, -gain * weight_l - start)
            weight_r = jnp.where(zonal, weight_r, gain * weight_r)
        carry_ref[:, tile * 256:tile * 256 + 128] = carry_l
        carry_ref[:, tile * 256 + 128:tile * 256 + 256] = carry_r
        fold = lambda w, c: jnp.sum(w * c, axis=0, keepdims=True)
        weights.append(((fold(weight_l, carry_l), fold(weight_l, carry_r)),
                        (fold(weight_r, carry_l), fold(weight_r, carry_r))))
    shape = (HALF_ROWS, LANES)
    lane, lane_scale, _, wind_field, rest_field = lane_fields(shape)
    out_row = iota(shape, 0)
    scale = jnp.where(out_row < HALF, 0, jnp.where(out_row < 2 * HALF, 1, 2))
    core = lat & 1
    column = fiota((HALF_ROWS, COLS), 1)
    for ref, half in ((send_ref, 1 - core), (keep_ref, core)):
        field = out_row - scale * HALF + half * HALF
        same = lane_scale == scale
        wind = same & (wind_field == field)
        rest = same & (rest_field == field)
        rate = table_ref[pl.ds(pl.multiple_of(half * HALF, 8), HALF), :]
        rate = jnp.concatenate([rate[:, s:s + 1] for s in range(SCALES)], axis=0)
        fall = jnp.exp(-rate * (column + 1.0))
        rise = jnp.exp(-rate * (COLS - column))
        for side in range(2):
            pick = lambda k: jnp.sum(
                jnp.where(wind, weights[0][side][k], 0.0) + jnp.where(rest, weights[1][side][k], 0.0),
                axis=1, keepdims=True)
            rows = slice(side * HALF_ROWS, (side + 1) * HALF_ROWS)
            ref[rows, :] = local_ref[half, rows, :] + pick(0) * fall + pick(1) * rise


def column_sums(table, lanes, part, theirs, edge, local):
    half = jax.ShapeDtypeStruct((2 * HALF_ROWS, COLS), F32)
    return pl.pallas_call(
        column_sums_kernel,
        in_specs=[VMEM] * 6,
        out_specs=[VMEM] * 3,
        out_shape=[jax.ShapeDtypeStruct((ROWS, 512), F32), half, half],
        compiler_params=params(),
        name="column_sums",
    )(table, lanes, part, theirs, edge, local)


LEFT = slice(0, HALF_ROWS)
RIGHT = slice(HALF_ROWS, 2 * HALF_ROWS)
STEPS = 21


def steps_kernel(table_ref, _, out_ref):
    lat = lat_index()
    odd = (lat & 1) == 1
    odd_chip = ((lat >> 1) & 1) == 1
    z = lat >> 2
    zf = z.astype(F32)
    rate = table_ref[pl.ds(pl.multiple_of((lat & 1) * HALF, 8), HALF), :]
    rate = jnp.concatenate([rate[:, s:s + 1] for s in range(SCALES)], axis=0)
    rate = jnp.broadcast_to(rate, (HALF_ROWS, LANES))
    power = lambda n: jnp.exp(-rate * n)
    quad = lambda n: power(4.0 * ROWS * n)
    one, zero = jnp.ones_like(rate), jnp.zeros_like(rate)
    device, chip = power(1.0 * ROWS), power(2.0 * ROWS)
    out = [jnp.where(odd, one, device), jnp.where(odd, device, one)]
    out += [jnp.where(odd_chip, one, chip), jnp.where(odd_chip, chip, one)]
    out += [power(1.0 + 4 * ROWS * jnp.maximum(7.0 - 2.0 * zf, 1.0))]
    for d in (1, 2, 3):
        other = z ^ d
        of = other.astype(F32)
        below = other < z
        gap = quad(jnp.abs(zf - of) - 1.0)
        out += [jnp.where(below, gap, zero), jnp.where(below, zero, gap), jnp.where(below, quad(3.0 - of), zero)]
    out += [quad(3.0 - zf), quad(3.0 - zf) * power(1.0)]
    out += [jnp.where(odd_chip, chip, one), jnp.where(odd_chip, one, zero)]
    out += [jnp.where(odd_chip, one, chip), jnp.where(odd_chip, zero, one)]
    out += [device]
    for k, value in enumerate(out):
        out_ref[k] = value


def lat_steps(table, before):
    return pl.pallas_call(
        steps_kernel,
        in_specs=[VMEM, ANY],
        out_specs=VMEM,
        out_shape=jax.ShapeDtypeStruct((STEPS, HALF_ROWS, LANES), F32),
        compiler_params=params(),
        name="lat_steps",
    )(table, before)


def by_tile(body):
    for b in range(PARTS):
        body(slice(b * LANES, (b + 1) * LANES))


def chip_merge_kernel(steps_ref, keep_ref, got_ref, chip_ref):
    def body(lanes):
        mine, other = steps_ref[0], steps_ref[1]
        chip_ref[LEFT, lanes] = mine * keep_ref[LEFT, lanes] + other * got_ref[LEFT, lanes]
        chip_ref[RIGHT, lanes] = other * keep_ref[RIGHT, lanes] + mine * got_ref[RIGHT, lanes]

    by_tile(body)


def chip_merge(steps, keep, got):
    return pl.pallas_call(
        chip_merge_kernel,
        in_specs=[VMEM] * 3,
        out_specs=VMEM,
        out_shape=jax.ShapeDtypeStruct((2 * HALF_ROWS, COLS), F32),
        compiler_params=params(),
        name="chip_merge",
    )(steps, keep, got)


def quad_merge_kernel(steps_ref, chip_ref, pair_ref, _, left_ref, s1_ref, s2_ref, s3_ref):
    z = lat_index() >> 2

    def body(lanes):
        mine, other, image = steps_ref[2], steps_ref[3], steps_ref[4]
        left = mine * chip_ref[LEFT, lanes] + other * pair_ref[LEFT, lanes]
        right = other * chip_ref[RIGHT, lanes] + mine * pair_ref[RIGHT, lanes]
        back = right - image * left
        left_ref[:, lanes] = left
        for d, ref in ((1, s1_ref), (2, s2_ref), (3, s3_ref)):
            ref[:, lanes] = jnp.where((z ^ d) > z, left, back)

    by_tile(body)


def quad_merge(steps, chip, pair, after):
    one = jax.ShapeDtypeStruct((HALF_ROWS, COLS), F32)
    return pl.pallas_call(
        quad_merge_kernel,
        in_specs=[VMEM] * 3 + [ANY],
        out_specs=[VMEM] * 4,
        out_shape=[one] * 4,
        compiler_params=params(),
        name="quad_merge",
    )(steps, chip, pair, after)


def lat_carry_kernel(steps_ref, keep_ref, got_ref, pair_ref, left_ref, g1_ref, g2_ref, g3_ref, _,
                     own_ref, send_ref):
    odd = (lat_index() & 1) == 1

    def body(lanes):
        left, right, whole = 0.0, 0.0, steps_ref[14] * left_ref[:, lanes]
        for k, ref in ((5, g1_ref), (8, g2_ref), (11, g3_ref)):
            g = ref[:, lanes]
            left = left + steps_ref[k] * g
            right = right + steps_ref[k + 1] * g
            whole = whole + steps_ref[k + 2] * g
        right = right - steps_ref[15] * whole
        left = steps_ref[16] * left + steps_ref[17] * pair_ref[LEFT, lanes]
        right = steps_ref[18] * right + steps_ref[19] * pair_ref[RIGHT, lanes]
        low_left = jnp.where(odd, got_ref[LEFT, lanes], keep_ref[LEFT, lanes])
        high_right = jnp.where(odd, keep_ref[RIGHT, lanes], got_ref[RIGHT, lanes])
        high_l = low_left + steps_ref[20] * left
        low_r = high_right + steps_ref[20] * right
        own_ref[LEFT, lanes] = jnp.where(odd, high_l, left)
        own_ref[RIGHT, lanes] = jnp.where(odd, right, low_r)
        send_ref[LEFT, lanes] = jnp.where(odd, left, high_l)
        send_ref[RIGHT, lanes] = jnp.where(odd, low_r, right)

    by_tile(body)


def lat_carry(steps, keep, got, pair, left, gs, after):
    half = jax.ShapeDtypeStruct((2 * HALF_ROWS, COLS), F32)
    return pl.pallas_call(
        lat_carry_kernel,
        in_specs=[VMEM] * 8 + [ANY],
        out_specs=[VMEM] * 2,
        out_shape=[half, half],
        compiler_params=params(),
        name="lat_carry",
    )(steps, keep, got, pair, left, *gs, after)


def local_filter_kernel(starts, use_x, use_carry, table_ref, carry_ref, x_ref, base_ref, out_ref):
    top = lat_index() == 0
    shape = (ROWS, LANES)
    row = fiota(shape, 0)
    lane = iota(shape, 1)
    source = jnp.where(lane >= ROWS, lane - ROWS, lane).astype(F32)
    used = lane < 2 * ROWS
    gap = jnp.abs(row - source)
    gap_low = jnp.abs(source - 1.0 - row)
    gap_high = jnp.abs(source + 1.0 - row)
    first = source == 0.0
    spread = jnp.abs(fiota((LANES, LANES), 0) - fiota((LANES, LANES), 1))
    tag = lane & 31
    corner = jnp.zeros((LANES, LANES), BF16)
    left_lane = (lane == LANES - 1) | (lane == 1) | (lane == 3)
    flat = lane[:1]
    row_scale = jnp.where((flat == LANES - 1) | (flat == 0), 0, jnp.where(flat <= 2, 1, 2))
    base = iota((8, LANES), 0)
    column = fiota((8, LANES), 1)

    def carry_tile(tile, virtual):
        left = carry_ref[:, tile * 256:tile * 256 + 128]
        right = carry_ref[:, tile * 256 + 128:tile * 256 + 256]
        left = pltpu.roll(left, (LANES - virtual) % LANES, 1)
        right = pltpu.roll(right, (LANES + 1 - virtual) % LANES, 1)
        return jnp.where(tag == 0, left, jnp.where(tag == 1, right, 0.0))

    def column_pass(matrices, x, carry):
        parts = [split(jnp.where(used, m, 0.0)) for m in matrices]
        lhs = jnp.concatenate([jnp.concatenate([mh, ml[:, :ROWS]], axis=1) for mh, ml in parts], axis=0)
        wide = [t for t in (x, carry) if t is not None]
        wide = wide[0] if len(wide) == 1 else jnp.concatenate(wide, axis=1)
        xh, xl = split(wide)
        rhs = jnp.concatenate([xh, xl, jnp.zeros((32, wide.shape[1]), BF16), xh], axis=0)
        return mm(lhs, rhs)

    def column_stage(f, wind):
        facts = table_ref[pl.ds(f, 1), :]
        rates = [facts[:, s:s + 1] for s in range(SCALES)]
        gains = [facts[:, SCALES + s:SCALES + s + 1] for s in range(SCALES)]
        plain = [gains[s] * jnp.exp(-rates[s] * gap) for s in range(SCALES)]
        if wind:
            slopes = []
            for s in range(SCALES):
                slope = jnp.exp(-rates[s] * gap_low) - jnp.exp(-rates[s] * gap_high)
                slope = slope - jnp.where(top & first, jnp.exp(-rates[s] * (row + 1.0)), 0.0)
                slopes.append((0.5 * gains[s]) * slope)
            stream = f < GROUP
            second_sign = 1.0 if stream else -1.0
            meridional = f if stream else f + 16
            zonal = f + 8
            pair = f + 8 if stream else f - 8
            w = column_pass(plain, -zonal_difference(x_ref[pair]), carry_tile(0, zonal))
            w = w + column_pass(slopes, second_sign * x_ref[f], carry_tile(0, meridional))
        else:
            w = column_pass(plain, x_ref[f] if use_x else None, carry_tile(1, f - WINDS) if use_carry else None)
        return rates, w

    def row_stage(rates, w):
        outs = []
        for s in range(SCALES):
            rows = slice(s * ROWS, (s + 1) * ROWS)
            stack = jnp.concatenate([w[rows, b * LANES:(b + 1) * LANES] for b in range(PARTS)], axis=0)
            wh, wl = split(stack)
            th, tl = split(jnp.exp(-rates[s] * spread))
            lhs = jnp.concatenate([wh, wl], axis=1)
            rhs = jnp.concatenate([jnp.concatenate([th, tl], axis=1), jnp.concatenate([th, corner], axis=1)], axis=0)
            out = mm(lhs, rhs)
            outs.append(out[:, :LANES] + out[:, LANES:])
        return outs

    def carry_stage(rates, w, outs):
        sums, outer = None, jnp.zeros((ROWS, LANES), F32)
        for s in range(SCALES):
            here = row_scale == s
            if use_carry:
                moved = pltpu.roll(w[s * ROWS:(s + 1) * ROWS, w.shape[1] - LANES:], LANES - 30 * s - 1, 1)
                outer = moved if s == 0 else jnp.where(here, moved, outer)
            if use_x:
                turned = outs[s] if s == 0 else pltpu.roll(outs[s], 2 * s, 1)
                sums = turned if s == 0 else jnp.where(here, turned, sums)
        rate_row = jnp.where(row_scale == 0, rates[0], jnp.where(row_scale == 1, rates[1], rates[2]))
        jump = jnp.exp(-rate_row * LANES)
        from_left, from_right = [outer], [outer]
        for b in range(PARTS - 1):
            ahead, behind = jump * from_left[-1], jump * from_right[-1]
            if use_x:
                ahead = ahead + sums[b * ROWS:(b + 1) * ROWS]
                behind = behind + sums[(PARTS - 1 - b) * ROWS:(PARTS - b) * ROWS]
            from_left.append(ahead)
            from_right.append(behind)
        carries = [jnp.where(left_lane, from_left[b], from_right[PARTS - 1 - b]) for b in range(PARTS)]
        ch, cl = split(jnp.concatenate(carries, axis=0))
        low_rate = jnp.where(base == 0, rates[0], jnp.where(base <= 2, rates[1], rates[2]))
        low_left = (base == 1) | (base == 3)
        low = jnp.where(base <= 4, jnp.exp(-low_rate * jnp.where(low_left, column + 1.0, LANES - column)), 0.0)
        high = jnp.where(base == 7, jnp.exp(-rates[0] * (column + 1.0)), 0.0)
        pad = jnp.zeros((8, LANES), F32)
        lh, ll = split(jnp.concatenate([low, pad], axis=0))
        hh, hl = split(jnp.concatenate([pad, high], axis=0))
        gap_rows = jnp.zeros((96, LANES), BF16)
        bh = jnp.concatenate([lh, gap_rows, hh], axis=0)
        bl = jnp.concatenate([ll, gap_rows, hl], axis=0)
        rhs = jnp.concatenate([jnp.concatenate([bh, bl], axis=1), jnp.concatenate([bh, corner], axis=1)], axis=0)
        return jnp.concatenate([ch, cl], axis=1), rhs

    for start in starts:
        wind = start < WINDS
        fields = [start + i for i in range(GROUP)]
        columns = [column_stage(f, wind) for f in fields]
        outs = [row_stage(*c) if use_x else None for c in columns]
        ranks = [carry_stage(*c, o) for c, o in zip(columns, outs)]
        for f, o, (lhs, rhs) in zip(fields, outs, ranks):
            out = mm(lhs, rhs)
            total = out[:, :LANES] + out[:, LANES:]
            if use_x:
                total = (o[0] + o[1]) + (o[2] + total)
            for b in range(PARTS):
                lanes = slice(b * LANES, (b + 1) * LANES)
                part = total[b * ROWS:(b + 1) * ROWS]
                if base_ref is not None:
                    part = part + base_ref[f - starts[0], :, lanes]
                out_ref[f - starts[0], :, lanes] = part


def local_filter(table, carry, x, first, count, before, base=None):
    starts = tuple(range(first, first + count, GROUP))
    use_x, use_carry = base is None, carry is not None
    names = ["table"] + ["carry"] * use_carry + ["x"] * use_x + ["base"] * (base is not None) + ["before"]
    arrays = {"table": table, "carry": carry, "x": x, "base": base, "before": before}
    specs = {"before": ANY}

    def body(*refs):
        by_name = dict(zip(names, refs))
        local_filter_kernel(starts, use_x, use_carry, by_name["table"], by_name.get("carry"),
                            by_name.get("x"), by_name.get("base"), refs[len(names)])

    return pl.pallas_call(
        body,
        in_specs=[specs.get(n, VMEM) for n in names],
        out_specs=VMEM,
        out_shape=jax.ShapeDtypeStruct((count, ROWS, COLS), F32),
        compiler_params=params(),
        cost_estimate=pl.CostEstimate(flops=int(count * 30000000), bytes_accessed=count * 150_000, transcendentals=0),
        name="local_filter",
    )(*[arrays[n] for n in names])


def add_carries(half, table_ref, carry_ref, z_refs, part, store):
    row = fiota((8, LANES), 0)
    up_steps, down_steps = row + 1.0, 8.0 - row
    tables = [carry_ref[side, s, part] for side in range(2) for s in range(SCALES)]
    start = pl.multiple_of((half * 3 + part) * GROUP, GROUP)
    group_facts = table_ref[pl.ds(start, GROUP), :]
    for i in range(GROUP):
        facts = group_facts[i:i + 1, :]
        ups = []
        for s in range(SCALES):
            r = jnp.broadcast_to(facts[:, s:s + 1], (8, LANES))
            w = jnp.broadcast_to(facts[:, SCALES + s:SCALES + s + 1], (8, LANES))
            jump = jnp.exp(-8.0 * r)
            up, down = [w * jnp.exp(-r * up_steps)], [w * jnp.exp(-r * down_steps)]
            for _ in range(ROWS // 8 - 1):
                up.append(up[-1] * jump)
                down.insert(0, down[0] * jump)
            ups.append((jnp.concatenate(up, axis=0), jnp.concatenate(down, axis=0)))
        for b in range(PARTS):
            lanes = slice(b * LANES, (b + 1) * LANES)
            total = jnp.where(half == 0, z_refs[part // 2][part % 2 * GROUP + i, :, lanes],
                              z_refs[(3 + part) // 2][(3 + part) % 2 * GROUP + i, :, lanes])
            for s in range(SCALES):
                total = total + ups[s][0] * tables[s][i:i + 1, lanes] + ups[s][1] * tables[SCALES + s][i:i + 1, lanes]
            store(i, lanes, total)


def finish_own_kernel(table_ref, carry_ref, z0_ref, z1_ref, z2_ref, out_ref):
    for part in range(3):
        def store(i, lanes, value):
            out_ref[part * GROUP + i, :, lanes] = value

        add_carries(lat_index() & 1, table_ref, carry_ref, (z0_ref, z1_ref, z2_ref), part, store)


def finish_own(table, carry, parts):
    return pl.pallas_call(
        finish_own_kernel,
        in_specs=[VMEM] * 5,
        out_specs=VMEM,
        out_shape=jax.ShapeDtypeStruct((HALF, ROWS, COLS), F32),
        compiler_params=params(),
        cost_estimate=pl.CostEstimate(flops=1_000_000_000, bytes_accessed=2_000_000, transcendentals=0),
        name="finish_own",
    )(table, carry.reshape(2, SCALES, 3, GROUP, COLS), *parts)


def finish_kernel(table_ref, carry_ref, z0_ref, z1_ref, z2_ref, own_ref, out_ref, buf_ref, sem):
    half = 1 - (lat_index() & 1)
    ready = pltpu.make_async_copy(own_ref, out_ref.at[pl.ds((1 - half) * HALF, HALF)], sem.at[3])
    ready.start()
    copies = [ready]
    for part in range(3):
        def store(i, lanes, value):
            buf_ref[part, i, :, lanes] = value

        add_carries(half, table_ref, carry_ref, (z0_ref, z1_ref, z2_ref), part, store)
        there = out_ref.at[pl.ds((half * 3 + part) * GROUP, GROUP)]
        copies.append(pltpu.make_async_copy(buf_ref.at[part], there, sem.at[part]))
        copies[-1].start()
    for copy in copies:
        copy.wait()


def finish(table, carry, parts, own):
    return pl.pallas_call(
        finish_kernel,
        in_specs=[VMEM] * 6,
        out_specs=HBM,
        out_shape=jax.ShapeDtypeStruct((FIELDS, ROWS, COLS), F32),
        scratch_shapes=[pltpu.VMEM((3, GROUP, ROWS, COLS), F32), pltpu.SemaphoreType.DMA((4,))],
        compiler_params=params(),
        name="finish",
    )(table, carry.reshape(2, SCALES, 3, GROUP, COLS), *parts, own)


def partner(axis, count, bit):
    return functools.partial(lax.ppermute, axis_name=axis, perm=[(i, i ^ bit) for i in range(count)])


def shards(x, lengths, weights):
    facts = jnp.concatenate([lengths.T, weights.T], axis=0)
    sums, edge, table, lanes, held = row_sums(facts, x)
    got = [partner("lon", NLON, d)(sums) for d in (1, 2, 3)]
    early = local_filter(table, None, held, 32, 16, sums)
    part, half = lon_merge(lanes, sums, got, early)
    theirs = partner("lon", NLON, 4)(half)
    local = local_sums(table, held, part)
    steps = lat_steps(table, part)
    carry, keep, send = column_sums(table, lanes, part, theirs, edge, local)
    got_core = partner("lat", NLAT, 1)(send)
    chip = chip_merge(steps, keep, got_core)
    pair = partner("lat", NLAT, 2)(chip)
    z0 = local_filter(table, carry, held, 0, 16, chip)
    left, *sends = quad_merge(steps, chip, pair, z0)
    gs = [partner("lat", NLAT, 4 * d)(t) for d, t in zip((1, 2, 3), sends)]
    z1 = local_filter(table, carry, held, 16, 16, left)
    z2 = local_filter(table, carry, held, 32, 16, z1, early)
    own, other = lat_carry(steps, keep, got_core, pair, left, gs, z2)
    got_carry = partner("lat", NLAT, 1)(other)
    done = finish_own(table, own, (z0, z1, z2))
    return finish(table, got_carry, (z0, z1, z2), done)


def solution(mesh):
    in_specs = (P(None, "lat", "lon"), P(), P())
    out_specs = P(None, "lat", "lon")
    return jax.shard_map(shards, mesh=mesh, in_specs=in_specs, out_specs=out_specs, check_vma=False)
```

```python
import functools

import jax
import jax.numpy as jnp
from jax import lax
from jax.experimental import pallas as pl
from jax.experimental.pallas import tpu as pltpu
from jax.sharding import PartitionSpec as P

LEVELS = 8
SCALES = 3
WINDS = 16
FIELDS = 48
ROWS = 48
COLS = 384
GROUP = 8
GROUPS = FIELDS // GROUP
NLAT = 16
NLON = 8
LANES = 128
PARTS = COLS // LANES
HALF = FIELDS // 2
HALF_ROWS = SCALES * HALF
F32 = jnp.float32
BF16 = jnp.bfloat16

VMEM = pl.BlockSpec(memory_space=pltpu.VMEM)
BIG = 48 * 1024 * 1024
WHOLE = 50 * 1024 * 1024


def lat_index():
    return lax.axis_index("lat")


def lon_index():
    return lax.axis_index("lon")


def params(**kw):
    return pltpu.CompilerParams(vmem_limit_bytes=BIG, **kw)


def iota(shape, dim):
    return lax.broadcasted_iota(jnp.int32, shape, dim)


def fiota(shape, dim):
    return iota(shape, dim).astype(F32)


def split(value):
    high = value.astype(BF16)
    return high, (value - high.astype(F32)).astype(BF16)


def mm(a, b):
    return jnp.dot(a, b, preferred_element_type=F32)


def lane_fields(shape):
    lane = iota(shape, 1)
    virtual = lane & 31
    wind_field = ((virtual >> 4) << 3) + (virtual & 7)
    return lane, lane >> 5, virtual, wind_field, virtual + WINDS


def exact(a, b, dims):
    return lax.dot_general(a, b, (dims, ((), ())), precision=lax.Precision.HIGHEST, preferred_element_type=F32)


def lane_rates(rate):
    shape = (FIELDS, LANES)
    _, _, _, wind_field, rest_field = lane_fields(shape)
    field = iota(shape, 0)
    lane = iota((1, LANES), 1)

    def pick(which):
        every = exact(rate, jnp.where(field == which, 1.0, 0.0).astype(F32), ((1,), (0,)))
        value = jnp.where(lane < 32, every[0:1], jnp.where(lane < 64, every[1:2], every[2:3]))
        return jnp.where(lane < 96, value, 0.0)

    return pick(wind_field), pick(rest_field)


def scale_weights(rate, weights):
    decay = jnp.exp(-rate)
    leak = 1.0 - decay
    cube = (1.0 + decay) * (1.0 + decay) * (1.0 + decay)
    coefficient = weights * cube / (leak * (1.0 + decay * decay))
    kappa = leak / (1.0 + decay)
    return coefficient * kappa * kappa


def lane_kinds(shape):
    _, _, virtual, _, _ = lane_fields(shape)
    second = virtual >= 16
    north = (virtual & 15) >= 8
    zonal = second != north
    sign = jnp.where(second | north, -1.0, 1.0).astype(F32)
    return zonal, sign


def row_sums_kernel(len_ref, x_ref, sums_ref, edge_ref, table_ref, lanes_ref, held_ref, w_ref, sem):
    lon = lon_index()
    copies = []
    for k, (start, stop) in enumerate(((0, WINDS), (WINDS, FIELDS))):
        here = pl.ds(start, stop - start)
        copies.append(pltpu.make_async_copy(x_ref.at[here], held_ref.at[here], sem.at[k]))
        copies[-1].start()
    rate = 1.0 / len_ref[0:SCALES, :]
    pair = lane_rates(rate)
    lanes_ref[...] = jnp.concatenate([pair[0], pair[1], jnp.ones((6, LANES), F32)], axis=0)
    column = fiota((COLS, LANES), 0)
    for tile, rates in enumerate(pair):
        for side, steps in enumerate((COLS - 1 - column, column)):
            high, low = split(jnp.exp(-rates * steps))
            lanes = slice(side * LANES, (side + 1) * LANES)
            w_ref[tile, 0:COLS, lanes] = high
            w_ref[tile, COLS:2 * COLS, lanes] = high
            w_ref[tile, 2 * COLS:, lanes] = low
    both = jnp.concatenate([rate, scale_weights(rate, len_ref[SCALES:, :]), jnp.ones((2, FIELDS), F32)], axis=0)
    eye = jnp.where(iota((8, LANES), 0) == iota((8, LANES), 1), 1.0, 0.0).astype(F32)
    table_ref[...] = exact(both, eye, ((0,), (0,)))
    lane = iota((ROWS, LANES), 1)
    virtual = lane & 31
    zero = jnp.zeros((ROWS, LANES), F32)
    left, right, first, last = zero, zero, zero, zero
    for g in range(GROUPS):
        if g in (0, 2):
            copies[g // 2].wait()
        x = held_ref[g * GROUP:(g + 1) * GROUP].reshape(GROUP * ROWS, COLS)
        xh, xl = split(x)
        res = mm(jnp.concatenate([xh, xl, xh], axis=1), w_ref[0 if g < 2 else 1])
        if g == 2:
            left, right = zero, zero
        for i in range(GROUP):
            rows = slice(i * ROWS, (i + 1) * ROWS)
            mine = (virtual & 15) == g * GROUP + i if g < 2 else virtual == (g - 2) * GROUP + i
            left = jnp.where(mine, res[rows, 0:128], left)
            right = jnp.where(mine, res[rows, 128:256], right)
            if g < 2:
                first = jnp.where(mine, x[rows, 0:1], first)
                last = jnp.where(mine, x[rows, COLS - 1:COLS], last)
        if g == 1:
            edge = jnp.where(lon == 0, first, jnp.where(lon == NLON - 1, last, 0.0))
            sums_ref[:, 0:128] = jnp.where(lane >= 96, edge, left)
            sums_ref[:, 128:256] = right
            edge_ref[:, 0:128] = first
            edge_ref[:, 128:256] = last
    sums_ref[:, 256:384] = left
    sums_ref[:, 384:512] = right


HBM = pl.BlockSpec(memory_space=pltpu.HBM)
ANY = pl.BlockSpec(memory_space=pl.ANY)


def row_sums(facts, x):
    return pl.pallas_call(
        row_sums_kernel,
        in_specs=[VMEM, HBM],
        out_specs=[VMEM] * 5,
        out_shape=[jax.ShapeDtypeStruct((ROWS, 512), F32), jax.ShapeDtypeStruct((ROWS, 256), F32),
                   jax.ShapeDtypeStruct((FIELDS, LANES), F32), jax.ShapeDtypeStruct((8, LANES), F32),
                   jax.ShapeDtypeStruct((FIELDS, ROWS, COLS), F32)],
        scratch_shapes=[pltpu.VMEM((2, 3 * COLS, 256), BF16), pltpu.SemaphoreType.DMA((2,))],
        compiler_params=pltpu.CompilerParams(vmem_limit_bytes=WHOLE),
        name="row_sums",
    )(facts, x)


def zonal_difference(x):
    shape = x.shape
    axis = len(shape) - 1
    column = iota(shape, axis)
    ahead = jnp.where(column == COLS - 1, 0.0, pltpu.roll(x, COLS - 1, axis))
    behind = jnp.where(column == 0, 0.0, pltpu.roll(x, 1, axis))
    return 0.5 * (ahead - behind)


def local_sums_kernel(table_ref, x_ref, _, out_ref):
    top = lat_index() == 0
    count = 2 * SCALES * GROUP
    shape = (count, LANES)
    out_row = iota(shape, 0)
    member = out_row & 7
    left_side = out_row < SCALES * GROUP
    lane = iota(shape, 1)
    source = jnp.where(lane >= ROWS, lane - ROWS, lane).astype(F32)
    used = lane < 2 * ROWS
    steps = jnp.where(left_side, ROWS - 1 - source, source)
    zeros = jnp.zeros((32, COLS), BF16)

    def weighted(matrix, x, i):
        mh, ml = split(jnp.where(used & (member == i), matrix, 0.0))
        xh, xl = split(x)
        return mm(jnp.concatenate([mh, ml[:, :ROWS]], axis=1), jnp.concatenate([xh, xl, zeros, xh], axis=0))

    def group_sums(group, wind):
        rate = table_ref[group * GROUP:(group + 1) * GROUP, :]
        row_rate = jnp.concatenate([rate[:, s:s + 1] for _ in range(2) for s in range(SCALES)], axis=0)
        wide = jnp.broadcast_to(row_rate, shape)
        plain = jnp.exp(-wide * steps)
        acc = jnp.zeros((count, COLS), F32)
        if wind:
            decay = jnp.exp(-wide)
            gain = 0.5 * (1.0 - decay * decay) / decay
            start = jnp.where(top & (source == 0.0), 0.5 * jnp.exp(-wide * ROWS), 0.0)
            slope = jnp.where(left_side, -gain * plain - start, gain * plain)
            second_sign = jnp.where(group == 0, 1.0, -1.0)
            for i in range(GROUP):
                acc += weighted(plain, -zonal_difference(x_ref[(1 - group) * GROUP + i]), i)
                acc += weighted(slope, second_sign * x_ref[group * GROUP + i], i)
        else:
            for i in range(GROUP):
                acc += weighted(plain, x_ref[group * GROUP + i], i)
        return acc, row_rate

    made = [group_sums(group, group < 2) for group in range(GROUPS)]
    acc = jnp.concatenate([m[0] for m in made], axis=0)
    factor = jnp.concatenate([jnp.broadcast_to(jnp.exp(-m[1]), (count, LANES)) for m in made], axis=0)
    factor = jnp.concatenate([factor] * PARTS, axis=1)
    column = iota(acc.shape, 1)
    forward, backward = acc, acc
    step = 1
    while step < COLS:
        forward = forward + factor * jnp.where(column >= step, pltpu.roll(forward, step, 1), 0.0)
        backward = backward + factor * jnp.where(column < COLS - step, pltpu.roll(backward, COLS - step, 1), 0.0)
        factor = factor * factor
        step *= 2
    acc = forward + backward - acc
    for group in range(GROUPS):
        for side in range(2):
            for s in range(SCALES):
                k = group * count + (side * SCALES + s) * GROUP
                out_ref[group // 3, side, s, group % 3] = acc[k:k + GROUP]


def local_sums(table, x, before):
    out = pl.pallas_call(
        local_sums_kernel,
        in_specs=[VMEM, VMEM, ANY],
        out_specs=VMEM,
        out_shape=jax.ShapeDtypeStruct((2, 2, SCALES, 3, GROUP, COLS), F32),
        compiler_params=params(),
        cost_estimate=pl.CostEstimate(flops=600000000, bytes_accessed=4_000_000, transcendentals=0),
        name="local_sums",
    )(table, x, before)
    return out.reshape(2, 2 * HALF_ROWS, COLS)


def lon_merge_kernel(lanes_ref, own_ref, g1_ref, g3_ref, g2_ref, _, part_ref, send_ref):
    y = lon_index() & 3
    high = lon_index() >= 4
    yf = y.astype(F32)
    zonal, _ = lane_kinds((1, LANES))
    lane = iota((1, LANES), 1)
    for tile in range(2):
        rate = lanes_ref[tile:tile + 1, :]
        step = lambda n: jnp.exp(-rate * (COLS * n))
        base = tile * 256
        lanes_l = slice(base, base + 128)
        lanes_r = slice(base + 128, base + 256)
        left_total = step(3.0 - yf) * own_ref[:, lanes_l]
        right_total = step(yf) * own_ref[:, lanes_r]
        left = jnp.zeros((ROWS, LANES), F32)
        right = jnp.zeros((ROWS, LANES), F32)
        for d, ref in ((1, g1_ref), (2, g2_ref), (3, g3_ref)):
            other = y ^ d
            of = other.astype(F32)
            below = other < y
            lg, rg = ref[:, lanes_l], ref[:, lanes_r]
            gap = jnp.abs(yf - of) - 1.0
            left = left + jnp.where(below, step(gap), 0.0) * lg
            right = right + jnp.where(below, 0.0, step(gap)) * rg
            left_total = left_total + step(3.0 - of) * lg
            right_total = right_total + step(of) * rg
        part_ref[:, lanes_l] = left
        part_ref[:, lanes_r] = right
        part_ref[:, 512 + tile * 128:640 + tile * 128] = left_total
        image = jnp.exp(-rate * (4.0 * COLS + 1.0))
        if tile == 0:
            image = jnp.where(zonal, -image, image)
            image = jnp.where(lane >= 96, -1.0, image)
            right_total = jnp.where(lane >= 96, 0.0, right_total)
        send_ref[:, tile * 128:tile * 128 + 128] = jnp.where(high, right_total - image * left_total, left_total)


def lon_merge(lanes, own, got, after):
    return pl.pallas_call(
        lon_merge_kernel,
        in_specs=[VMEM] * 5 + [ANY],
        out_specs=[VMEM, VMEM],
        out_shape=[jax.ShapeDtypeStruct((ROWS, 768), F32), jax.ShapeDtypeStruct((ROWS, 256), F32)],
        compiler_params=params(),
        name="lon_merge",
    )(lanes, own, got[0], got[2], got[1], after)


def spread_edges(tile):
    lane = iota(tile.shape, 1)
    out = tile
    for k in range(6):
        out = jnp.where((lane >> 4) == k, pltpu.roll(tile, (k * 16 + 32) % LANES, 1), out)
    return out


def column_sums_kernel(table_ref, lanes_ref, part_ref, theirs_ref, edge_ref, local_ref,
                       carry_ref, keep_ref, send_ref):
    lat, lon = lat_index(), lon_index()
    y = lon & 3
    yf = y.astype(F32)
    high = lon >= 4
    highf = jnp.where(high, 1.0, 0.0)
    lowf = 1.0 - highf
    lonf = lon.astype(F32)
    top = lat == 0
    rates = (lanes_ref[0:1, :], lanes_ref[1:2, :])
    zonal, sign = lane_kinds((1, LANES))
    row = fiota((ROWS, LANES), 0)
    weights = []
    for tile in range(2):
        rate = rates[tile]
        step = lambda n: jnp.exp(-rate * (COLS * n))
        decay = jnp.exp(-rate)
        theirs = theirs_ref[:, tile * 128:tile * 128 + 128]
        half = part_ref[:, 512 + tile * 128:640 + tile * 128]
        left = part_ref[:, tile * 256:tile * 256 + 128] + (highf * step(yf)) * theirs
        right = part_ref[:, tile * 256 + 128:tile * 256 + 256] + (lowf * step(3.0 - yf)) * theirs
        whole = (highf + lowf * step(4.0)) * half + (highf * step(4.0)) * theirs
        end = step(7.0 - lonf)
        weight_l = jnp.exp(-rate * (ROWS - 1 - row))
        weight_r = jnp.exp(-rate * row)
        carry_l = left
        carry_r = right - (end * decay) * whole
        if tile == 0:
            v0 = spread_edges(lowf * half + highf * theirs)
            vn = spread_edges(highf * half + lowf * theirs)
            gain = 0.5 * (1.0 - decay * decay) / decay
            initial = -0.5 * (v0 + vn / decay)
            zonal_l = step(lonf) * initial - gain * left + 0.5 * edge_ref[:, 0:128]
            zonal_r = (gain * right - 0.5 * edge_ref[:, 128:256]
                       + end * (gain * v0 - decay * (step(8.0) * initial - gain * whole)))
            carry_l = sign * jnp.where(zonal, zonal_l, carry_l)
            carry_r = sign * jnp.where(zonal, zonal_r, carry_r)
            start = jnp.where(top & (row == 0.0), 0.5 * jnp.exp(-rate * ROWS), 0.0)
            weight_l = jnp.where(zonal, weight_l, -gain * weight_l - start)
            weight_r = jnp.where(zonal, weight_r, gain * weight_r)
        carry_ref[:, tile * 256:tile * 256 + 128] = carry_l
        carry_ref[:, tile * 256 + 128:tile * 256 + 256] = carry_r
        fold = lambda w, c: jnp.sum(w * c, axis=0, keepdims=True)
        weights.append(((fold(weight_l, carry_l), fold(weight_l, carry_r)),
                        (fold(weight_r, carry_l), fold(weight_r, carry_r))))
    shape = (HALF_ROWS, LANES)
    lane, lane_scale, _, wind_field, rest_field = lane_fields(shape)
    out_row = iota(shape, 0)
    scale = jnp.where(out_row < HALF, 0, jnp.where(out_row < 2 * HALF, 1, 2))
    core = lat & 1
    column = fiota((HALF_ROWS, COLS), 1)
    for ref, half in ((send_ref, 1 - core), (keep_ref, core)):
        field = out_row - scale * HALF + half * HALF
        same = lane_scale == scale
        wind = same & (wind_field == field)
        rest = same & (rest_field == field)
        rate = table_ref[pl.ds(pl.multiple_of(half * HALF, 8), HALF), :]
        rate = jnp.concatenate([rate[:, s:s + 1] for s in range(SCALES)], axis=0)
        fall = jnp.exp(-rate * (column + 1.0))
        rise = jnp.exp(-rate * (COLS - column))
        for side in range(2):
            pick = lambda k: jnp.sum(
                jnp.where(wind, weights[0][side][k], 0.0) + jnp.where(rest, weights[1][side][k], 0.0),
                axis=1, keepdims=True)
            rows = slice(side * HALF_ROWS, (side + 1) * HALF_ROWS)
            ref[rows, :] = local_ref[half, rows, :] + pick(0) * fall + pick(1) * rise


def column_sums(table, lanes, part, theirs, edge, local):
    half = jax.ShapeDtypeStruct((2 * HALF_ROWS, COLS), F32)
    return pl.pallas_call(
        column_sums_kernel,
        in_specs=[VMEM] * 6,
        out_specs=[VMEM] * 3,
        out_shape=[jax.ShapeDtypeStruct((ROWS, 512), F32), half, half],
        compiler_params=params(),
        name="column_sums",
    )(table, lanes, part, theirs, edge, local)


LEFT = slice(0, HALF_ROWS)
RIGHT = slice(HALF_ROWS, 2 * HALF_ROWS)
STEPS = 21


def steps_kernel(table_ref, _, out_ref):
    lat = lat_index()
    odd = (lat & 1) == 1
    odd_chip = ((lat >> 1) & 1) == 1
    z = lat >> 2
    zf = z.astype(F32)
    rate = table_ref[pl.ds(pl.multiple_of((lat & 1) * HALF, 8), HALF), :]
    rate = jnp.concatenate([rate[:, s:s + 1] for s in range(SCALES)], axis=0)
    rate = jnp.broadcast_to(rate, (HALF_ROWS, LANES))
    power = lambda n: jnp.exp(-rate * n)
    quad = lambda n: power(4.0 * ROWS * n)
    one, zero = jnp.ones_like(rate), jnp.zeros_like(rate)
    device, chip = power(1.0 * ROWS), power(2.0 * ROWS)
    out = [jnp.where(odd, one, device), jnp.where(odd, device, one)]
    out += [jnp.where(odd_chip, one, chip), jnp.where(odd_chip, chip, one)]
    out += [power(1.0 + 4 * ROWS * jnp.maximum(7.0 - 2.0 * zf, 1.0))]
    for d in (1, 2, 3):
        other = z ^ d
        of = other.astype(F32)
        below = other < z
        gap = quad(jnp.abs(zf - of) - 1.0)
        out += [jnp.where(below, gap, zero), jnp.where(below, zero, gap), jnp.where(below, quad(3.0 - of), zero)]
    out += [quad(3.0 - zf), quad(3.0 - zf) * power(1.0)]
    out += [jnp.where(odd_chip, chip, one), jnp.where(odd_chip, one, zero)]
    out += [jnp.where(odd_chip, one, chip), jnp.where(odd_chip, zero, one)]
    out += [device]
    for k, value in enumerate(out):
        out_ref[k] = value


def lat_steps(table, before):
    return pl.pallas_call(
        steps_kernel,
        in_specs=[VMEM, ANY],
        out_specs=VMEM,
        out_shape=jax.ShapeDtypeStruct((STEPS, HALF_ROWS, LANES), F32),
        compiler_params=params(),
        name="lat_steps",
    )(table, before)


def by_tile(body):
    for b in range(PARTS):
        body(slice(b * LANES, (b + 1) * LANES))


def chip_merge_kernel(steps_ref, keep_ref, got_ref, chip_ref):
    def body(lanes):
        mine, other = steps_ref[0], steps_ref[1]
        chip_ref[LEFT, lanes] = mine * keep_ref[LEFT, lanes] + other * got_ref[LEFT, lanes]
        chip_ref[RIGHT, lanes] = other * keep_ref[RIGHT, lanes] + mine * got_ref[RIGHT, lanes]

    by_tile(body)


def chip_merge(steps, keep, got):
    return pl.pallas_call(
        chip_merge_kernel,
        in_specs=[VMEM] * 3,
        out_specs=VMEM,
        out_shape=jax.ShapeDtypeStruct((2 * HALF_ROWS, COLS), F32),
        compiler_params=params(),
        name="chip_merge",
    )(steps, keep, got)


def quad_merge_kernel(steps_ref, chip_ref, pair_ref, _, left_ref, s1_ref, s2_ref, s3_ref):
    z = lat_index() >> 2

    def body(lanes):
        mine, other, image = steps_ref[2], steps_ref[3], steps_ref[4]
        left = mine * chip_ref[LEFT, lanes] + other * pair_ref[LEFT, lanes]
        right = other * chip_ref[RIGHT, lanes] + mine * pair_ref[RIGHT, lanes]
        back = right - image * left
        left_ref[:, lanes] = left
        for d, ref in ((1, s1_ref), (2, s2_ref), (3, s3_ref)):
            ref[:, lanes] = jnp.where((z ^ d) > z, left, back)

    by_tile(body)


def quad_merge(steps, chip, pair, after):
    one = jax.ShapeDtypeStruct((HALF_ROWS, COLS), F32)
    return pl.pallas_call(
        quad_merge_kernel,
        in_specs=[VMEM] * 3 + [ANY],
        out_specs=[VMEM] * 4,
        out_shape=[one] * 4,
        compiler_params=params(),
        name="quad_merge",
    )(steps, chip, pair, after)


def lat_carry_kernel(steps_ref, keep_ref, got_ref, pair_ref, left_ref, g2_ref, g1_ref, g3_ref, _,
                     own_ref, send_ref):
    odd = (lat_index() & 1) == 1

    def body(lanes):
        left, right, whole = 0.0, 0.0, steps_ref[14] * left_ref[:, lanes]
        for k, ref in ((5, g1_ref), (8, g2_ref), (11, g3_ref)):
            g = ref[:, lanes]
            left = left + steps_ref[k] * g
            right = right + steps_ref[k + 1] * g
            whole = whole + steps_ref[k + 2] * g
        right = right - steps_ref[15] * whole
        left = steps_ref[16] * left + steps_ref[17] * pair_ref[LEFT, lanes]
        right = steps_ref[18] * right + steps_ref[19] * pair_ref[RIGHT, lanes]
        low_left = jnp.where(odd, got_ref[LEFT, lanes], keep_ref[LEFT, lanes])
        high_right = jnp.where(odd, keep_ref[RIGHT, lanes], got_ref[RIGHT, lanes])
        high_l = low_left + steps_ref[20] * left
        low_r = high_right + steps_ref[20] * right
        own_ref[LEFT, lanes] = jnp.where(odd, high_l, left)
        own_ref[RIGHT, lanes] = jnp.where(odd, right, low_r)
        send_ref[LEFT, lanes] = jnp.where(odd, left, high_l)
        send_ref[RIGHT, lanes] = jnp.where(odd, low_r, right)

    by_tile(body)


def lat_carry(steps, keep, got, pair, left, gs, after):
    half = jax.ShapeDtypeStruct((2 * HALF_ROWS, COLS), F32)
    return pl.pallas_call(
        lat_carry_kernel,
        in_specs=[VMEM] * 8 + [ANY],
        out_specs=[VMEM] * 2,
        out_shape=[half, half],
        compiler_params=params(),
        name="lat_carry",
    )(steps, keep, got, pair, left, gs[1], gs[0], gs[2], after)


def local_filter_kernel(starts, use_x, use_carry, table_ref, carry_ref, x_ref, base_ref, out_ref):
    top = lat_index() == 0
    shape = (ROWS, LANES)
    row = fiota(shape, 0)
    lane = iota(shape, 1)
    source = jnp.where(lane >= ROWS, lane - ROWS, lane).astype(F32)
    used = lane < 2 * ROWS
    gap = jnp.abs(row - source)
    gap_low = jnp.abs(source - 1.0 - row)
    gap_high = jnp.abs(source + 1.0 - row)
    first = source == 0.0
    spread = jnp.abs(fiota((LANES, LANES), 0) - fiota((LANES, LANES), 1))
    tag = lane & 31
    corner = jnp.zeros((LANES, LANES), BF16)
    left_lane = (lane == LANES - 1) | (lane == 1) | (lane == 3)
    flat = lane[:1]
    row_scale = jnp.where((flat == LANES - 1) | (flat == 0), 0, jnp.where(flat <= 2, 1, 2))
    base = iota((8, LANES), 0)
    column = fiota((8, LANES), 1)

    def carry_tile(tile, virtual):
        left = carry_ref[:, tile * 256:tile * 256 + 128]
        right = carry_ref[:, tile * 256 + 128:tile * 256 + 256]
        left = pltpu.roll(left, (LANES - virtual) % LANES, 1)
        right = pltpu.roll(right, (LANES + 1 - virtual) % LANES, 1)
        return jnp.where(tag == 0, left, jnp.where(tag == 1, right, 0.0))

    def column_pass(matrices, x, carry):
        parts = [split(jnp.where(used, m, 0.0)) for m in matrices]
        lhs = jnp.concatenate([jnp.concatenate([mh, ml[:, :ROWS]], axis=1) for mh, ml in parts], axis=0)
        wide = [t for t in (x, carry) if t is not None]
        wide = wide[0] if len(wide) == 1 else jnp.concatenate(wide, axis=1)
        xh, xl = split(wide)
        rhs = jnp.concatenate([xh, xl, jnp.zeros((32, wide.shape[1]), BF16), xh], axis=0)
        return mm(lhs, rhs)

    def column_stage(f, wind):
        facts = table_ref[pl.ds(f, 1), :]
        rates = [facts[:, s:s + 1] for s in range(SCALES)]
        gains = [facts[:, SCALES + s:SCALES + s + 1] for s in range(SCALES)]
        plain = [gains[s] * jnp.exp(-rates[s] * gap) for s in range(SCALES)]
        if wind:
            slopes = []
            for s in range(SCALES):
                slope = jnp.exp(-rates[s] * gap_low) - jnp.exp(-rates[s] * gap_high)
                slope = slope - jnp.where(top & first, jnp.exp(-rates[s] * (row + 1.0)), 0.0)
                slopes.append((0.5 * gains[s]) * slope)
            stream = f < GROUP
            second_sign = 1.0 if stream else -1.0
            meridional = f if stream else f + 16
            zonal = f + 8
            pair = f + 8 if stream else f - 8
            w = column_pass(plain, -zonal_difference(x_ref[pair]), carry_tile(0, zonal))
            w = w + column_pass(slopes, second_sign * x_ref[f], carry_tile(0, meridional))
        else:
            w = column_pass(plain, x_ref[f] if use_x else None, carry_tile(1, f - WINDS) if use_carry else None)
        return rates, w

    def row_stage(rates, w):
        outs = []
        for s in range(SCALES):
            rows = slice(s * ROWS, (s + 1) * ROWS)
            stack = jnp.concatenate([w[rows, b * LANES:(b + 1) * LANES] for b in range(PARTS)], axis=0)
            wh, wl = split(stack)
            th, tl = split(jnp.exp(-rates[s] * spread))
            lhs = jnp.concatenate([wh, wl], axis=1)
            rhs = jnp.concatenate([jnp.concatenate([th, tl], axis=1), jnp.concatenate([th, corner], axis=1)], axis=0)
            out = mm(lhs, rhs)
            outs.append(out[:, :LANES] + out[:, LANES:])
        return outs

    def carry_stage(rates, w, outs):
        sums, outer = None, jnp.zeros((ROWS, LANES), F32)
        for s in range(SCALES):
            here = row_scale == s
            if use_carry:
                moved = pltpu.roll(w[s * ROWS:(s + 1) * ROWS, w.shape[1] - LANES:], LANES - 30 * s - 1, 1)
                outer = moved if s == 0 else jnp.where(here, moved, outer)
            if use_x:
                turned = outs[s] if s == 0 else pltpu.roll(outs[s], 2 * s, 1)
                sums = turned if s == 0 else jnp.where(here, turned, sums)
        rate_row = jnp.where(row_scale == 0, rates[0], jnp.where(row_scale == 1, rates[1], rates[2]))
        jump = jnp.exp(-rate_row * LANES)
        from_left, from_right = [outer], [outer]
        for b in range(PARTS - 1):
            ahead, behind = jump * from_left[-1], jump * from_right[-1]
            if use_x:
                ahead = ahead + sums[b * ROWS:(b + 1) * ROWS]
                behind = behind + sums[(PARTS - 1 - b) * ROWS:(PARTS - b) * ROWS]
            from_left.append(ahead)
            from_right.append(behind)
        carries = [jnp.where(left_lane, from_left[b], from_right[PARTS - 1 - b]) for b in range(PARTS)]
        ch, cl = split(jnp.concatenate(carries, axis=0))
        low_rate = jnp.where(base == 0, rates[0], jnp.where(base <= 2, rates[1], rates[2]))
        low_left = (base == 1) | (base == 3)
        low = jnp.where(base <= 4, jnp.exp(-low_rate * jnp.where(low_left, column + 1.0, LANES - column)), 0.0)
        high = jnp.where(base == 7, jnp.exp(-rates[0] * (column + 1.0)), 0.0)
        pad = jnp.zeros((8, LANES), F32)
        lh, ll = split(jnp.concatenate([low, pad], axis=0))
        hh, hl = split(jnp.concatenate([pad, high], axis=0))
        gap_rows = jnp.zeros((96, LANES), BF16)
        bh = jnp.concatenate([lh, gap_rows, hh], axis=0)
        bl = jnp.concatenate([ll, gap_rows, hl], axis=0)
        rhs = jnp.concatenate([jnp.concatenate([bh, bl], axis=1), jnp.concatenate([bh, corner], axis=1)], axis=0)
        return jnp.concatenate([ch, cl], axis=1), rhs

    for start in starts:
        wind = start < WINDS
        fields = [start + i for i in range(GROUP)]
        columns = [column_stage(f, wind) for f in fields]
        outs = [row_stage(*c) if use_x else None for c in columns]
        ranks = [carry_stage(*c, o) for c, o in zip(columns, outs)]
        for f, o, (lhs, rhs) in zip(fields, outs, ranks):
            out = mm(lhs, rhs)
            total = out[:, :LANES] + out[:, LANES:]
            if use_x:
                total = (o[0] + o[1]) + (o[2] + total)
            for b in range(PARTS):
                lanes = slice(b * LANES, (b + 1) * LANES)
                part = total[b * ROWS:(b + 1) * ROWS]
                if base_ref is not None:
                    part = part + base_ref[f - starts[0], :, lanes]
                out_ref[f - starts[0], :, lanes] = part


def local_filter(table, carry, x, first, count, before, base=None):
    starts = tuple(range(first, first + count, GROUP))
    use_x, use_carry = base is None, carry is not None
    names = ["table"] + ["carry"] * use_carry + ["x"] * use_x + ["base"] * (base is not None) + ["before"]
    arrays = {"table": table, "carry": carry, "x": x, "base": base, "before": before}
    specs = {"before": ANY}

    def body(*refs):
        by_name = dict(zip(names, refs))
        local_filter_kernel(starts, use_x, use_carry, by_name["table"], by_name.get("carry"),
                            by_name.get("x"), by_name.get("base"), refs[len(names)])

    return pl.pallas_call(
        body,
        in_specs=[specs.get(n, VMEM) for n in names],
        out_specs=VMEM,
        out_shape=jax.ShapeDtypeStruct((count, ROWS, COLS), F32),
        compiler_params=params(),
        cost_estimate=pl.CostEstimate(flops=int(count * 30000000), bytes_accessed=count * 150_000, transcendentals=0),
        name="local_filter",
    )(*[arrays[n] for n in names])


def add_carries(half, table_ref, carry_ref, z_refs, part, store):
    row = fiota((8, LANES), 0)
    up_steps, down_steps = row + 1.0, 8.0 - row
    tables = [carry_ref[side, s, part] for side in range(2) for s in range(SCALES)]
    start = pl.multiple_of((half * 3 + part) * GROUP, GROUP)
    group_facts = table_ref[pl.ds(start, GROUP), :]
    for i in range(GROUP):
        facts = group_facts[i:i + 1, :]
        ups = []
        for s in range(SCALES):
            r = jnp.broadcast_to(facts[:, s:s + 1], (8, LANES))
            w = jnp.broadcast_to(facts[:, SCALES + s:SCALES + s + 1], (8, LANES))
            jump = jnp.exp(-8.0 * r)
            up, down = [w * jnp.exp(-r * up_steps)], [w * jnp.exp(-r * down_steps)]
            for _ in range(ROWS // 8 - 1):
                up.append(up[-1] * jump)
                down.insert(0, down[0] * jump)
            ups.append((jnp.concatenate(up, axis=0), jnp.concatenate(down, axis=0)))
        for b in range(PARTS):
            lanes = slice(b * LANES, (b + 1) * LANES)
            total = jnp.where(half == 0, z_refs[part // 2][part % 2 * GROUP + i, :, lanes],
                              z_refs[(3 + part) // 2][(3 + part) % 2 * GROUP + i, :, lanes])
            for s in range(SCALES):
                total = total + ups[s][0] * tables[s][i:i + 1, lanes] + ups[s][1] * tables[SCALES + s][i:i + 1, lanes]
            store(i, lanes, total)


def finish_own_kernel(table_ref, carry_ref, z0_ref, z1_ref, z2_ref, out_ref):
    for part in range(3):
        def store(i, lanes, value):
            out_ref[part * GROUP + i, :, lanes] = value

        add_carries(lat_index() & 1, table_ref, carry_ref, (z0_ref, z1_ref, z2_ref), part, store)


def finish_own(table, carry, parts):
    return pl.pallas_call(
        finish_own_kernel,
        in_specs=[VMEM] * 5,
        out_specs=VMEM,
        out_shape=jax.ShapeDtypeStruct((HALF, ROWS, COLS), F32),
        compiler_params=params(),
        cost_estimate=pl.CostEstimate(flops=1_000_000_000, bytes_accessed=2_000_000, transcendentals=0),
        name="finish_own",
    )(table, carry.reshape(2, SCALES, 3, GROUP, COLS), *parts)


def finish_kernel(table_ref, carry_ref, z0_ref, z1_ref, z2_ref, own_ref, out_ref, buf_ref, sem):
    half = 1 - (lat_index() & 1)
    ready = pltpu.make_async_copy(own_ref, out_ref.at[pl.ds((1 - half) * HALF, HALF)], sem.at[3])
    ready.start()
    copies = [ready]
    for part in range(3):
        def store(i, lanes, value):
            buf_ref[part, i, :, lanes] = value

        add_carries(half, table_ref, carry_ref, (z0_ref, z1_ref, z2_ref), part, store)
        there = out_ref.at[pl.ds((half * 3 + part) * GROUP, GROUP)]
        copies.append(pltpu.make_async_copy(buf_ref.at[part], there, sem.at[part]))
        copies[-1].start()
    for copy in copies:
        copy.wait()


def finish(table, carry, parts, own):
    return pl.pallas_call(
        finish_kernel,
        in_specs=[VMEM] * 6,
        out_specs=HBM,
        out_shape=jax.ShapeDtypeStruct((FIELDS, ROWS, COLS), F32),
        scratch_shapes=[pltpu.VMEM((3, GROUP, ROWS, COLS), F32), pltpu.SemaphoreType.DMA((4,))],
        compiler_params=params(),
        name="finish",
    )(table, carry.reshape(2, SCALES, 3, GROUP, COLS), *parts, own)


def partner(axis, count, bit):
    return functools.partial(lax.ppermute, axis_name=axis, perm=[(i, i ^ bit) for i in range(count)])


def shards(x, lengths, weights):
    facts = jnp.concatenate([lengths.T, weights.T], axis=0)
    sums, edge, table, lanes, held = row_sums(facts, x)
    got = [partner("lon", NLON, d)(sums) for d in (1, 2, 3)]
    early = local_filter(table, None, held, 32, 16, sums)
    part, half = lon_merge(lanes, sums, got, early)
    theirs = partner("lon", NLON, 4)(half)
    local = local_sums(table, held, part)
    steps = lat_steps(table, part)
    carry, keep, send = column_sums(table, lanes, part, theirs, edge, local)
    got_core = partner("lat", NLAT, 1)(send)
    chip = chip_merge(steps, keep, got_core)
    pair = partner("lat", NLAT, 2)(chip)
    z0 = local_filter(table, carry, held, 0, 16, chip)
    left, *sends = quad_merge(steps, chip, pair, z0)
    gs = [partner("lat", NLAT, 4 * d)(t) for d, t in zip((1, 2, 3), sends)]
    z1 = local_filter(table, carry, held, 16, 16, left)
    z2 = local_filter(table, carry, held, 32, 16, z1, early)
    own, other = lat_carry(steps, keep, got_core, pair, left, gs, z2)
    got_carry = partner("lat", NLAT, 1)(other)
    done = finish_own(table, own, (z0, z1, z2))
    return finish(table, got_carry, (z0, z1, z2), done)


def solution(mesh):
    in_specs = (P(None, "lat", "lon"), P(), P())
    out_specs = P(None, "lat", "lon")
    return jax.shard_map(shards, mesh=mesh, in_specs=in_specs, out_specs=out_specs, check_vma=False)
```

```python
import functools

import jax
import jax.numpy as jnp
from jax import lax
from jax.experimental import pallas as pl
from jax.experimental.pallas import tpu as pltpu
from jax.sharding import PartitionSpec as P

LEVELS = 8
SCALES = 3
WINDS = 16
FIELDS = 48
ROWS = 48
COLS = 384
GROUP = 8
GROUPS = FIELDS // GROUP
NLAT = 16
NLON = 8
LANES = 128
PARTS = COLS // LANES
HALF = FIELDS // 2
HALF_ROWS = SCALES * HALF
F32 = jnp.float32
BF16 = jnp.bfloat16

VMEM = pl.BlockSpec(memory_space=pltpu.VMEM)
BIG = 48 * 1024 * 1024
WHOLE = 50 * 1024 * 1024


def lat_index():
    return lax.axis_index("lat")


def lon_index():
    return lax.axis_index("lon")


def params(**kw):
    return pltpu.CompilerParams(vmem_limit_bytes=BIG, **kw)


def iota(shape, dim):
    return lax.broadcasted_iota(jnp.int32, shape, dim)


def fiota(shape, dim):
    return iota(shape, dim).astype(F32)


def split(value):
    high = value.astype(BF16)
    return high, (value - high.astype(F32)).astype(BF16)


def mm(a, b):
    return jnp.dot(a, b, preferred_element_type=F32)


def lane_fields(shape):
    lane = iota(shape, 1)
    virtual = lane & 31
    wind_field = ((virtual >> 4) << 3) + (virtual & 7)
    return lane, lane >> 5, virtual, wind_field, virtual + WINDS


def exact(a, b, dims):
    return lax.dot_general(a, b, (dims, ((), ())), precision=lax.Precision.HIGHEST, preferred_element_type=F32)


def lane_rates(rate):
    shape = (FIELDS, LANES)
    _, _, _, wind_field, rest_field = lane_fields(shape)
    field = iota(shape, 0)
    lane = iota((1, LANES), 1)

    def pick(which):
        every = exact(rate, jnp.where(field == which, 1.0, 0.0).astype(F32), ((1,), (0,)))
        value = jnp.where(lane < 32, every[0:1], jnp.where(lane < 64, every[1:2], every[2:3]))
        return jnp.where(lane < 96, value, 0.0)

    return pick(wind_field), pick(rest_field)


def scale_weights(rate, weights):
    decay = jnp.exp(-rate)
    leak = 1.0 - decay
    cube = (1.0 + decay) * (1.0 + decay) * (1.0 + decay)
    coefficient = weights * cube / (leak * (1.0 + decay * decay))
    kappa = leak / (1.0 + decay)
    return coefficient * kappa * kappa


def lane_kinds(shape):
    _, _, virtual, _, _ = lane_fields(shape)
    second = virtual >= 16
    north = (virtual & 15) >= 8
    zonal = second != north
    sign = jnp.where(second | north, -1.0, 1.0).astype(F32)
    return zonal, sign


def row_sums_kernel(len_ref, x_ref, sums_ref, edge_ref, table_ref, lanes_ref, held_ref, w_ref, sem):
    lon = lon_index()
    copies = []
    for k, (start, stop) in enumerate(((0, WINDS), (WINDS, FIELDS))):
        here = pl.ds(start, stop - start)
        copies.append(pltpu.make_async_copy(x_ref.at[here], held_ref.at[here], sem.at[k]))
        copies[-1].start()
    rate = 1.0 / len_ref[0:SCALES, :]
    pair = lane_rates(rate)
    lanes_ref[...] = jnp.concatenate([pair[0], pair[1], jnp.ones((6, LANES), F32)], axis=0)
    column = fiota((COLS, LANES), 0)
    for tile, rates in enumerate(pair):
        for side, steps in enumerate((COLS - 1 - column, column)):
            high, low = split(jnp.exp(-rates * steps))
            lanes = slice(side * LANES, (side + 1) * LANES)
            w_ref[tile, 0:COLS, lanes] = high
            w_ref[tile, COLS:2 * COLS, lanes] = high
            w_ref[tile, 2 * COLS:, lanes] = low
    both = jnp.concatenate([rate, scale_weights(rate, len_ref[SCALES:, :]), jnp.ones((2, FIELDS), F32)], axis=0)
    eye = jnp.where(iota((8, LANES), 0) == iota((8, LANES), 1), 1.0, 0.0).astype(F32)
    table_ref[...] = exact(both, eye, ((0,), (0,)))
    lane = iota((ROWS, LANES), 1)
    virtual = lane & 31
    zero = jnp.zeros((ROWS, LANES), F32)
    left, right, first, last = zero, zero, zero, zero
    for g in range(GROUPS):
        if g in (0, 2):
            copies[g // 2].wait()
        x = held_ref[g * GROUP:(g + 1) * GROUP].reshape(GROUP * ROWS, COLS)
        xh, xl = split(x)
        res = mm(jnp.concatenate([xh, xl, xh], axis=1), w_ref[0 if g < 2 else 1])
        if g == 2:
            left, right = zero, zero
        for i in range(GROUP):
            rows = slice(i * ROWS, (i + 1) * ROWS)
            mine = (virtual & 15) == g * GROUP + i if g < 2 else virtual == (g - 2) * GROUP + i
            left = jnp.where(mine, res[rows, 0:128], left)
            right = jnp.where(mine, res[rows, 128:256], right)
            if g < 2:
                first = jnp.where(mine, x[rows, 0:1], first)
                last = jnp.where(mine, x[rows, COLS - 1:COLS], last)
        if g == 1:
            edge = jnp.where(lon == 0, first, jnp.where(lon == NLON - 1, last, 0.0))
            sums_ref[:, 0:128] = jnp.where(lane >= 96, edge, left)
            sums_ref[:, 128:256] = right
            edge_ref[:, 0:128] = first
            edge_ref[:, 128:256] = last
    sums_ref[:, 256:384] = left
    sums_ref[:, 384:512] = right


HBM = pl.BlockSpec(memory_space=pltpu.HBM)
ANY = pl.BlockSpec(memory_space=pl.ANY)


def row_sums(facts, x):
    return pl.pallas_call(
        row_sums_kernel,
        in_specs=[VMEM, HBM],
        out_specs=[VMEM] * 5,
        out_shape=[jax.ShapeDtypeStruct((ROWS, 512), F32), jax.ShapeDtypeStruct((ROWS, 256), F32),
                   jax.ShapeDtypeStruct((FIELDS, LANES), F32), jax.ShapeDtypeStruct((8, LANES), F32),
                   jax.ShapeDtypeStruct((FIELDS, ROWS, COLS), F32)],
        scratch_shapes=[pltpu.VMEM((2, 3 * COLS, 256), BF16), pltpu.SemaphoreType.DMA((2,))],
        compiler_params=pltpu.CompilerParams(vmem_limit_bytes=WHOLE),
        name="row_sums",
    )(facts, x)


def zonal_difference(x):
    shape = x.shape
    axis = len(shape) - 1
    column = iota(shape, axis)
    ahead = jnp.where(column == COLS - 1, 0.0, pltpu.roll(x, COLS - 1, axis))
    behind = jnp.where(column == 0, 0.0, pltpu.roll(x, 1, axis))
    return 0.5 * (ahead - behind)


def column_piece_sums(table_ref, x_ref, groups):
    top = lat_index() == 0
    count = 2 * SCALES * GROUP
    shape = (count, LANES)
    out_row = iota(shape, 0)
    member = out_row & 7
    left_side = out_row < SCALES * GROUP
    lane = iota(shape, 1)
    source = jnp.where(lane >= ROWS, lane - ROWS, lane).astype(F32)
    used = lane < 2 * ROWS
    steps = jnp.where(left_side, ROWS - 1 - source, source)
    zeros = jnp.zeros((32, COLS), BF16)

    def weighted(matrix, x, i):
        mh, ml = split(jnp.where(used & (member == i), matrix, 0.0))
        xh, xl = split(x)
        return mm(jnp.concatenate([mh, ml[:, :ROWS]], axis=1), jnp.concatenate([xh, xl, zeros, xh], axis=0))

    def group_sums(group, wind):
        rate = table_ref[group * GROUP:(group + 1) * GROUP, :]
        row_rate = jnp.concatenate([rate[:, s:s + 1] for _ in range(2) for s in range(SCALES)], axis=0)
        wide = jnp.broadcast_to(row_rate, shape)
        plain = jnp.exp(-wide * steps)
        acc = jnp.zeros((count, COLS), F32)
        if wind:
            decay = jnp.exp(-wide)
            gain = 0.5 * (1.0 - decay * decay) / decay
            start = jnp.where(top & (source == 0.0), 0.5 * jnp.exp(-wide * ROWS), 0.0)
            slope = jnp.where(left_side, -gain * plain - start, gain * plain)
            second_sign = jnp.where(group == 0, 1.0, -1.0)
            for i in range(GROUP):
                acc += weighted(plain, -zonal_difference(x_ref[(1 - group) * GROUP + i]), i)
                acc += weighted(slope, second_sign * x_ref[group * GROUP + i], i)
        else:
            for i in range(GROUP):
                acc += weighted(plain, x_ref[group * GROUP + i], i)
        return acc, row_rate

    return [group_sums(group, group < 2) for group in groups]


def wind_sums_kernel(table_ref, x_ref, _, out_ref):
    made = column_piece_sums(table_ref, x_ref, (0, 1))
    out_ref[...] = jnp.concatenate([m[0] for m in made], axis=0)


def wind_sums(table, x, before):
    return pl.pallas_call(
        wind_sums_kernel,
        in_specs=[VMEM, VMEM, ANY],
        out_specs=VMEM,
        out_shape=jax.ShapeDtypeStruct((4 * SCALES * GROUP, COLS), F32),
        compiler_params=params(),
        cost_estimate=pl.CostEstimate(flops=300_000_000, bytes_accessed=1_000_000, transcendentals=0),
        name="wind_sums",
    )(table, x, before)


def local_sums_kernel(table_ref, x_ref, winds_ref, _, out_ref):
    count = 2 * SCALES * GROUP
    made = column_piece_sums(table_ref, x_ref, range(2, GROUPS))
    acc = jnp.concatenate([winds_ref[...]] + [m[0] for m in made], axis=0)
    factors = []
    for group in range(GROUPS):
        rate = table_ref[group * GROUP:(group + 1) * GROUP, :]
        row_rate = jnp.concatenate([rate[:, s:s + 1] for _ in range(2) for s in range(SCALES)], axis=0)
        factors.append(jnp.broadcast_to(jnp.exp(-row_rate), (count, LANES)))
    factor = jnp.concatenate(factors, axis=0)
    factor = jnp.concatenate([factor] * PARTS, axis=1)
    column = iota(acc.shape, 1)
    forward, backward = acc, acc
    step = 1
    while step < COLS:
        forward = forward + factor * jnp.where(column >= step, pltpu.roll(forward, step, 1), 0.0)
        backward = backward + factor * jnp.where(column < COLS - step, pltpu.roll(backward, COLS - step, 1), 0.0)
        factor = factor * factor
        step *= 2
    acc = forward + backward - acc
    for group in range(GROUPS):
        for side in range(2):
            for s in range(SCALES):
                k = group * count + (side * SCALES + s) * GROUP
                out_ref[group // 3, side, s, group % 3] = acc[k:k + GROUP]


def local_sums(table, x, winds, before):
    out = pl.pallas_call(
        local_sums_kernel,
        in_specs=[VMEM, VMEM, VMEM, ANY],
        out_specs=VMEM,
        out_shape=jax.ShapeDtypeStruct((2, 2, SCALES, 3, GROUP, COLS), F32),
        compiler_params=params(),
        cost_estimate=pl.CostEstimate(flops=600000000, bytes_accessed=4_000_000, transcendentals=0),
        name="local_sums",
    )(table, x, winds, before)
    return out.reshape(2, 2 * HALF_ROWS, COLS)


def lon_merge_kernel(lanes_ref, own_ref, g1_ref, g3_ref, g2_ref, _, part_ref, send_ref):
    y = lon_index() & 3
    high = lon_index() >= 4
    yf = y.astype(F32)
    zonal, _ = lane_kinds((1, LANES))
    lane = iota((1, LANES), 1)
    for tile in range(2):
        rate = lanes_ref[tile:tile + 1, :]
        step = lambda n: jnp.exp(-rate * (COLS * n))
        base = tile * 256
        lanes_l = slice(base, base + 128)
        lanes_r = slice(base + 128, base + 256)
        left_total = step(3.0 - yf) * own_ref[:, lanes_l]
        right_total = step(yf) * own_ref[:, lanes_r]
        left = jnp.zeros((ROWS, LANES), F32)
        right = jnp.zeros((ROWS, LANES), F32)
        for d, ref in ((1, g1_ref), (2, g2_ref), (3, g3_ref)):
            other = y ^ d
            of = other.astype(F32)
            below = other < y
            lg, rg = ref[:, lanes_l], ref[:, lanes_r]
            gap = jnp.abs(yf - of) - 1.0
            left = left + jnp.where(below, step(gap), 0.0) * lg
            right = right + jnp.where(below, 0.0, step(gap)) * rg
            left_total = left_total + step(3.0 - of) * lg
            right_total = right_total + step(of) * rg
        part_ref[:, lanes_l] = left
        part_ref[:, lanes_r] = right
        part_ref[:, 512 + tile * 128:640 + tile * 128] = left_total
        image = jnp.exp(-rate * (4.0 * COLS + 1.0))
        if tile == 0:
            image = jnp.where(zonal, -image, image)
            image = jnp.where(lane >= 96, -1.0, image)
            right_total = jnp.where(lane >= 96, 0.0, right_total)
        send_ref[:, tile * 128:tile * 128 + 128] = jnp.where(high, right_total - image * left_total, left_total)


def lon_merge(lanes, own, got, after):
    return pl.pallas_call(
        lon_merge_kernel,
        in_specs=[VMEM] * 5 + [ANY],
        out_specs=[VMEM, VMEM],
        out_shape=[jax.ShapeDtypeStruct((ROWS, 768), F32), jax.ShapeDtypeStruct((ROWS, 256), F32)],
        compiler_params=params(),
        name="lon_merge",
    )(lanes, own, got[0], got[2], got[1], after)


def spread_edges(tile):
    lane = iota(tile.shape, 1)
    out = tile
    for k in range(6):
        out = jnp.where((lane >> 4) == k, pltpu.roll(tile, (k * 16 + 32) % LANES, 1), out)
    return out


def column_sums_kernel(table_ref, lanes_ref, part_ref, theirs_ref, edge_ref, local_ref,
                       carry_ref, keep_ref, send_ref):
    lat, lon = lat_index(), lon_index()
    y = lon & 3
    yf = y.astype(F32)
    high = lon >= 4
    highf = jnp.where(high, 1.0, 0.0)
    lowf = 1.0 - highf
    lonf = lon.astype(F32)
    top = lat == 0
    rates = (lanes_ref[0:1, :], lanes_ref[1:2, :])
    zonal, sign = lane_kinds((1, LANES))
    row = fiota((ROWS, LANES), 0)
    weights = []
    for tile in range(2):
        rate = rates[tile]
        step = lambda n: jnp.exp(-rate * (COLS * n))
        decay = jnp.exp(-rate)
        theirs = theirs_ref[:, tile * 128:tile * 128 + 128]
        half = part_ref[:, 512 + tile * 128:640 + tile * 128]
        left = part_ref[:, tile * 256:tile * 256 + 128] + (highf * step(yf)) * theirs
        right = part_ref[:, tile * 256 + 128:tile * 256 + 256] + (lowf * step(3.0 - yf)) * theirs
        whole = (highf + lowf * step(4.0)) * half + (highf * step(4.0)) * theirs
        end = step(7.0 - lonf)
        weight_l = jnp.exp(-rate * (ROWS - 1 - row))
        weight_r = jnp.exp(-rate * row)
        carry_l = left
        carry_r = right - (end * decay) * whole
        if tile == 0:
            v0 = spread_edges(lowf * half + highf * theirs)
            vn = spread_edges(highf * half + lowf * theirs)
            gain = 0.5 * (1.0 - decay * decay) / decay
            initial = -0.5 * (v0 + vn / decay)
            zonal_l = step(lonf) * initial - gain * left + 0.5 * edge_ref[:, 0:128]
            zonal_r = (gain * right - 0.5 * edge_ref[:, 128:256]
                       + end * (gain * v0 - decay * (step(8.0) * initial - gain * whole)))
            carry_l = sign * jnp.where(zonal, zonal_l, carry_l)
            carry_r = sign * jnp.where(zonal, zonal_r, carry_r)
            start = jnp.where(top & (row == 0.0), 0.5 * jnp.exp(-rate * ROWS), 0.0)
            weight_l = jnp.where(zonal, weight_l, -gain * weight_l - start)
            weight_r = jnp.where(zonal, weight_r, gain * weight_r)
        carry_ref[:, tile * 256:tile * 256 + 128] = carry_l
        carry_ref[:, tile * 256 + 128:tile * 256 + 256] = carry_r
        fold = lambda w, c: jnp.sum(w * c, axis=0, keepdims=True)
        weights.append(((fold(weight_l, carry_l), fold(weight_l, carry_r)),
                        (fold(weight_r, carry_l), fold(weight_r, carry_r))))
    shape = (HALF_ROWS, LANES)
    lane, lane_scale, _, wind_field, rest_field = lane_fields(shape)
    out_row = iota(shape, 0)
    scale = jnp.where(out_row < HALF, 0, jnp.where(out_row < 2 * HALF, 1, 2))
    core = lat & 1
    column = fiota((HALF_ROWS, COLS), 1)
    for ref, half in ((send_ref, 1 - core), (keep_ref, core)):
        field = out_row - scale * HALF + half * HALF
        same = lane_scale == scale
        wind = same & (wind_field == field)
        rest = same & (rest_field == field)
        rate = table_ref[pl.ds(pl.multiple_of(half * HALF, 8), HALF), :]
        rate = jnp.concatenate([rate[:, s:s + 1] for s in range(SCALES)], axis=0)
        fall = jnp.exp(-rate * (column + 1.0))
        rise = jnp.exp(-rate * (COLS - column))
        for side in range(2):
            pick = lambda k: jnp.sum(
                jnp.where(wind, weights[0][side][k], 0.0) + jnp.where(rest, weights[1][side][k], 0.0),
                axis=1, keepdims=True)
            rows = slice(side * HALF_ROWS, (side + 1) * HALF_ROWS)
            ref[rows, :] = local_ref[half, rows, :] + pick(0) * fall + pick(1) * rise


def column_sums(table, lanes, part, theirs, edge, local):
    half = jax.ShapeDtypeStruct((2 * HALF_ROWS, COLS), F32)
    return pl.pallas_call(
        column_sums_kernel,
        in_specs=[VMEM] * 6,
        out_specs=[VMEM] * 3,
        out_shape=[jax.ShapeDtypeStruct((ROWS, 512), F32), half, half],
        compiler_params=params(),
        name="column_sums",
    )(table, lanes, part, theirs, edge, local)


LEFT = slice(0, HALF_ROWS)
RIGHT = slice(HALF_ROWS, 2 * HALF_ROWS)
STEPS = 21


def steps_kernel(table_ref, _, out_ref):
    lat = lat_index()
    odd = (lat & 1) == 1
    odd_chip = ((lat >> 1) & 1) == 1
    z = lat >> 2
    zf = z.astype(F32)
    rate = table_ref[pl.ds(pl.multiple_of((lat & 1) * HALF, 8), HALF), :]
    rate = jnp.concatenate([rate[:, s:s + 1] for s in range(SCALES)], axis=0)
    rate = jnp.broadcast_to(rate, (HALF_ROWS, LANES))
    power = lambda n: jnp.exp(-rate * n)
    quad = lambda n: power(4.0 * ROWS * n)
    one, zero = jnp.ones_like(rate), jnp.zeros_like(rate)
    device, chip = power(1.0 * ROWS), power(2.0 * ROWS)
    out = [jnp.where(odd, one, device), jnp.where(odd, device, one)]
    out += [jnp.where(odd_chip, one, chip), jnp.where(odd_chip, chip, one)]
    out += [power(1.0 + 4 * ROWS * jnp.maximum(7.0 - 2.0 * zf, 1.0))]
    for d in (1, 2, 3):
        other = z ^ d
        of = other.astype(F32)
        below = other < z
        gap = quad(jnp.abs(zf - of) - 1.0)
        out += [jnp.where(below, gap, zero), jnp.where(below, zero, gap), jnp.where(below, quad(3.0 - of), zero)]
    out += [quad(3.0 - zf), quad(3.0 - zf) * power(1.0)]
    out += [jnp.where(odd_chip, chip, one), jnp.where(odd_chip, one, zero)]
    out += [jnp.where(odd_chip, one, chip), jnp.where(odd_chip, zero, one)]
    out += [device]
    for k, value in enumerate(out):
        out_ref[k] = value


def lat_steps(table, before):
    return pl.pallas_call(
        steps_kernel,
        in_specs=[VMEM, ANY],
        out_specs=VMEM,
        out_shape=jax.ShapeDtypeStruct((STEPS, HALF_ROWS, LANES), F32),
        compiler_params=params(),
        name="lat_steps",
    )(table, before)


def by_tile(body):
    for b in range(PARTS):
        body(slice(b * LANES, (b + 1) * LANES))


def chip_merge_kernel(steps_ref, keep_ref, got_ref, chip_ref):
    def body(lanes):
        mine, other = steps_ref[0], steps_ref[1]
        chip_ref[LEFT, lanes] = mine * keep_ref[LEFT, lanes] + other * got_ref[LEFT, lanes]
        chip_ref[RIGHT, lanes] = other * keep_ref[RIGHT, lanes] + mine * got_ref[RIGHT, lanes]

    by_tile(body)


def chip_merge(steps, keep, got):
    return pl.pallas_call(
        chip_merge_kernel,
        in_specs=[VMEM] * 3,
        out_specs=VMEM,
        out_shape=jax.ShapeDtypeStruct((2 * HALF_ROWS, COLS), F32),
        compiler_params=params(),
        name="chip_merge",
    )(steps, keep, got)


def quad_merge_kernel(steps_ref, chip_ref, pair_ref, _, left_ref, s1_ref, s2_ref, s3_ref):
    z = lat_index() >> 2

    def body(lanes):
        mine, other, image = steps_ref[2], steps_ref[3], steps_ref[4]
        left = mine * chip_ref[LEFT, lanes] + other * pair_ref[LEFT, lanes]
        right = other * chip_ref[RIGHT, lanes] + mine * pair_ref[RIGHT, lanes]
        back = right - image * left
        left_ref[:, lanes] = left
        for d, ref in ((1, s1_ref), (2, s2_ref), (3, s3_ref)):
            ref[:, lanes] = jnp.where((z ^ d) > z, left, back)

    by_tile(body)


def quad_merge(steps, chip, pair, after):
    one = jax.ShapeDtypeStruct((HALF_ROWS, COLS), F32)
    return pl.pallas_call(
        quad_merge_kernel,
        in_specs=[VMEM] * 3 + [ANY],
        out_specs=[VMEM] * 4,
        out_shape=[one] * 4,
        compiler_params=params(),
        name="quad_merge",
    )(steps, chip, pair, after)


def lat_carry_kernel(steps_ref, keep_ref, got_ref, pair_ref, left_ref, g2_ref, g1_ref, g3_ref, _,
                     own_ref, send_ref):
    odd = (lat_index() & 1) == 1

    def body(lanes):
        left, right, whole = 0.0, 0.0, steps_ref[14] * left_ref[:, lanes]
        for k, ref in ((5, g1_ref), (8, g2_ref), (11, g3_ref)):
            g = ref[:, lanes]
            left = left + steps_ref[k] * g
            right = right + steps_ref[k + 1] * g
            whole = whole + steps_ref[k + 2] * g
        right = right - steps_ref[15] * whole
        left = steps_ref[16] * left + steps_ref[17] * pair_ref[LEFT, lanes]
        right = steps_ref[18] * right + steps_ref[19] * pair_ref[RIGHT, lanes]
        low_left = jnp.where(odd, got_ref[LEFT, lanes], keep_ref[LEFT, lanes])
        high_right = jnp.where(odd, keep_ref[RIGHT, lanes], got_ref[RIGHT, lanes])
        high_l = low_left + steps_ref[20] * left
        low_r = high_right + steps_ref[20] * right
        own_ref[LEFT, lanes] = jnp.where(odd, high_l, left)
        own_ref[RIGHT, lanes] = jnp.where(odd, right, low_r)
        send_ref[LEFT, lanes] = jnp.where(odd, left, high_l)
        send_ref[RIGHT, lanes] = jnp.where(odd, low_r, right)

    by_tile(body)


def lat_carry(steps, keep, got, pair, left, gs, after):
    half = jax.ShapeDtypeStruct((2 * HALF_ROWS, COLS), F32)
    return pl.pallas_call(
        lat_carry_kernel,
        in_specs=[VMEM] * 8 + [ANY],
        out_specs=[VMEM] * 2,
        out_shape=[half, half],
        compiler_params=params(),
        name="lat_carry",
    )(steps, keep, got, pair, left, gs[1], gs[0], gs[2], after)


def local_filter_kernel(starts, use_x, use_carry, table_ref, carry_ref, x_ref, base_ref, out_ref):
    top = lat_index() == 0
    shape = (ROWS, LANES)
    row = fiota(shape, 0)
    lane = iota(shape, 1)
    source = jnp.where(lane >= ROWS, lane - ROWS, lane).astype(F32)
    used = lane < 2 * ROWS
    gap = jnp.abs(row - source)
    gap_low = jnp.abs(source - 1.0 - row)
    gap_high = jnp.abs(source + 1.0 - row)
    first = source == 0.0
    spread = jnp.abs(fiota((LANES, LANES), 0) - fiota((LANES, LANES), 1))
    tag = lane & 31
    corner = jnp.zeros((LANES, LANES), BF16)
    left_lane = (lane == LANES - 1) | (lane == 1) | (lane == 3)
    flat = lane[:1]
    row_scale = jnp.where((flat == LANES - 1) | (flat == 0), 0, jnp.where(flat <= 2, 1, 2))
    base = iota((8, LANES), 0)
    column = fiota((8, LANES), 1)

    def carry_tile(tile, virtual):
        left = carry_ref[:, tile * 256:tile * 256 + 128]
        right = carry_ref[:, tile * 256 + 128:tile * 256 + 256]
        left = pltpu.roll(left, (LANES - virtual) % LANES, 1)
        right = pltpu.roll(right, (LANES + 1 - virtual) % LANES, 1)
        return jnp.where(tag == 0, left, jnp.where(tag == 1, right, 0.0))

    def column_pass(matrices, x, carry):
        parts = [split(jnp.where(used, m, 0.0)) for m in matrices]
        lhs = jnp.concatenate([jnp.concatenate([mh, ml[:, :ROWS]], axis=1) for mh, ml in parts], axis=0)
        wide = [t for t in (x, carry) if t is not None]
        wide = wide[0] if len(wide) == 1 else jnp.concatenate(wide, axis=1)
        xh, xl = split(wide)
        rhs = jnp.concatenate([xh, xl, jnp.zeros((32, wide.shape[1]), BF16), xh], axis=0)
        return mm(lhs, rhs)

    def column_stage(f, wind):
        facts = table_ref[pl.ds(f, 1), :]
        rates = [facts[:, s:s + 1] for s in range(SCALES)]
        gains = [facts[:, SCALES + s:SCALES + s + 1] for s in range(SCALES)]
        plain = [gains[s] * jnp.exp(-rates[s] * gap) for s in range(SCALES)]
        if wind:
            slopes = []
            for s in range(SCALES):
                slope = jnp.exp(-rates[s] * gap_low) - jnp.exp(-rates[s] * gap_high)
                slope = slope - jnp.where(top & first, jnp.exp(-rates[s] * (row + 1.0)), 0.0)
                slopes.append((0.5 * gains[s]) * slope)
            stream = f < GROUP
            second_sign = 1.0 if stream else -1.0
            meridional = f if stream else f + 16
            zonal = f + 8
            pair = f + 8 if stream else f - 8
            w = column_pass(plain, -zonal_difference(x_ref[pair]), carry_tile(0, zonal))
            w = w + column_pass(slopes, second_sign * x_ref[f], carry_tile(0, meridional))
        else:
            w = column_pass(plain, x_ref[f] if use_x else None, carry_tile(1, f - WINDS) if use_carry else None)
        return rates, w

    def row_stage(rates, w):
        outs = []
        for s in range(SCALES):
            rows = slice(s * ROWS, (s + 1) * ROWS)
            stack = jnp.concatenate([w[rows, b * LANES:(b + 1) * LANES] for b in range(PARTS)], axis=0)
            wh, wl = split(stack)
            th, tl = split(jnp.exp(-rates[s] * spread))
            lhs = jnp.concatenate([wh, wl], axis=1)
            rhs = jnp.concatenate([jnp.concatenate([th, tl], axis=1), jnp.concatenate([th, corner], axis=1)], axis=0)
            out = mm(lhs, rhs)
            outs.append(out[:, :LANES] + out[:, LANES:])
        return outs

    def carry_stage(rates, w, outs):
        sums, outer = None, jnp.zeros((ROWS, LANES), F32)
        for s in range(SCALES):
            here = row_scale == s
            if use_carry:
                moved = pltpu.roll(w[s * ROWS:(s + 1) * ROWS, w.shape[1] - LANES:], LANES - 30 * s - 1, 1)
                outer = moved if s == 0 else jnp.where(here, moved, outer)
            if use_x:
                turned = outs[s] if s == 0 else pltpu.roll(outs[s], 2 * s, 1)
                sums = turned if s == 0 else jnp.where(here, turned, sums)
        rate_row = jnp.where(row_scale == 0, rates[0], jnp.where(row_scale == 1, rates[1], rates[2]))
        jump = jnp.exp(-rate_row * LANES)
        from_left, from_right = [outer], [outer]
        for b in range(PARTS - 1):
            ahead, behind = jump * from_left[-1], jump * from_right[-1]
            if use_x:
                ahead = ahead + sums[b * ROWS:(b + 1) * ROWS]
                behind = behind + sums[(PARTS - 1 - b) * ROWS:(PARTS - b) * ROWS]
            from_left.append(ahead)
            from_right.append(behind)
        carries = [jnp.where(left_lane, from_left[b], from_right[PARTS - 1 - b]) for b in range(PARTS)]
        ch, cl = split(jnp.concatenate(carries, axis=0))
        low_rate = jnp.where(base == 0, rates[0], jnp.where(base <= 2, rates[1], rates[2]))
        low_left = (base == 1) | (base == 3)
        low = jnp.where(base <= 4, jnp.exp(-low_rate * jnp.where(low_left, column + 1.0, LANES - column)), 0.0)
        high = jnp.where(base == 7, jnp.exp(-rates[0] * (column + 1.0)), 0.0)
        pad = jnp.zeros((8, LANES), F32)
        lh, ll = split(jnp.concatenate([low, pad], axis=0))
        hh, hl = split(jnp.concatenate([pad, high], axis=0))
        gap_rows = jnp.zeros((96, LANES), BF16)
        bh = jnp.concatenate([lh, gap_rows, hh], axis=0)
        bl = jnp.concatenate([ll, gap_rows, hl], axis=0)
        rhs = jnp.concatenate([jnp.concatenate([bh, bl], axis=1), jnp.concatenate([bh, corner], axis=1)], axis=0)
        return jnp.concatenate([ch, cl], axis=1), rhs

    for start in starts:
        wind = start < WINDS
        fields = [start + i for i in range(GROUP)]
        columns = [column_stage(f, wind) for f in fields]
        outs = [row_stage(*c) if use_x else None for c in columns]
        ranks = [carry_stage(*c, o) for c, o in zip(columns, outs)]
        for f, o, (lhs, rhs) in zip(fields, outs, ranks):
            out = mm(lhs, rhs)
            total = out[:, :LANES] + out[:, LANES:]
            if use_x:
                total = (o[0] + o[1]) + (o[2] + total)
            for b in range(PARTS):
                lanes = slice(b * LANES, (b + 1) * LANES)
                part = total[b * ROWS:(b + 1) * ROWS]
                if base_ref is not None:
                    part = part + base_ref[f - starts[0], :, lanes]
                out_ref[f - starts[0], :, lanes] = part


def local_filter(table, carry, x, first, count, before, base=None):
    starts = tuple(range(first, first + count, GROUP))
    use_x, use_carry = base is None, carry is not None
    names = ["table"] + ["carry"] * use_carry + ["x"] * use_x + ["base"] * (base is not None) + ["before"]
    arrays = {"table": table, "carry": carry, "x": x, "base": base, "before": before}
    specs = {"before": ANY}

    def body(*refs):
        by_name = dict(zip(names, refs))
        local_filter_kernel(starts, use_x, use_carry, by_name["table"], by_name.get("carry"),
                            by_name.get("x"), by_name.get("base"), refs[len(names)])

    return pl.pallas_call(
        body,
        in_specs=[specs.get(n, VMEM) for n in names],
        out_specs=VMEM,
        out_shape=jax.ShapeDtypeStruct((count, ROWS, COLS), F32),
        compiler_params=params(),
        cost_estimate=pl.CostEstimate(flops=int(count * 30000000), bytes_accessed=count * 150_000, transcendentals=0),
        name="local_filter",
    )(*[arrays[n] for n in names])


def add_carries(half, table_ref, carry_ref, z_refs, part, store):
    row = fiota((8, LANES), 0)
    up_steps, down_steps = row + 1.0, 8.0 - row
    tables = [carry_ref[side, s, part] for side in range(2) for s in range(SCALES)]
    start = pl.multiple_of((half * 3 + part) * GROUP, GROUP)
    group_facts = table_ref[pl.ds(start, GROUP), :]
    for i in range(GROUP):
        facts = group_facts[i:i + 1, :]
        ups = []
        for s in range(SCALES):
            r = jnp.broadcast_to(facts[:, s:s + 1], (8, LANES))
            w = jnp.broadcast_to(facts[:, SCALES + s:SCALES + s + 1], (8, LANES))
            jump = jnp.exp(-8.0 * r)
            up, down = [w * jnp.exp(-r * up_steps)], [w * jnp.exp(-r * down_steps)]
            for _ in range(ROWS // 8 - 1):
                up.append(up[-1] * jump)
                down.insert(0, down[0] * jump)
            ups.append((jnp.concatenate(up, axis=0), jnp.concatenate(down, axis=0)))
        for b in range(PARTS):
            lanes = slice(b * LANES, (b + 1) * LANES)
            total = jnp.where(half == 0, z_refs[part // 2][part % 2 * GROUP + i, :, lanes],
                              z_refs[(3 + part) // 2][(3 + part) % 2 * GROUP + i, :, lanes])
            for s in range(SCALES):
                total = total + ups[s][0] * tables[s][i:i + 1, lanes] + ups[s][1] * tables[SCALES + s][i:i + 1, lanes]
            store(i, lanes, total)


def finish_own_kernel(table_ref, carry_ref, z0_ref, z1_ref, z2_ref, out_ref):
    for part in range(3):
        def store(i, lanes, value):
            out_ref[part * GROUP + i, :, lanes] = value

        add_carries(lat_index() & 1, table_ref, carry_ref, (z0_ref, z1_ref, z2_ref), part, store)


def finish_own(table, carry, parts):
    return pl.pallas_call(
        finish_own_kernel,
        in_specs=[VMEM] * 5,
        out_specs=VMEM,
        out_shape=jax.ShapeDtypeStruct((HALF, ROWS, COLS), F32),
        compiler_params=params(),
        cost_estimate=pl.CostEstimate(flops=1_000_000_000, bytes_accessed=2_000_000, transcendentals=0),
        name="finish_own",
    )(table, carry.reshape(2, SCALES, 3, GROUP, COLS), *parts)


def finish_kernel(table_ref, carry_ref, z0_ref, z1_ref, z2_ref, own_ref, out_ref, buf_ref, sem):
    half = 1 - (lat_index() & 1)
    ready = pltpu.make_async_copy(own_ref, out_ref.at[pl.ds((1 - half) * HALF, HALF)], sem.at[3])
    ready.start()
    copies = [ready]
    for part in range(3):
        def store(i, lanes, value):
            buf_ref[part, i, :, lanes] = value

        add_carries(half, table_ref, carry_ref, (z0_ref, z1_ref, z2_ref), part, store)
        there = out_ref.at[pl.ds((half * 3 + part) * GROUP, GROUP)]
        copies.append(pltpu.make_async_copy(buf_ref.at[part], there, sem.at[part]))
        copies[-1].start()
    for copy in copies:
        copy.wait()


def finish(table, carry, parts, own):
    return pl.pallas_call(
        finish_kernel,
        in_specs=[VMEM] * 6,
        out_specs=HBM,
        out_shape=jax.ShapeDtypeStruct((FIELDS, ROWS, COLS), F32),
        scratch_shapes=[pltpu.VMEM((3, GROUP, ROWS, COLS), F32), pltpu.SemaphoreType.DMA((4,))],
        compiler_params=params(),
        name="finish",
    )(table, carry.reshape(2, SCALES, 3, GROUP, COLS), *parts, own)


def partner(axis, count, bit):
    return functools.partial(lax.ppermute, axis_name=axis, perm=[(i, i ^ bit) for i in range(count)])


def shards(x, lengths, weights):
    facts = jnp.concatenate([lengths.T, weights.T], axis=0)
    sums, edge, table, lanes, held = row_sums(facts, x)
    got = [partner("lon", NLON, d)(sums) for d in (1, 2, 3)]
    early = local_filter(table, None, held, 32, 16, sums)
    winds = wind_sums(table, held, early)
    part, half = lon_merge(lanes, sums, got, winds)
    theirs = partner("lon", NLON, 4)(half)
    local = local_sums(table, held, winds, part)
    steps = lat_steps(table, part)
    carry, keep, send = column_sums(table, lanes, part, theirs, edge, local)
    got_core = partner("lat", NLAT, 1)(send)
    chip = chip_merge(steps, keep, got_core)
    pair = partner("lat", NLAT, 2)(chip)
    z2 = local_filter(table, carry, held, 32, 16, chip, early)
    z0 = local_filter(table, carry, held, 0, 16, z2)
    left, *sends = quad_merge(steps, chip, pair, z0)
    gs = [partner("lat", NLAT, 4 * d)(t) for d, t in zip((1, 2, 3), sends)]
    z1 = local_filter(table, carry, held, 16, 16, left)
    own, other = lat_carry(steps, keep, got_core, pair, left, gs, z1)
    got_carry = partner("lat", NLAT, 1)(other)
    done = finish_own(table, own, (z0, z1, z2))
    return finish(table, got_carry, (z0, z1, z2), done)


def solution(mesh):
    in_specs = (P(None, "lat", "lon"), P(), P())
    out_specs = P(None, "lat", "lon")
    return jax.shard_map(shards, mesh=mesh, in_specs=in_specs, out_specs=out_specs, check_vma=False)
```

```python
import functools

import jax
import jax.numpy as jnp
from jax import lax
from jax.experimental import pallas as pl
from jax.experimental.pallas import tpu as pltpu
from jax.sharding import PartitionSpec as P

LEVELS = 8
SCALES = 3
WINDS = 16
FIELDS = 48
ROWS = 48
COLS = 384
GROUP = 8
GROUPS = FIELDS // GROUP
NLAT = 16
NLON = 8
LANES = 128
PARTS = COLS // LANES
HALF = FIELDS // 2
HALF_ROWS = SCALES * HALF
F32 = jnp.float32
BF16 = jnp.bfloat16

VMEM = pl.BlockSpec(memory_space=pltpu.VMEM)
BIG = 48 * 1024 * 1024
WHOLE = 50 * 1024 * 1024


def lat_index():
    return lax.axis_index("lat")


def lon_index():
    return lax.axis_index("lon")


def params(**kw):
    return pltpu.CompilerParams(vmem_limit_bytes=BIG, **kw)


def iota(shape, dim):
    return lax.broadcasted_iota(jnp.int32, shape, dim)


def fiota(shape, dim):
    return iota(shape, dim).astype(F32)


def split(value):
    high = value.astype(BF16)
    return high, (value - high.astype(F32)).astype(BF16)


def mm(a, b):
    return jnp.dot(a, b, preferred_element_type=F32)


def lane_fields(shape):
    lane = iota(shape, 1)
    virtual = lane & 31
    wind_field = ((virtual >> 4) << 3) + (virtual & 7)
    return lane, lane >> 5, virtual, wind_field, virtual + WINDS


def exact(a, b, dims):
    return lax.dot_general(a, b, (dims, ((), ())), precision=lax.Precision.HIGHEST, preferred_element_type=F32)


def lane_rates(rate):
    shape = (FIELDS, LANES)
    _, _, _, wind_field, rest_field = lane_fields(shape)
    field = iota(shape, 0)
    lane = iota((1, LANES), 1)

    def pick(which):
        every = exact(rate, jnp.where(field == which, 1.0, 0.0).astype(F32), ((1,), (0,)))
        value = jnp.where(lane < 32, every[0:1], jnp.where(lane < 64, every[1:2], every[2:3]))
        return jnp.where(lane < 96, value, 0.0)

    return pick(wind_field), pick(rest_field)


def scale_weights(rate, weights):
    decay = jnp.exp(-rate)
    leak = 1.0 - decay
    cube = (1.0 + decay) * (1.0 + decay) * (1.0 + decay)
    coefficient = weights * cube / (leak * (1.0 + decay * decay))
    kappa = leak / (1.0 + decay)
    return coefficient * kappa * kappa


def lane_kinds(shape):
    _, _, virtual, _, _ = lane_fields(shape)
    second = virtual >= 16
    north = (virtual & 15) >= 8
    zonal = second != north
    sign = jnp.where(second | north, -1.0, 1.0).astype(F32)
    return zonal, sign


def row_sums_kernel(len_ref, x_ref, sums_ref, edge_ref, table_ref, lanes_ref, held_ref, w_ref, sem):
    lon = lon_index()
    copies = []
    for k, (start, stop) in enumerate(((0, WINDS), (WINDS, FIELDS))):
        here = pl.ds(start, stop - start)
        copies.append(pltpu.make_async_copy(x_ref.at[here], held_ref.at[here], sem.at[k]))
        copies[-1].start()
    rate = 1.0 / len_ref[0:SCALES, :]
    pair = lane_rates(rate)
    lanes_ref[...] = jnp.concatenate([pair[0], pair[1], jnp.ones((6, LANES), F32)], axis=0)
    column = fiota((COLS, LANES), 0)
    for tile, rates in enumerate(pair):
        for side, steps in enumerate((COLS - 1 - column, column)):
            high, low = split(jnp.exp(-rates * steps))
            lanes = slice(side * LANES, (side + 1) * LANES)
            w_ref[tile, 0:COLS, lanes] = high
            w_ref[tile, COLS:2 * COLS, lanes] = high
            w_ref[tile, 2 * COLS:, lanes] = low
    both = jnp.concatenate([rate, scale_weights(rate, len_ref[SCALES:, :]), jnp.ones((2, FIELDS), F32)], axis=0)
    eye = jnp.where(iota((8, LANES), 0) == iota((8, LANES), 1), 1.0, 0.0).astype(F32)
    table_ref[...] = exact(both, eye, ((0,), (0,)))
    lane = iota((ROWS, LANES), 1)
    virtual = lane & 31
    zero = jnp.zeros((ROWS, LANES), F32)
    left, right, first, last = zero, zero, zero, zero
    for g in range(GROUPS):
        if g in (0, 2):
            copies[g // 2].wait()
        x = held_ref[g * GROUP:(g + 1) * GROUP].reshape(GROUP * ROWS, COLS)
        xh, xl = split(x)
        res = mm(jnp.concatenate([xh, xl, xh], axis=1), w_ref[0 if g < 2 else 1])
        if g == 2:
            left, right = zero, zero
        for i in range(GROUP):
            rows = slice(i * ROWS, (i + 1) * ROWS)
            mine = (virtual & 15) == g * GROUP + i if g < 2 else virtual == (g - 2) * GROUP + i
            left = jnp.where(mine, res[rows, 0:128], left)
            right = jnp.where(mine, res[rows, 128:256], right)
            if g < 2:
                first = jnp.where(mine, x[rows, 0:1], first)
                last = jnp.where(mine, x[rows, COLS - 1:COLS], last)
        if g == 1:
            edge = jnp.where(lon == 0, first, jnp.where(lon == NLON - 1, last, 0.0))
            sums_ref[:, 0:128] = jnp.where(lane >= 96, edge, left)
            sums_ref[:, 128:256] = right
            edge_ref[:, 0:128] = first
            edge_ref[:, 128:256] = last
    sums_ref[:, 256:384] = left
    sums_ref[:, 384:512] = right


HBM = pl.BlockSpec(memory_space=pltpu.HBM)
ANY = pl.BlockSpec(memory_space=pl.ANY)


def row_sums(facts, x):
    return pl.pallas_call(
        row_sums_kernel,
        in_specs=[VMEM, HBM],
        out_specs=[VMEM] * 5,
        out_shape=[jax.ShapeDtypeStruct((ROWS, 512), F32), jax.ShapeDtypeStruct((ROWS, 256), F32),
                   jax.ShapeDtypeStruct((FIELDS, LANES), F32), jax.ShapeDtypeStruct((8, LANES), F32),
                   jax.ShapeDtypeStruct((FIELDS, ROWS, COLS), F32)],
        scratch_shapes=[pltpu.VMEM((2, 3 * COLS, 256), BF16), pltpu.SemaphoreType.DMA((2,))],
        compiler_params=pltpu.CompilerParams(vmem_limit_bytes=WHOLE),
        name="row_sums",
    )(facts, x)


def zonal_difference(x):
    shape = x.shape
    axis = len(shape) - 1
    column = iota(shape, axis)
    ahead = jnp.where(column == COLS - 1, 0.0, pltpu.roll(x, COLS - 1, axis))
    behind = jnp.where(column == 0, 0.0, pltpu.roll(x, 1, axis))
    return 0.5 * (ahead - behind)


def column_piece_sums(table_ref, x_ref, groups):
    top = lat_index() == 0
    count = 2 * SCALES * GROUP
    shape = (count, LANES)
    out_row = iota(shape, 0)
    member = out_row & 7
    left_side = out_row < SCALES * GROUP
    lane = iota(shape, 1)
    source = jnp.where(lane >= ROWS, lane - ROWS, lane).astype(F32)
    used = lane < 2 * ROWS
    steps = jnp.where(left_side, ROWS - 1 - source, source)
    zeros = jnp.zeros((32, COLS), BF16)

    def weighted(matrix, x, i):
        mh, ml = split(jnp.where(used & (member == i), matrix, 0.0))
        xh, xl = split(x)
        return mm(jnp.concatenate([mh, ml[:, :ROWS]], axis=1), jnp.concatenate([xh, xl, zeros, xh], axis=0))

    def group_sums(group, wind):
        rate = table_ref[group * GROUP:(group + 1) * GROUP, :]
        row_rate = jnp.concatenate([rate[:, s:s + 1] for _ in range(2) for s in range(SCALES)], axis=0)
        wide = jnp.broadcast_to(row_rate, shape)
        plain = jnp.exp(-wide * steps)
        acc = jnp.zeros((count, COLS), F32)
        if wind:
            decay = jnp.exp(-wide)
            gain = 0.5 * (1.0 - decay * decay) / decay
            start = jnp.where(top & (source == 0.0), 0.5 * jnp.exp(-wide * ROWS), 0.0)
            slope = jnp.where(left_side, -gain * plain - start, gain * plain)
            second_sign = jnp.where(group == 0, 1.0, -1.0)
            for i in range(GROUP):
                acc += weighted(plain, -zonal_difference(x_ref[(1 - group) * GROUP + i]), i)
                acc += weighted(slope, second_sign * x_ref[group * GROUP + i], i)
        else:
            for i in range(GROUP):
                acc += weighted(plain, x_ref[group * GROUP + i], i)
        return acc, row_rate

    return [group_sums(group, group < 2) for group in groups]


def wind_sums_kernel(table_ref, x_ref, _, out_ref):
    made = column_piece_sums(table_ref, x_ref, (0, 1))
    out_ref[...] = jnp.concatenate([m[0] for m in made], axis=0)


def wind_sums(table, x, before):
    return pl.pallas_call(
        wind_sums_kernel,
        in_specs=[VMEM, VMEM, ANY],
        out_specs=VMEM,
        out_shape=jax.ShapeDtypeStruct((4 * SCALES * GROUP, COLS), F32),
        compiler_params=params(),
        cost_estimate=pl.CostEstimate(flops=300_000_000, bytes_accessed=1_000_000, transcendentals=0),
        name="wind_sums",
    )(table, x, before)


def local_sums_kernel(table_ref, x_ref, winds_ref, _, out_ref):
    count = 2 * SCALES * GROUP
    made = column_piece_sums(table_ref, x_ref, range(2, GROUPS))
    acc = jnp.concatenate([winds_ref[...]] + [m[0] for m in made], axis=0)
    factors = []
    for group in range(GROUPS):
        rate = table_ref[group * GROUP:(group + 1) * GROUP, :]
        row_rate = jnp.concatenate([rate[:, s:s + 1] for _ in range(2) for s in range(SCALES)], axis=0)
        factors.append(jnp.broadcast_to(jnp.exp(-row_rate), (count, LANES)))
    factor = jnp.concatenate(factors, axis=0)
    factor = jnp.concatenate([factor] * PARTS, axis=1)
    column = iota(acc.shape, 1)
    forward, backward = acc, acc
    step = 1
    while step < COLS:
        forward = forward + factor * jnp.where(column >= step, pltpu.roll(forward, step, 1), 0.0)
        backward = backward + factor * jnp.where(column < COLS - step, pltpu.roll(backward, COLS - step, 1), 0.0)
        factor = factor * factor
        step *= 2
    acc = forward + backward - acc
    for group in range(GROUPS):
        for side in range(2):
            for s in range(SCALES):
                k = group * count + (side * SCALES + s) * GROUP
                out_ref[group // 3, side, s, group % 3] = acc[k:k + GROUP]


def local_sums(table, x, winds, before):
    out = pl.pallas_call(
        local_sums_kernel,
        in_specs=[VMEM, VMEM, VMEM, ANY],
        out_specs=VMEM,
        out_shape=jax.ShapeDtypeStruct((2, 2, SCALES, 3, GROUP, COLS), F32),
        compiler_params=params(),
        cost_estimate=pl.CostEstimate(flops=600000000, bytes_accessed=4_000_000, transcendentals=0),
        name="local_sums",
    )(table, x, winds, before)
    return out.reshape(2, 2 * HALF_ROWS, COLS)


def lon_merge_kernel(lanes_ref, own_ref, g1_ref, g3_ref, g2_ref, _, part_ref, send_ref):
    y = lon_index() & 3
    high = lon_index() >= 4
    yf = y.astype(F32)
    zonal, _ = lane_kinds((1, LANES))
    lane = iota((1, LANES), 1)
    for tile in range(2):
        rate = lanes_ref[tile:tile + 1, :]
        step = lambda n: jnp.exp(-rate * (COLS * n))
        base = tile * 256
        lanes_l = slice(base, base + 128)
        lanes_r = slice(base + 128, base + 256)
        left_total = step(3.0 - yf) * own_ref[:, lanes_l]
        right_total = step(yf) * own_ref[:, lanes_r]
        left = jnp.zeros((ROWS, LANES), F32)
        right = jnp.zeros((ROWS, LANES), F32)
        for d, ref in ((1, g1_ref), (2, g2_ref), (3, g3_ref)):
            other = y ^ d
            of = other.astype(F32)
            below = other < y
            lg, rg = ref[:, lanes_l], ref[:, lanes_r]
            gap = jnp.abs(yf - of) - 1.0
            left = left + jnp.where(below, step(gap), 0.0) * lg
            right = right + jnp.where(below, 0.0, step(gap)) * rg
            left_total = left_total + step(3.0 - of) * lg
            right_total = right_total + step(of) * rg
        part_ref[:, lanes_l] = left
        part_ref[:, lanes_r] = right
        part_ref[:, 512 + tile * 128:640 + tile * 128] = left_total
        image = jnp.exp(-rate * (4.0 * COLS + 1.0))
        if tile == 0:
            image = jnp.where(zonal, -image, image)
            image = jnp.where(lane >= 96, -1.0, image)
            right_total = jnp.where(lane >= 96, 0.0, right_total)
        send_ref[:, tile * 128:tile * 128 + 128] = jnp.where(high, right_total - image * left_total, left_total)


def lon_merge(lanes, own, got, after):
    return pl.pallas_call(
        lon_merge_kernel,
        in_specs=[VMEM] * 5 + [ANY],
        out_specs=[VMEM, VMEM],
        out_shape=[jax.ShapeDtypeStruct((ROWS, 768), F32), jax.ShapeDtypeStruct((ROWS, 256), F32)],
        compiler_params=params(),
        name="lon_merge",
    )(lanes, own, got[0], got[2], got[1], after)


def spread_edges(tile):
    lane = iota(tile.shape, 1)
    out = tile
    for k in range(6):
        out = jnp.where((lane >> 4) == k, pltpu.roll(tile, (k * 16 + 32) % LANES, 1), out)
    return out


def column_sums_kernel(table_ref, lanes_ref, part_ref, theirs_ref, edge_ref, local_ref,
                       carry_ref, keep_ref, send_ref):
    lat, lon = lat_index(), lon_index()
    y = lon & 3
    yf = y.astype(F32)
    high = lon >= 4
    highf = jnp.where(high, 1.0, 0.0)
    lowf = 1.0 - highf
    lonf = lon.astype(F32)
    top = lat == 0
    rates = (lanes_ref[0:1, :], lanes_ref[1:2, :])
    zonal, sign = lane_kinds((1, LANES))
    row = fiota((ROWS, LANES), 0)
    weights = []
    for tile in range(2):
        rate = rates[tile]
        step = lambda n: jnp.exp(-rate * (COLS * n))
        decay = jnp.exp(-rate)
        theirs = theirs_ref[:, tile * 128:tile * 128 + 128]
        half = part_ref[:, 512 + tile * 128:640 + tile * 128]
        left = part_ref[:, tile * 256:tile * 256 + 128] + (highf * step(yf)) * theirs
        right = part_ref[:, tile * 256 + 128:tile * 256 + 256] + (lowf * step(3.0 - yf)) * theirs
        whole = (highf + lowf * step(4.0)) * half + (highf * step(4.0)) * theirs
        end = step(7.0 - lonf)
        weight_l = jnp.exp(-rate * (ROWS - 1 - row))
        weight_r = jnp.exp(-rate * row)
        carry_l = left
        carry_r = right - (end * decay) * whole
        if tile == 0:
            v0 = spread_edges(lowf * half + highf * theirs)
            vn = spread_edges(highf * half + lowf * theirs)
            gain = 0.5 * (1.0 - decay * decay) / decay
            initial = -0.5 * (v0 + vn / decay)
            zonal_l = step(lonf) * initial - gain * left + 0.5 * edge_ref[:, 0:128]
            zonal_r = (gain * right - 0.5 * edge_ref[:, 128:256]
                       + end * (gain * v0 - decay * (step(8.0) * initial - gain * whole)))
            carry_l = sign * jnp.where(zonal, zonal_l, carry_l)
            carry_r = sign * jnp.where(zonal, zonal_r, carry_r)
            start = jnp.where(top & (row == 0.0), 0.5 * jnp.exp(-rate * ROWS), 0.0)
            weight_l = jnp.where(zonal, weight_l, -gain * weight_l - start)
            weight_r = jnp.where(zonal, weight_r, gain * weight_r)
        carry_ref[:, tile * 256:tile * 256 + 128] = carry_l
        carry_ref[:, tile * 256 + 128:tile * 256 + 256] = carry_r
        fold = lambda w, c: jnp.sum(w * c, axis=0, keepdims=True)
        weights.append(((fold(weight_l, carry_l), fold(weight_l, carry_r)),
                        (fold(weight_r, carry_l), fold(weight_r, carry_r))))
    shape = (HALF_ROWS, LANES)
    lane, lane_scale, _, wind_field, rest_field = lane_fields(shape)
    out_row = iota(shape, 0)
    scale = jnp.where(out_row < HALF, 0, jnp.where(out_row < 2 * HALF, 1, 2))
    core = lat & 1
    column = fiota((HALF_ROWS, COLS), 1)
    for ref, half in ((send_ref, 1 - core), (keep_ref, core)):
        field = out_row - scale * HALF + half * HALF
        same = lane_scale == scale
        wind = same & (wind_field == field)
        rest = same & (rest_field == field)
        rate = table_ref[pl.ds(pl.multiple_of(half * HALF, 8), HALF), :]
        rate = jnp.concatenate([rate[:, s:s + 1] for s in range(SCALES)], axis=0)
        fall = jnp.exp(-rate * (column + 1.0))
        rise = jnp.exp(-rate * (COLS - column))
        for side in range(2):
            pick = lambda k: jnp.sum(
                jnp.where(wind, weights[0][side][k], 0.0) + jnp.where(rest, weights[1][side][k], 0.0),
                axis=1, keepdims=True)
            rows = slice(side * HALF_ROWS, (side + 1) * HALF_ROWS)
            ref[rows, :] = local_ref[half, rows, :] + pick(0) * fall + pick(1) * rise


def column_sums(table, lanes, part, theirs, edge, local):
    half = jax.ShapeDtypeStruct((2 * HALF_ROWS, COLS), F32)
    return pl.pallas_call(
        column_sums_kernel,
        in_specs=[VMEM] * 6,
        out_specs=[VMEM] * 3,
        out_shape=[jax.ShapeDtypeStruct((ROWS, 512), F32), half, half],
        compiler_params=params(),
        name="column_sums",
    )(table, lanes, part, theirs, edge, local)


LEFT = slice(0, HALF_ROWS)
RIGHT = slice(HALF_ROWS, 2 * HALF_ROWS)
STEPS = 21


def steps_kernel(table_ref, _, out_ref):
    lat = lat_index()
    odd = (lat & 1) == 1
    odd_chip = ((lat >> 1) & 1) == 1
    z = lat >> 2
    zf = z.astype(F32)
    rate = table_ref[pl.ds(pl.multiple_of((lat & 1) * HALF, 8), HALF), :]
    rate = jnp.concatenate([rate[:, s:s + 1] for s in range(SCALES)], axis=0)
    rate = jnp.broadcast_to(rate, (HALF_ROWS, LANES))
    power = lambda n: jnp.exp(-rate * n)
    quad = lambda n: power(4.0 * ROWS * n)
    one, zero = jnp.ones_like(rate), jnp.zeros_like(rate)
    device, chip = power(1.0 * ROWS), power(2.0 * ROWS)
    out = [jnp.where(odd, one, device), jnp.where(odd, device, one)]
    out += [jnp.where(odd_chip, one, chip), jnp.where(odd_chip, chip, one)]
    out += [power(1.0 + 4 * ROWS * jnp.maximum(7.0 - 2.0 * zf, 1.0))]
    for d in (1, 2, 3):
        other = z ^ d
        of = other.astype(F32)
        below = other < z
        gap = quad(jnp.abs(zf - of) - 1.0)
        out += [jnp.where(below, gap, zero), jnp.where(below, zero, gap), jnp.where(below, quad(3.0 - of), zero)]
    out += [quad(3.0 - zf), quad(3.0 - zf) * power(1.0)]
    out += [jnp.where(odd_chip, chip, one), jnp.where(odd_chip, one, zero)]
    out += [jnp.where(odd_chip, one, chip), jnp.where(odd_chip, zero, one)]
    out += [device]
    for k, value in enumerate(out):
        out_ref[k] = value


def lat_steps(table, before):
    return pl.pallas_call(
        steps_kernel,
        in_specs=[VMEM, ANY],
        out_specs=VMEM,
        out_shape=jax.ShapeDtypeStruct((STEPS, HALF_ROWS, LANES), F32),
        compiler_params=params(),
        name="lat_steps",
    )(table, before)


def by_tile(body):
    for b in range(PARTS):
        body(slice(b * LANES, (b + 1) * LANES))


def chip_merge_kernel(steps_ref, keep_ref, got_ref, chip_ref):
    def body(lanes):
        mine, other = steps_ref[0], steps_ref[1]
        chip_ref[LEFT, lanes] = mine * keep_ref[LEFT, lanes] + other * got_ref[LEFT, lanes]
        chip_ref[RIGHT, lanes] = other * keep_ref[RIGHT, lanes] + mine * got_ref[RIGHT, lanes]

    by_tile(body)


def chip_merge(steps, keep, got):
    return pl.pallas_call(
        chip_merge_kernel,
        in_specs=[VMEM] * 3,
        out_specs=VMEM,
        out_shape=jax.ShapeDtypeStruct((2 * HALF_ROWS, COLS), F32),
        compiler_params=params(),
        name="chip_merge",
    )(steps, keep, got)


def quad_merge_kernel(steps_ref, chip_ref, pair_ref, _, left_ref, s1_ref, s2_ref, s3_ref):
    z = lat_index() >> 2

    def body(lanes):
        mine, other, image = steps_ref[2], steps_ref[3], steps_ref[4]
        left = mine * chip_ref[LEFT, lanes] + other * pair_ref[LEFT, lanes]
        right = other * chip_ref[RIGHT, lanes] + mine * pair_ref[RIGHT, lanes]
        back = right - image * left
        left_ref[:, lanes] = left
        for d, ref in ((1, s1_ref), (2, s2_ref), (3, s3_ref)):
            ref[:, lanes] = jnp.where((z ^ d) > z, left, back)

    by_tile(body)


def quad_merge(steps, chip, pair, after):
    one = jax.ShapeDtypeStruct((HALF_ROWS, COLS), F32)
    return pl.pallas_call(
        quad_merge_kernel,
        in_specs=[VMEM] * 3 + [ANY],
        out_specs=[VMEM] * 4,
        out_shape=[one] * 4,
        compiler_params=params(),
        name="quad_merge",
    )(steps, chip, pair, after)


def lat_carry_kernel(steps_ref, keep_ref, got_ref, pair_ref, left_ref, g2_ref, g1_ref, g3_ref, _,
                     own_ref, send_ref):
    odd = (lat_index() & 1) == 1

    def body(lanes):
        left, right, whole = 0.0, 0.0, steps_ref[14] * left_ref[:, lanes]
        for k, ref in ((5, g1_ref), (8, g2_ref), (11, g3_ref)):
            g = ref[:, lanes]
            left = left + steps_ref[k] * g
            right = right + steps_ref[k + 1] * g
            whole = whole + steps_ref[k + 2] * g
        right = right - steps_ref[15] * whole
        left = steps_ref[16] * left + steps_ref[17] * pair_ref[LEFT, lanes]
        right = steps_ref[18] * right + steps_ref[19] * pair_ref[RIGHT, lanes]
        low_left = jnp.where(odd, got_ref[LEFT, lanes], keep_ref[LEFT, lanes])
        high_right = jnp.where(odd, keep_ref[RIGHT, lanes], got_ref[RIGHT, lanes])
        high_l = low_left + steps_ref[20] * left
        low_r = high_right + steps_ref[20] * right
        own_ref[LEFT, lanes] = jnp.where(odd, high_l, left)
        own_ref[RIGHT, lanes] = jnp.where(odd, right, low_r)
        send_ref[LEFT, lanes] = jnp.where(odd, left, high_l)
        send_ref[RIGHT, lanes] = jnp.where(odd, low_r, right)

    by_tile(body)


def lat_carry(steps, keep, got, pair, left, gs, after):
    half = jax.ShapeDtypeStruct((2 * HALF_ROWS, COLS), F32)
    return pl.pallas_call(
        lat_carry_kernel,
        in_specs=[VMEM] * 8 + [ANY],
        out_specs=[VMEM] * 2,
        out_shape=[half, half],
        compiler_params=params(),
        name="lat_carry",
    )(steps, keep, got, pair, left, gs[1], gs[0], gs[2], after)


def local_filter_kernel(starts, use_x, use_carry, table_ref, carry_ref, x_ref, base_ref, out_ref):
    top = lat_index() == 0
    shape = (ROWS, LANES)
    row = fiota(shape, 0)
    lane = iota(shape, 1)
    source = jnp.where(lane >= ROWS, lane - ROWS, lane).astype(F32)
    used = lane < 2 * ROWS
    gap = jnp.abs(row - source)
    gap_low = jnp.abs(source - 1.0 - row)
    gap_high = jnp.abs(source + 1.0 - row)
    first = source == 0.0
    spread = jnp.abs(fiota((LANES, LANES), 0) - fiota((LANES, LANES), 1))
    tag = lane & 31
    corner = jnp.zeros((LANES, LANES), BF16)
    left_lane = (lane == LANES - 1) | (lane == 1) | (lane == 3)
    flat = lane[:1]
    row_scale = jnp.where((flat == LANES - 1) | (flat == 0), 0, jnp.where(flat <= 2, 1, 2))
    base = iota((8, LANES), 0)
    column = fiota((8, LANES), 1)

    def carry_tile(tile, virtual):
        left = carry_ref[:, tile * 256:tile * 256 + 128]
        right = carry_ref[:, tile * 256 + 128:tile * 256 + 256]
        left = pltpu.roll(left, (LANES - virtual) % LANES, 1)
        right = pltpu.roll(right, (LANES + 1 - virtual) % LANES, 1)
        return jnp.where(tag == 0, left, jnp.where(tag == 1, right, 0.0))

    def column_pass(matrices, x, carry):
        parts = [split(jnp.where(used, m, 0.0)) for m in matrices]
        lhs = jnp.concatenate([jnp.concatenate([mh, ml[:, :ROWS]], axis=1) for mh, ml in parts], axis=0)
        wide = [t for t in (x, carry) if t is not None]
        wide = wide[0] if len(wide) == 1 else jnp.concatenate(wide, axis=1)
        xh, xl = split(wide)
        rhs = jnp.concatenate([xh, xl, jnp.zeros((32, wide.shape[1]), BF16), xh], axis=0)
        return mm(lhs, rhs)

    def column_stage(f, wind):
        facts = table_ref[pl.ds(f, 1), :]
        rates = [facts[:, s:s + 1] for s in range(SCALES)]
        gains = [facts[:, SCALES + s:SCALES + s + 1] for s in range(SCALES)]
        plain = [gains[s] * jnp.exp(-rates[s] * gap) for s in range(SCALES)]
        if wind:
            slopes = []
            for s in range(SCALES):
                slope = jnp.exp(-rates[s] * gap_low) - jnp.exp(-rates[s] * gap_high)
                slope = slope - jnp.where(top & first, jnp.exp(-rates[s] * (row + 1.0)), 0.0)
                slopes.append((0.5 * gains[s]) * slope)
            stream = f < GROUP
            second_sign = 1.0 if stream else -1.0
            meridional = f if stream else f + 16
            zonal = f + 8
            pair = f + 8 if stream else f - 8
            w = column_pass(plain, -zonal_difference(x_ref[pair]), carry_tile(0, zonal))
            w = w + column_pass(slopes, second_sign * x_ref[f], carry_tile(0, meridional))
        else:
            w = column_pass(plain, x_ref[f] if use_x else None, carry_tile(1, f - WINDS) if use_carry else None)
        return rates, w

    def row_stage(rates, w):
        outs = []
        for s in range(SCALES):
            rows = slice(s * ROWS, (s + 1) * ROWS)
            stack = jnp.concatenate([w[rows, b * LANES:(b + 1) * LANES] for b in range(PARTS)], axis=0)
            wh, wl = split(stack)
            th, tl = split(jnp.exp(-rates[s] * spread))
            lhs = jnp.concatenate([wh, wl], axis=1)
            rhs = jnp.concatenate([jnp.concatenate([th, tl], axis=1), jnp.concatenate([th, corner], axis=1)], axis=0)
            out = mm(lhs, rhs)
            outs.append(out[:, :LANES] + out[:, LANES:])
        return outs

    def carry_stage(rates, w, outs):
        sums, outer = None, jnp.zeros((ROWS, LANES), F32)
        for s in range(SCALES):
            here = row_scale == s
            if use_carry:
                moved = pltpu.roll(w[s * ROWS:(s + 1) * ROWS, w.shape[1] - LANES:], LANES - 30 * s - 1, 1)
                outer = moved if s == 0 else jnp.where(here, moved, outer)
            if use_x:
                turned = outs[s] if s == 0 else pltpu.roll(outs[s], 2 * s, 1)
                sums = turned if s == 0 else jnp.where(here, turned, sums)
        rate_row = jnp.where(row_scale == 0, rates[0], jnp.where(row_scale == 1, rates[1], rates[2]))
        jump = jnp.exp(-rate_row * LANES)
        from_left, from_right = [outer], [outer]
        for b in range(PARTS - 1):
            ahead, behind = jump * from_left[-1], jump * from_right[-1]
            if use_x:
                ahead = ahead + sums[b * ROWS:(b + 1) * ROWS]
                behind = behind + sums[(PARTS - 1 - b) * ROWS:(PARTS - b) * ROWS]
            from_left.append(ahead)
            from_right.append(behind)
        carries = [jnp.where(left_lane, from_left[b], from_right[PARTS - 1 - b]) for b in range(PARTS)]
        ch, cl = split(jnp.concatenate(carries, axis=0))
        low_rate = jnp.where(base == 0, rates[0], jnp.where(base <= 2, rates[1], rates[2]))
        low_left = (base == 1) | (base == 3)
        low = jnp.where(base <= 4, jnp.exp(-low_rate * jnp.where(low_left, column + 1.0, LANES - column)), 0.0)
        high = jnp.where(base == 7, jnp.exp(-rates[0] * (column + 1.0)), 0.0)
        pad = jnp.zeros((8, LANES), F32)
        lh, ll = split(jnp.concatenate([low, pad], axis=0))
        hh, hl = split(jnp.concatenate([pad, high], axis=0))
        gap_rows = jnp.zeros((96, LANES), BF16)
        bh = jnp.concatenate([lh, gap_rows, hh], axis=0)
        bl = jnp.concatenate([ll, gap_rows, hl], axis=0)
        rhs = jnp.concatenate([jnp.concatenate([bh, bl], axis=1), jnp.concatenate([bh, corner], axis=1)], axis=0)
        return jnp.concatenate([ch, cl], axis=1), rhs

    for start in starts:
        wind = start < WINDS
        fields = [start + i for i in range(GROUP)]
        columns = [column_stage(f, wind) for f in fields]
        outs = [row_stage(*c) if use_x else None for c in columns]
        ranks = [carry_stage(*c, o) for c, o in zip(columns, outs)]
        for f, o, (lhs, rhs) in zip(fields, outs, ranks):
            out = mm(lhs, rhs)
            total = out[:, :LANES] + out[:, LANES:]
            if use_x:
                total = (o[0] + o[1]) + (o[2] + total)
            for b in range(PARTS):
                lanes = slice(b * LANES, (b + 1) * LANES)
                part = total[b * ROWS:(b + 1) * ROWS]
                if base_ref is not None:
                    part = part + base_ref[f - starts[0], :, lanes]
                out_ref[f - starts[0], :, lanes] = part


def local_filter(table, carry, x, first, count, before, base=None):
    starts = tuple(range(first, first + count, GROUP))
    use_x, use_carry = base is None, carry is not None
    names = ["table"] + ["carry"] * use_carry + ["x"] * use_x + ["base"] * (base is not None) + ["before"]
    arrays = {"table": table, "carry": carry, "x": x, "base": base, "before": before}
    specs = {"before": ANY}

    def body(*refs):
        by_name = dict(zip(names, refs))
        local_filter_kernel(starts, use_x, use_carry, by_name["table"], by_name.get("carry"),
                            by_name.get("x"), by_name.get("base"), refs[len(names)])

    return pl.pallas_call(
        body,
        in_specs=[specs.get(n, VMEM) for n in names],
        out_specs=VMEM,
        out_shape=jax.ShapeDtypeStruct((count, ROWS, COLS), F32),
        compiler_params=params(),
        cost_estimate=pl.CostEstimate(flops=int(count * 30000000), bytes_accessed=count * 150_000, transcendentals=0),
        name="local_filter",
    )(*[arrays[n] for n in names])


def add_carries(half, table_ref, carry_ref, z_refs, part, store):
    row = fiota((8, LANES), 0)
    up_steps, down_steps = row + 1.0, 8.0 - row
    tables = [carry_ref[side, s, part] for side in range(2) for s in range(SCALES)]
    start = pl.multiple_of((half * 3 + part) * GROUP, GROUP)
    group_facts = table_ref[pl.ds(start, GROUP), :]
    for i in range(GROUP):
        facts = group_facts[i:i + 1, :]
        ups = []
        for s in range(SCALES):
            r = jnp.broadcast_to(facts[:, s:s + 1], (8, LANES))
            w = jnp.broadcast_to(facts[:, SCALES + s:SCALES + s + 1], (8, LANES))
            jump = jnp.exp(-8.0 * r)
            up, down = [w * jnp.exp(-r * up_steps)], [w * jnp.exp(-r * down_steps)]
            for _ in range(ROWS // 8 - 1):
                up.append(up[-1] * jump)
                down.insert(0, down[0] * jump)
            ups.append((jnp.concatenate(up, axis=0), jnp.concatenate(down, axis=0)))
        for b in range(PARTS):
            lanes = slice(b * LANES, (b + 1) * LANES)
            total = jnp.where(half == 0, z_refs[part // 2][part % 2 * GROUP + i, :, lanes],
                              z_refs[(3 + part) // 2][(3 + part) % 2 * GROUP + i, :, lanes])
            for s in range(SCALES):
                total = total + ups[s][0] * tables[s][i:i + 1, lanes] + ups[s][1] * tables[SCALES + s][i:i + 1, lanes]
            store(i, lanes, total)


def finish_own_kernel(table_ref, carry_ref, z0_ref, z1_ref, z2_ref, out_ref, own_ref, buf_ref, sem):
    half = lat_index() & 1
    z_refs = (z0_ref, z1_ref, z2_ref)

    def store_first(i, lanes, value):
        buf_ref[i, :, lanes] = value

    add_carries(half, table_ref, carry_ref, z_refs, 0, store_first)
    copy = pltpu.make_async_copy(buf_ref, out_ref.at[pl.ds(half * HALF, GROUP)], sem)
    copy.start()
    for part in (1, 2):
        def store(i, lanes, value):
            own_ref[(part - 1) * GROUP + i, :, lanes] = value

        add_carries(half, table_ref, carry_ref, z_refs, part, store)
    copy.wait()


def finish_own(table, carry, parts):
    return pl.pallas_call(
        finish_own_kernel,
        in_specs=[VMEM] * 5,
        out_specs=[HBM, VMEM],
        out_shape=[jax.ShapeDtypeStruct((FIELDS, ROWS, COLS), F32), jax.ShapeDtypeStruct((2 * GROUP, ROWS, COLS), F32)],
        scratch_shapes=[pltpu.VMEM((GROUP, ROWS, COLS), F32), pltpu.SemaphoreType.DMA],
        compiler_params=params(),
        cost_estimate=pl.CostEstimate(flops=1_000_000_000, bytes_accessed=2_000_000, transcendentals=0),
        name="finish_own",
    )(table, carry.reshape(2, SCALES, 3, GROUP, COLS), *parts)


def finish_kernel(table_ref, carry_ref, z0_ref, z1_ref, z2_ref, own_ref, _, out_ref, buf_ref, sem):
    half = 1 - (lat_index() & 1)
    mine = (1 - half) * HALF + GROUP
    ready = pltpu.make_async_copy(own_ref, out_ref.at[pl.ds(mine, 2 * GROUP)], sem.at[3])
    ready.start()
    copies = [ready]
    for part in range(3):
        def store(i, lanes, value):
            buf_ref[part, i, :, lanes] = value

        add_carries(half, table_ref, carry_ref, (z0_ref, z1_ref, z2_ref), part, store)
        there = out_ref.at[pl.ds((half * 3 + part) * GROUP, GROUP)]
        copies.append(pltpu.make_async_copy(buf_ref.at[part], there, sem.at[part]))
        copies[-1].start()
    for copy in copies:
        copy.wait()


def finish(table, carry, parts, own, out):
    return pl.pallas_call(
        finish_kernel,
        in_specs=[VMEM] * 6 + [HBM],
        out_specs=HBM,
        out_shape=jax.ShapeDtypeStruct((FIELDS, ROWS, COLS), F32),
        scratch_shapes=[pltpu.VMEM((3, GROUP, ROWS, COLS), F32), pltpu.SemaphoreType.DMA((4,))],
        input_output_aliases={6: 0},
        compiler_params=params(),
        name="finish",
    )(table, carry.reshape(2, SCALES, 3, GROUP, COLS), *parts, own, out)


def partner(axis, count, bit):
    return functools.partial(lax.ppermute, axis_name=axis, perm=[(i, i ^ bit) for i in range(count)])


def shards(x, lengths, weights):
    facts = jnp.concatenate([lengths.T, weights.T], axis=0)
    sums, edge, table, lanes, held = row_sums(facts, x)
    got = [partner("lon", NLON, d)(sums) for d in (1, 2, 3)]
    early = local_filter(table, None, held, 32, 16, sums)
    winds = wind_sums(table, held, early)
    part, half = lon_merge(lanes, sums, got, winds)
    theirs = partner("lon", NLON, 4)(half)
    local = local_sums(table, held, winds, part)
    steps = lat_steps(table, part)
    carry, keep, send = column_sums(table, lanes, part, theirs, edge, local)
    got_core = partner("lat", NLAT, 1)(send)
    chip = chip_merge(steps, keep, got_core)
    pair = partner("lat", NLAT, 2)(chip)
    z2 = local_filter(table, carry, held, 32, 16, chip, early)
    z0 = local_filter(table, carry, held, 0, 16, z2)
    left, *sends = quad_merge(steps, chip, pair, z0)
    gs = [partner("lat", NLAT, 4 * d)(t) for d, t in zip((1, 2, 3), sends)]
    z1 = local_filter(table, carry, held, 16, 16, left)
    own, other = lat_carry(steps, keep, got_core, pair, left, gs, z1)
    got_carry = partner("lat", NLAT, 1)(other)
    out, done = finish_own(table, own, (z0, z1, z2))
    return finish(table, got_carry, (z0, z1, z2), done, out)


def solution(mesh):
    in_specs = (P(None, "lat", "lon"), P(), P())
    out_specs = P(None, "lat", "lon")
    return jax.shard_map(shards, mesh=mesh, in_specs=in_specs, out_specs=out_specs, check_vma=False)
```

```python
import functools

import jax
import jax.numpy as jnp
from jax import lax
from jax.experimental import pallas as pl
from jax.experimental.pallas import tpu as pltpu
from jax.sharding import PartitionSpec as P

LEVELS = 8
SCALES = 3
WINDS = 16
FIELDS = 48
ROWS = 48
COLS = 384
GROUP = 8
GROUPS = FIELDS // GROUP
NLAT = 16
NLON = 8
LANES = 128
PARTS = COLS // LANES
HALF = FIELDS // 2
HALF_ROWS = SCALES * HALF
F32 = jnp.float32
BF16 = jnp.bfloat16

VMEM = pl.BlockSpec(memory_space=pltpu.VMEM)
BIG = 48 * 1024 * 1024
WHOLE = 50 * 1024 * 1024


def lat_index():
    return lax.axis_index("lat")


def lon_index():
    return lax.axis_index("lon")


def params(**kw):
    return pltpu.CompilerParams(vmem_limit_bytes=BIG, **kw)


def iota(shape, dim):
    return lax.broadcasted_iota(jnp.int32, shape, dim)


def fiota(shape, dim):
    return iota(shape, dim).astype(F32)


def split(value):
    high = value.astype(BF16)
    return high, (value - high.astype(F32)).astype(BF16)


def mm(a, b):
    return jnp.dot(a, b, preferred_element_type=F32)


def lane_fields(shape):
    lane = iota(shape, 1)
    virtual = lane & 31
    wind_field = ((virtual >> 4) << 3) + (virtual & 7)
    return lane, lane >> 5, virtual, wind_field, virtual + WINDS


def exact(a, b, dims):
    return lax.dot_general(a, b, (dims, ((), ())), precision=lax.Precision.HIGHEST, preferred_element_type=F32)


def lane_rates(rate):
    shape = (FIELDS, LANES)
    _, _, _, wind_field, rest_field = lane_fields(shape)
    field = iota(shape, 0)
    lane = iota((1, LANES), 1)

    def pick(which):
        every = exact(rate, jnp.where(field == which, 1.0, 0.0).astype(F32), ((1,), (0,)))
        value = jnp.where(lane < 32, every[0:1], jnp.where(lane < 64, every[1:2], every[2:3]))
        return jnp.where(lane < 96, value, 0.0)

    return pick(wind_field), pick(rest_field)


def scale_weights(rate, weights):
    decay = jnp.exp(-rate)
    leak = 1.0 - decay
    cube = (1.0 + decay) * (1.0 + decay) * (1.0 + decay)
    coefficient = weights * cube / (leak * (1.0 + decay * decay))
    kappa = leak / (1.0 + decay)
    return coefficient * kappa * kappa


def lane_kinds(shape):
    _, _, virtual, _, _ = lane_fields(shape)
    second = virtual >= 16
    north = (virtual & 15) >= 8
    zonal = second != north
    sign = jnp.where(second | north, -1.0, 1.0).astype(F32)
    return zonal, sign


def row_sums_kernel(len_ref, x_ref, sums_ref, edge_ref, table_ref, lanes_ref, held_ref, w_ref, sem):
    lon = lon_index()
    copies = []
    for k, (start, stop) in enumerate(((0, WINDS), (WINDS, FIELDS))):
        here = pl.ds(start, stop - start)
        copies.append(pltpu.make_async_copy(x_ref.at[here], held_ref.at[here], sem.at[k]))
        copies[-1].start()
    rate = 1.0 / len_ref[0:SCALES, :]
    pair = lane_rates(rate)
    lanes_ref[...] = jnp.concatenate([pair[0], pair[1], jnp.ones((6, LANES), F32)], axis=0)
    column = fiota((COLS, LANES), 0)
    for tile, rates in enumerate(pair):
        for side, steps in enumerate((COLS - 1 - column, column)):
            high, low = split(jnp.exp(-rates * steps))
            lanes = slice(side * LANES, (side + 1) * LANES)
            w_ref[tile, 0:COLS, lanes] = high
            w_ref[tile, COLS:2 * COLS, lanes] = high
            w_ref[tile, 2 * COLS:, lanes] = low
    both = jnp.concatenate([rate, scale_weights(rate, len_ref[SCALES:, :]), jnp.ones((2, FIELDS), F32)], axis=0)
    eye = jnp.where(iota((8, LANES), 0) == iota((8, LANES), 1), 1.0, 0.0).astype(F32)
    table_ref[...] = exact(both, eye, ((0,), (0,)))
    lane = iota((ROWS, LANES), 1)
    virtual = lane & 31
    zero = jnp.zeros((ROWS, LANES), F32)
    left, right, first, last = zero, zero, zero, zero
    for g in range(GROUPS):
        if g in (0, 2):
            copies[g // 2].wait()
        x = held_ref[g * GROUP:(g + 1) * GROUP].reshape(GROUP * ROWS, COLS)
        xh, xl = split(x)
        res = mm(jnp.concatenate([xh, xl, xh], axis=1), w_ref[0 if g < 2 else 1])
        if g == 2:
            left, right = zero, zero
        for i in range(GROUP):
            rows = slice(i * ROWS, (i + 1) * ROWS)
            mine = (virtual & 15) == g * GROUP + i if g < 2 else virtual == (g - 2) * GROUP + i
            left = jnp.where(mine, res[rows, 0:128], left)
            right = jnp.where(mine, res[rows, 128:256], right)
            if g < 2:
                first = jnp.where(mine, x[rows, 0:1], first)
                last = jnp.where(mine, x[rows, COLS - 1:COLS], last)
        if g == 1:
            edge = jnp.where(lon == 0, first, jnp.where(lon == NLON - 1, last, 0.0))
            sums_ref[:, 0:128] = jnp.where(lane >= 96, edge, left)
            sums_ref[:, 128:256] = right
            edge_ref[:, 0:128] = first
            edge_ref[:, 128:256] = last
    sums_ref[:, 256:384] = left
    sums_ref[:, 384:512] = right


HBM = pl.BlockSpec(memory_space=pltpu.HBM)
ANY = pl.BlockSpec(memory_space=pl.ANY)


def row_sums(facts, x):
    return pl.pallas_call(
        row_sums_kernel,
        in_specs=[VMEM, HBM],
        out_specs=[VMEM] * 5,
        out_shape=[jax.ShapeDtypeStruct((ROWS, 512), F32), jax.ShapeDtypeStruct((ROWS, 256), F32),
                   jax.ShapeDtypeStruct((FIELDS, LANES), F32), jax.ShapeDtypeStruct((8, LANES), F32),
                   jax.ShapeDtypeStruct((FIELDS, ROWS, COLS), F32)],
        scratch_shapes=[pltpu.VMEM((2, 3 * COLS, 256), BF16), pltpu.SemaphoreType.DMA((2,))],
        compiler_params=pltpu.CompilerParams(vmem_limit_bytes=WHOLE),
        name="row_sums",
    )(facts, x)


def zonal_difference(x):
    shape = x.shape
    axis = len(shape) - 1
    column = iota(shape, axis)
    ahead = jnp.where(column == COLS - 1, 0.0, pltpu.roll(x, COLS - 1, axis))
    behind = jnp.where(column == 0, 0.0, pltpu.roll(x, 1, axis))
    return 0.5 * (ahead - behind)


def column_piece_sums(table_ref, x_ref, groups):
    top = lat_index() == 0
    count = 2 * SCALES * GROUP
    shape = (count, LANES)
    out_row = iota(shape, 0)
    member = out_row & 7
    left_side = out_row < SCALES * GROUP
    lane = iota(shape, 1)
    source = jnp.where(lane >= ROWS, lane - ROWS, lane).astype(F32)
    used = lane < 2 * ROWS
    steps = jnp.where(left_side, ROWS - 1 - source, source)
    zeros = jnp.zeros((32, COLS), BF16)

    def weighted(matrix, x, i):
        mh, ml = split(jnp.where(used & (member == i), matrix, 0.0))
        xh, xl = split(x)
        return mm(jnp.concatenate([mh, ml[:, :ROWS]], axis=1), jnp.concatenate([xh, xl, zeros, xh], axis=0))

    def group_sums(group, wind):
        rate = table_ref[group * GROUP:(group + 1) * GROUP, :]
        row_rate = jnp.concatenate([rate[:, s:s + 1] for _ in range(2) for s in range(SCALES)], axis=0)
        wide = jnp.broadcast_to(row_rate, shape)
        plain = jnp.exp(-wide * steps)
        acc = jnp.zeros((count, COLS), F32)
        if wind:
            decay = jnp.exp(-wide)
            gain = 0.5 * (1.0 - decay * decay) / decay
            start = jnp.where(top & (source == 0.0), 0.5 * jnp.exp(-wide * ROWS), 0.0)
            slope = jnp.where(left_side, -gain * plain - start, gain * plain)
            second_sign = jnp.where(group == 0, 1.0, -1.0)
            for i in range(GROUP):
                acc += weighted(plain, -zonal_difference(x_ref[(1 - group) * GROUP + i]), i)
                acc += weighted(slope, second_sign * x_ref[group * GROUP + i], i)
        else:
            for i in range(GROUP):
                acc += weighted(plain, x_ref[group * GROUP + i], i)
        return acc, row_rate

    return [group_sums(group, group < 2) for group in groups]


def wind_sums_kernel(table_ref, x_ref, _, out_ref):
    made = column_piece_sums(table_ref, x_ref, (0, 1))
    out_ref[...] = jnp.concatenate([m[0] for m in made], axis=0)


def wind_sums(table, x, before):
    return pl.pallas_call(
        wind_sums_kernel,
        in_specs=[VMEM, VMEM, ANY],
        out_specs=VMEM,
        out_shape=jax.ShapeDtypeStruct((4 * SCALES * GROUP, COLS), F32),
        compiler_params=params(),
        cost_estimate=pl.CostEstimate(flops=300_000_000, bytes_accessed=1_000_000, transcendentals=0),
        name="wind_sums",
    )(table, x, before)


def local_sums_kernel(table_ref, x_ref, winds_ref, _, out_ref):
    count = 2 * SCALES * GROUP
    made = column_piece_sums(table_ref, x_ref, range(2, GROUPS))
    acc = jnp.concatenate([winds_ref[...]] + [m[0] for m in made], axis=0)
    factors = []
    for group in range(GROUPS):
        rate = table_ref[group * GROUP:(group + 1) * GROUP, :]
        row_rate = jnp.concatenate([rate[:, s:s + 1] for _ in range(2) for s in range(SCALES)], axis=0)
        factors.append(jnp.broadcast_to(jnp.exp(-row_rate), (count, LANES)))
    factor = jnp.concatenate(factors, axis=0)
    factor = jnp.concatenate([factor] * PARTS, axis=1)
    column = iota(acc.shape, 1)
    forward, backward = acc, acc
    step = 1
    while step < COLS:
        forward = forward + factor * jnp.where(column >= step, pltpu.roll(forward, step, 1), 0.0)
        backward = backward + factor * jnp.where(column < COLS - step, pltpu.roll(backward, COLS - step, 1), 0.0)
        factor = factor * factor
        step *= 2
    acc = forward + backward - acc
    for group in range(GROUPS):
        for side in range(2):
            for s in range(SCALES):
                k = group * count + (side * SCALES + s) * GROUP
                out_ref[group // 3, side, s, group % 3] = acc[k:k + GROUP]


def local_sums(table, x, winds, before):
    out = pl.pallas_call(
        local_sums_kernel,
        in_specs=[VMEM, VMEM, VMEM, ANY],
        out_specs=VMEM,
        out_shape=jax.ShapeDtypeStruct((2, 2, SCALES, 3, GROUP, COLS), F32),
        compiler_params=params(),
        cost_estimate=pl.CostEstimate(flops=600000000, bytes_accessed=4_000_000, transcendentals=0),
        name="local_sums",
    )(table, x, winds, before)
    return out.reshape(2, 2 * HALF_ROWS, COLS)


def lon_merge_kernel(lanes_ref, own_ref, g1_ref, g3_ref, g2_ref, _, part_ref, send_ref):
    y = lon_index() & 3
    high = lon_index() >= 4
    yf = y.astype(F32)
    zonal, _ = lane_kinds((1, LANES))
    lane = iota((1, LANES), 1)
    for tile in range(2):
        rate = lanes_ref[tile:tile + 1, :]
        step = lambda n: jnp.exp(-rate * (COLS * n))
        base = tile * 256
        lanes_l = slice(base, base + 128)
        lanes_r = slice(base + 128, base + 256)
        left_total = step(3.0 - yf) * own_ref[:, lanes_l]
        right_total = step(yf) * own_ref[:, lanes_r]
        left = jnp.zeros((ROWS, LANES), F32)
        right = jnp.zeros((ROWS, LANES), F32)
        for d, ref in ((1, g1_ref), (2, g2_ref), (3, g3_ref)):
            other = y ^ d
            of = other.astype(F32)
            below = other < y
            lg, rg = ref[:, lanes_l], ref[:, lanes_r]
            gap = jnp.abs(yf - of) - 1.0
            left = left + jnp.where(below, step(gap), 0.0) * lg
            right = right + jnp.where(below, 0.0, step(gap)) * rg
            left_total = left_total + step(3.0 - of) * lg
            right_total = right_total + step(of) * rg
        part_ref[:, lanes_l] = left
        part_ref[:, lanes_r] = right
        part_ref[:, 512 + tile * 128:640 + tile * 128] = left_total
        image = jnp.exp(-rate * (4.0 * COLS + 1.0))
        if tile == 0:
            image = jnp.where(zonal, -image, image)
            image = jnp.where(lane >= 96, -1.0, image)
            right_total = jnp.where(lane >= 96, 0.0, right_total)
        send_ref[:, tile * 128:tile * 128 + 128] = jnp.where(high, right_total - image * left_total, left_total)


def lon_merge(lanes, own, got, after):
    return pl.pallas_call(
        lon_merge_kernel,
        in_specs=[VMEM] * 5 + [ANY],
        out_specs=[VMEM, VMEM],
        out_shape=[jax.ShapeDtypeStruct((ROWS, 768), F32), jax.ShapeDtypeStruct((ROWS, 256), F32)],
        compiler_params=params(),
        name="lon_merge",
    )(lanes, own, got[0], got[2], got[1], after)


def spread_edges(tile):
    lane = iota(tile.shape, 1)
    out = tile
    for k in range(6):
        out = jnp.where((lane >> 4) == k, pltpu.roll(tile, (k * 16 + 32) % LANES, 1), out)
    return out


def column_sums_kernel(table_ref, lanes_ref, part_ref, theirs_ref, edge_ref, local_ref,
                       carry_ref, keep_ref, send_ref):
    lat, lon = lat_index(), lon_index()
    y = lon & 3
    yf = y.astype(F32)
    high = lon >= 4
    highf = jnp.where(high, 1.0, 0.0)
    lowf = 1.0 - highf
    lonf = lon.astype(F32)
    top = lat == 0
    rates = (lanes_ref[0:1, :], lanes_ref[1:2, :])
    zonal, sign = lane_kinds((1, LANES))
    row = fiota((ROWS, LANES), 0)
    weights = []
    for tile in range(2):
        rate = rates[tile]
        step = lambda n: jnp.exp(-rate * (COLS * n))
        decay = jnp.exp(-rate)
        theirs = theirs_ref[:, tile * 128:tile * 128 + 128]
        half = part_ref[:, 512 + tile * 128:640 + tile * 128]
        left = part_ref[:, tile * 256:tile * 256 + 128] + (highf * step(yf)) * theirs
        right = part_ref[:, tile * 256 + 128:tile * 256 + 256] + (lowf * step(3.0 - yf)) * theirs
        whole = (highf + lowf * step(4.0)) * half + (highf * step(4.0)) * theirs
        end = step(7.0 - lonf)
        weight_l = jnp.exp(-rate * (ROWS - 1 - row))
        weight_r = jnp.exp(-rate * row)
        carry_l = left
        carry_r = right - (end * decay) * whole
        if tile == 0:
            v0 = spread_edges(lowf * half + highf * theirs)
            vn = spread_edges(highf * half + lowf * theirs)
            gain = 0.5 * (1.0 - decay * decay) / decay
            initial = -0.5 * (v0 + vn / decay)
            zonal_l = step(lonf) * initial - gain * left + 0.5 * edge_ref[:, 0:128]
            zonal_r = (gain * right - 0.5 * edge_ref[:, 128:256]
                       + end * (gain * v0 - decay * (step(8.0) * initial - gain * whole)))
            carry_l = sign * jnp.where(zonal, zonal_l, carry_l)
            carry_r = sign * jnp.where(zonal, zonal_r, carry_r)
            start = jnp.where(top & (row == 0.0), 0.5 * jnp.exp(-rate * ROWS), 0.0)
            weight_l = jnp.where(zonal, weight_l, -gain * weight_l - start)
            weight_r = jnp.where(zonal, weight_r, gain * weight_r)
        carry_ref[:, tile * 256:tile * 256 + 128] = carry_l
        carry_ref[:, tile * 256 + 128:tile * 256 + 256] = carry_r
        fold = lambda w, c: jnp.sum(w * c, axis=0, keepdims=True)
        weights.append(((fold(weight_l, carry_l), fold(weight_l, carry_r)),
                        (fold(weight_r, carry_l), fold(weight_r, carry_r))))
    shape = (HALF_ROWS, LANES)
    lane, lane_scale, _, wind_field, rest_field = lane_fields(shape)
    out_row = iota(shape, 0)
    scale = jnp.where(out_row < HALF, 0, jnp.where(out_row < 2 * HALF, 1, 2))
    core = lat & 1
    column = fiota((HALF_ROWS, COLS), 1)
    for ref, half in ((send_ref, 1 - core), (keep_ref, core)):
        field = out_row - scale * HALF + half * HALF
        same = lane_scale == scale
        wind = same & (wind_field == field)
        rest = same & (rest_field == field)
        rate = table_ref[pl.ds(pl.multiple_of(half * HALF, 8), HALF), :]
        rate = jnp.concatenate([rate[:, s:s + 1] for s in range(SCALES)], axis=0)
        fall = jnp.exp(-rate * (column + 1.0))
        rise = jnp.exp(-rate * (COLS - column))
        for side in range(2):
            pick = lambda k: jnp.sum(
                jnp.where(wind, weights[0][side][k], 0.0) + jnp.where(rest, weights[1][side][k], 0.0),
                axis=1, keepdims=True)
            rows = slice(side * HALF_ROWS, (side + 1) * HALF_ROWS)
            ref[rows, :] = local_ref[half, rows, :] + pick(0) * fall + pick(1) * rise


def column_sums(table, lanes, part, theirs, edge, local):
    half = jax.ShapeDtypeStruct((2 * HALF_ROWS, COLS), F32)
    return pl.pallas_call(
        column_sums_kernel,
        in_specs=[VMEM] * 6,
        out_specs=[VMEM] * 3,
        out_shape=[jax.ShapeDtypeStruct((ROWS, 512), F32), half, half],
        compiler_params=params(),
        name="column_sums",
    )(table, lanes, part, theirs, edge, local)


LEFT = slice(0, HALF_ROWS)
RIGHT = slice(HALF_ROWS, 2 * HALF_ROWS)
STEPS = 21


def steps_kernel(table_ref, _, out_ref):
    lat = lat_index()
    odd = (lat & 1) == 1
    odd_chip = ((lat >> 1) & 1) == 1
    z = lat >> 2
    zf = z.astype(F32)
    rate = table_ref[pl.ds(pl.multiple_of((lat & 1) * HALF, 8), HALF), :]
    rate = jnp.concatenate([rate[:, s:s + 1] for s in range(SCALES)], axis=0)
    rate = jnp.broadcast_to(rate, (HALF_ROWS, LANES))
    power = lambda n: jnp.exp(-rate * n)
    quad = lambda n: power(4.0 * ROWS * n)
    one, zero = jnp.ones_like(rate), jnp.zeros_like(rate)
    device, chip = power(1.0 * ROWS), power(2.0 * ROWS)
    out = [jnp.where(odd, one, device), jnp.where(odd, device, one)]
    out += [jnp.where(odd_chip, one, chip), jnp.where(odd_chip, chip, one)]
    out += [power(1.0 + 4 * ROWS * jnp.maximum(7.0 - 2.0 * zf, 1.0))]
    for d in (1, 2, 3):
        other = z ^ d
        of = other.astype(F32)
        below = other < z
        gap = quad(jnp.abs(zf - of) - 1.0)
        out += [jnp.where(below, gap, zero), jnp.where(below, zero, gap), jnp.where(below, quad(3.0 - of), zero)]
    out += [quad(3.0 - zf), quad(3.0 - zf) * power(1.0)]
    out += [jnp.where(odd_chip, chip, one), jnp.where(odd_chip, one, zero)]
    out += [jnp.where(odd_chip, one, chip), jnp.where(odd_chip, zero, one)]
    out += [device]
    for k, value in enumerate(out):
        out_ref[k] = value


def lat_steps(table, before):
    return pl.pallas_call(
        steps_kernel,
        in_specs=[VMEM, ANY],
        out_specs=VMEM,
        out_shape=jax.ShapeDtypeStruct((STEPS, HALF_ROWS, LANES), F32),
        compiler_params=params(),
        name="lat_steps",
    )(table, before)


def by_tile(body):
    for b in range(PARTS):
        body(slice(b * LANES, (b + 1) * LANES))


def chip_merge_kernel(steps_ref, keep_ref, got_ref, chip_ref):
    def body(lanes):
        mine, other = steps_ref[0], steps_ref[1]
        chip_ref[LEFT, lanes] = mine * keep_ref[LEFT, lanes] + other * got_ref[LEFT, lanes]
        chip_ref[RIGHT, lanes] = other * keep_ref[RIGHT, lanes] + mine * got_ref[RIGHT, lanes]

    by_tile(body)


def chip_merge(steps, keep, got):
    return pl.pallas_call(
        chip_merge_kernel,
        in_specs=[VMEM] * 3,
        out_specs=VMEM,
        out_shape=jax.ShapeDtypeStruct((2 * HALF_ROWS, COLS), F32),
        compiler_params=params(),
        name="chip_merge",
    )(steps, keep, got)


def quad_merge_kernel(steps_ref, chip_ref, pair_ref, _, left_ref, s1_ref, s2_ref, s3_ref):
    z = lat_index() >> 2

    def body(lanes):
        mine, other, image = steps_ref[2], steps_ref[3], steps_ref[4]
        left = mine * chip_ref[LEFT, lanes] + other * pair_ref[LEFT, lanes]
        right = other * chip_ref[RIGHT, lanes] + mine * pair_ref[RIGHT, lanes]
        back = right - image * left
        left_ref[:, lanes] = left
        for d, ref in ((1, s1_ref), (2, s2_ref), (3, s3_ref)):
            ref[:, lanes] = jnp.where((z ^ d) > z, left, back)

    by_tile(body)


def quad_merge(steps, chip, pair, after):
    one = jax.ShapeDtypeStruct((HALF_ROWS, COLS), F32)
    return pl.pallas_call(
        quad_merge_kernel,
        in_specs=[VMEM] * 3 + [ANY],
        out_specs=[VMEM] * 4,
        out_shape=[one] * 4,
        compiler_params=params(),
        name="quad_merge",
    )(steps, chip, pair, after)


def lat_carry_kernel(steps_ref, keep_ref, got_ref, pair_ref, left_ref, g2_ref, g1_ref, g3_ref, _,
                     own_ref, send_ref):
    odd = (lat_index() & 1) == 1

    def body(lanes):
        left, right, whole = 0.0, 0.0, steps_ref[14] * left_ref[:, lanes]
        for k, ref in ((5, g1_ref), (8, g2_ref), (11, g3_ref)):
            g = ref[:, lanes]
            left = left + steps_ref[k] * g
            right = right + steps_ref[k + 1] * g
            whole = whole + steps_ref[k + 2] * g
        right = right - steps_ref[15] * whole
        left = steps_ref[16] * left + steps_ref[17] * pair_ref[LEFT, lanes]
        right = steps_ref[18] * right + steps_ref[19] * pair_ref[RIGHT, lanes]
        low_left = jnp.where(odd, got_ref[LEFT, lanes], keep_ref[LEFT, lanes])
        high_right = jnp.where(odd, keep_ref[RIGHT, lanes], got_ref[RIGHT, lanes])
        high_l = low_left + steps_ref[20] * left
        low_r = high_right + steps_ref[20] * right
        own_ref[LEFT, lanes] = jnp.where(odd, high_l, left)
        own_ref[RIGHT, lanes] = jnp.where(odd, right, low_r)
        send_ref[LEFT, lanes] = jnp.where(odd, left, high_l)
        send_ref[RIGHT, lanes] = jnp.where(odd, low_r, right)

    by_tile(body)


def lat_carry(steps, keep, got, pair, left, gs, after):
    half = jax.ShapeDtypeStruct((2 * HALF_ROWS, COLS), F32)
    return pl.pallas_call(
        lat_carry_kernel,
        in_specs=[VMEM] * 8 + [ANY],
        out_specs=[VMEM] * 2,
        out_shape=[half, half],
        compiler_params=params(),
        name="lat_carry",
    )(steps, keep, got, pair, left, gs[1], gs[0], gs[2], after)


def local_filter_kernel(starts, use_x, use_carry, table_ref, carry_ref, x_ref, base_ref, out_ref):
    top = lat_index() == 0
    shape = (ROWS, LANES)
    row = fiota(shape, 0)
    lane = iota(shape, 1)
    source = jnp.where(lane >= ROWS, lane - ROWS, lane).astype(F32)
    used = lane < 2 * ROWS
    gap = jnp.abs(row - source)
    gap_low = jnp.abs(source - 1.0 - row)
    gap_high = jnp.abs(source + 1.0 - row)
    first = source == 0.0
    spread = jnp.abs(fiota((LANES, LANES), 0) - fiota((LANES, LANES), 1))
    tag = lane & 31
    corner = jnp.zeros((LANES, LANES), BF16)
    left_lane = (lane == LANES - 1) | (lane == 1) | (lane == 3)
    flat = lane[:1]
    row_scale = jnp.where((flat == LANES - 1) | (flat == 0), 0, jnp.where(flat <= 2, 1, 2))
    base = iota((8, LANES), 0)
    column = fiota((8, LANES), 1)

    def carry_tile(tile, virtual):
        left = carry_ref[:, tile * 256:tile * 256 + 128]
        right = carry_ref[:, tile * 256 + 128:tile * 256 + 256]
        left = pltpu.roll(left, (LANES - virtual) % LANES, 1)
        right = pltpu.roll(right, (LANES + 1 - virtual) % LANES, 1)
        return jnp.where(tag == 0, left, jnp.where(tag == 1, right, 0.0))

    def column_pass(matrices, x, carry):
        parts = [split(jnp.where(used, m, 0.0)) for m in matrices]
        lhs = jnp.concatenate([jnp.concatenate([mh, ml[:, :ROWS]], axis=1) for mh, ml in parts], axis=0)
        wide = [t for t in (x, carry) if t is not None]
        wide = wide[0] if len(wide) == 1 else jnp.concatenate(wide, axis=1)
        xh, xl = split(wide)
        rhs = jnp.concatenate([xh, xl, jnp.zeros((32, wide.shape[1]), BF16), xh], axis=0)
        return mm(lhs, rhs)

    def column_stage(f, wind):
        facts = table_ref[pl.ds(f, 1), :]
        rates = [facts[:, s:s + 1] for s in range(SCALES)]
        gains = [facts[:, SCALES + s:SCALES + s + 1] for s in range(SCALES)]
        plain = [gains[s] * jnp.exp(-rates[s] * gap) for s in range(SCALES)]
        if wind:
            slopes = []
            for s in range(SCALES):
                slope = jnp.exp(-rates[s] * gap_low) - jnp.exp(-rates[s] * gap_high)
                slope = slope - jnp.where(top & first, jnp.exp(-rates[s] * (row + 1.0)), 0.0)
                slopes.append((0.5 * gains[s]) * slope)
            stream = f < GROUP
            second_sign = 1.0 if stream else -1.0
            meridional = f if stream else f + 16
            zonal = f + 8
            pair = f + 8 if stream else f - 8
            w = column_pass(plain, -zonal_difference(x_ref[pair]), carry_tile(0, zonal))
            w = w + column_pass(slopes, second_sign * x_ref[f], carry_tile(0, meridional))
        else:
            w = column_pass(plain, x_ref[f] if use_x else None, carry_tile(1, f - WINDS) if use_carry else None)
        return rates, w

    def row_stage(rates, w):
        outs = []
        for s in range(SCALES):
            rows = slice(s * ROWS, (s + 1) * ROWS)
            stack = jnp.concatenate([w[rows, b * LANES:(b + 1) * LANES] for b in range(PARTS)], axis=0)
            wh, wl = split(stack)
            th, tl = split(jnp.exp(-rates[s] * spread))
            lhs = jnp.concatenate([wh, wl], axis=1)
            rhs = jnp.concatenate([jnp.concatenate([th, tl], axis=1), jnp.concatenate([th, corner], axis=1)], axis=0)
            out = mm(lhs, rhs)
            outs.append(out[:, :LANES] + out[:, LANES:])
        return outs

    def carry_stage(rates, w, outs):
        sums, outer = None, jnp.zeros((ROWS, LANES), F32)
        for s in range(SCALES):
            here = row_scale == s
            if use_carry:
                moved = pltpu.roll(w[s * ROWS:(s + 1) * ROWS, w.shape[1] - LANES:], LANES - 30 * s - 1, 1)
                outer = moved if s == 0 else jnp.where(here, moved, outer)
            if use_x:
                turned = outs[s] if s == 0 else pltpu.roll(outs[s], 2 * s, 1)
                sums = turned if s == 0 else jnp.where(here, turned, sums)
        rate_row = jnp.where(row_scale == 0, rates[0], jnp.where(row_scale == 1, rates[1], rates[2]))
        jump = jnp.exp(-rate_row * LANES)
        from_left, from_right = [outer], [outer]
        for b in range(PARTS - 1):
            ahead, behind = jump * from_left[-1], jump * from_right[-1]
            if use_x:
                ahead = ahead + sums[b * ROWS:(b + 1) * ROWS]
                behind = behind + sums[(PARTS - 1 - b) * ROWS:(PARTS - b) * ROWS]
            from_left.append(ahead)
            from_right.append(behind)
        carries = [jnp.where(left_lane, from_left[b], from_right[PARTS - 1 - b]) for b in range(PARTS)]
        ch, cl = split(jnp.concatenate(carries, axis=0))
        low_rate = jnp.where(base == 0, rates[0], jnp.where(base <= 2, rates[1], rates[2]))
        low_left = (base == 1) | (base == 3)
        low = jnp.where(base <= 4, jnp.exp(-low_rate * jnp.where(low_left, column + 1.0, LANES - column)), 0.0)
        high = jnp.where(base == 7, jnp.exp(-rates[0] * (column + 1.0)), 0.0)
        pad = jnp.zeros((8, LANES), F32)
        lh, ll = split(jnp.concatenate([low, pad], axis=0))
        hh, hl = split(jnp.concatenate([pad, high], axis=0))
        gap_rows = jnp.zeros((96, LANES), BF16)
        bh = jnp.concatenate([lh, gap_rows, hh], axis=0)
        bl = jnp.concatenate([ll, gap_rows, hl], axis=0)
        rhs = jnp.concatenate([jnp.concatenate([bh, bl], axis=1), jnp.concatenate([bh, corner], axis=1)], axis=0)
        return jnp.concatenate([ch, cl], axis=1), rhs

    for start in starts:
        wind = start < WINDS
        fields = [start + i for i in range(GROUP)]
        columns = [column_stage(f, wind) for f in fields]
        outs = [row_stage(*c) if use_x else None for c in columns]
        ranks = [carry_stage(*c, o) for c, o in zip(columns, outs)]
        for f, o, (lhs, rhs) in zip(fields, outs, ranks):
            out = mm(lhs, rhs)
            total = out[:, :LANES] + out[:, LANES:]
            if use_x:
                total = (o[0] + o[1]) + (o[2] + total)
            for b in range(PARTS):
                lanes = slice(b * LANES, (b + 1) * LANES)
                part = total[b * ROWS:(b + 1) * ROWS]
                if base_ref is not None:
                    part = part + base_ref[f - starts[0], :, lanes]
                out_ref[f - starts[0], :, lanes] = part


def local_filter(table, carry, x, first, count, before, base=None):
    starts = tuple(range(first, first + count, GROUP))
    use_x, use_carry = base is None, carry is not None
    names = ["table"] + ["carry"] * use_carry + ["x"] * use_x + ["base"] * (base is not None) + ["before"]
    arrays = {"table": table, "carry": carry, "x": x, "base": base, "before": before}
    specs = {"before": ANY}

    def body(*refs):
        by_name = dict(zip(names, refs))
        local_filter_kernel(starts, use_x, use_carry, by_name["table"], by_name.get("carry"),
                            by_name.get("x"), by_name.get("base"), refs[len(names)])

    return pl.pallas_call(
        body,
        in_specs=[specs.get(n, VMEM) for n in names],
        out_specs=VMEM,
        out_shape=jax.ShapeDtypeStruct((count, ROWS, COLS), F32),
        compiler_params=params(),
        cost_estimate=pl.CostEstimate(flops=int(count * 30000000), bytes_accessed=count * 150_000, transcendentals=0),
        name="local_filter",
    )(*[arrays[n] for n in names])


PLACE = ((0, 0), (0, 1), (1, 0), (1, 1), (1, 2), (2, 0))


def add_carries(half, table_ref, carry_ref, z_refs, part, store):
    row = fiota((8, LANES), 0)
    up_steps, down_steps = row + 1.0, 8.0 - row
    tables = [carry_ref[side, s, part] for side in range(2) for s in range(SCALES)]
    start = pl.multiple_of((half * 3 + part) * GROUP, GROUP)
    group_facts = table_ref[pl.ds(start, GROUP), :]
    for i in range(GROUP):
        facts = group_facts[i:i + 1, :]
        ups = []
        for s in range(SCALES):
            r = jnp.broadcast_to(facts[:, s:s + 1], (8, LANES))
            w = jnp.broadcast_to(facts[:, SCALES + s:SCALES + s + 1], (8, LANES))
            jump = jnp.exp(-8.0 * r)
            up, down = [w * jnp.exp(-r * up_steps)], [w * jnp.exp(-r * down_steps)]
            for _ in range(ROWS // 8 - 1):
                up.append(up[-1] * jump)
                down.insert(0, down[0] * jump)
            ups.append((jnp.concatenate(up, axis=0), jnp.concatenate(down, axis=0)))
        for b in range(PARTS):
            lanes = slice(b * LANES, (b + 1) * LANES)
            total = jnp.where(half == 0, z_refs[PLACE[part][0]][PLACE[part][1] * GROUP + i, :, lanes],
                              z_refs[PLACE[3 + part][0]][PLACE[3 + part][1] * GROUP + i, :, lanes])
            for s in range(SCALES):
                total = total + ups[s][0] * tables[s][i:i + 1, lanes] + ups[s][1] * tables[SCALES + s][i:i + 1, lanes]
            store(i, lanes, total)


def finish_own_kernel(table_ref, carry_ref, z0_ref, z1_ref, z2_ref, out_ref):
    for part in range(3):
        def store(i, lanes, value):
            out_ref[part * GROUP + i, :, lanes] = value

        add_carries(lat_index() & 1, table_ref, carry_ref, (z0_ref, z1_ref, z2_ref), part, store)


def finish_own(table, carry, parts):
    return pl.pallas_call(
        finish_own_kernel,
        in_specs=[VMEM] * 5,
        out_specs=VMEM,
        out_shape=jax.ShapeDtypeStruct((HALF, ROWS, COLS), F32),
        compiler_params=params(),
        cost_estimate=pl.CostEstimate(flops=1_000_000_000, bytes_accessed=2_000_000, transcendentals=0),
        name="finish_own",
    )(table, carry.reshape(2, SCALES, 3, GROUP, COLS), *parts)


def finish_kernel(table_ref, carry_ref, z0_ref, z1_ref, z2_ref, own_ref, out_ref, buf_ref, sem):
    half = 1 - (lat_index() & 1)
    ready = pltpu.make_async_copy(own_ref, out_ref.at[pl.ds((1 - half) * HALF, HALF)], sem.at[3])
    ready.start()
    copies = [ready]
    for part in range(3):
        def store(i, lanes, value):
            buf_ref[part, i, :, lanes] = value

        add_carries(half, table_ref, carry_ref, (z0_ref, z1_ref, z2_ref), part, store)
        there = out_ref.at[pl.ds((half * 3 + part) * GROUP, GROUP)]
        copies.append(pltpu.make_async_copy(buf_ref.at[part], there, sem.at[part]))
        copies[-1].start()
    for copy in copies:
        copy.wait()


def finish(table, carry, parts, own):
    return pl.pallas_call(
        finish_kernel,
        in_specs=[VMEM] * 6,
        out_specs=HBM,
        out_shape=jax.ShapeDtypeStruct((FIELDS, ROWS, COLS), F32),
        scratch_shapes=[pltpu.VMEM((3, GROUP, ROWS, COLS), F32), pltpu.SemaphoreType.DMA((4,))],
        compiler_params=params(),
        name="finish",
    )(table, carry.reshape(2, SCALES, 3, GROUP, COLS), *parts, own)


def partner(axis, count, bit):
    return functools.partial(lax.ppermute, axis_name=axis, perm=[(i, i ^ bit) for i in range(count)])


def shards(x, lengths, weights):
    facts = jnp.concatenate([lengths.T, weights.T], axis=0)
    sums, edge, table, lanes, held = row_sums(facts, x)
    got = [partner("lon", NLON, d)(sums) for d in (1, 2, 3)]
    early = local_filter(table, None, held, 40, 8, sums)
    winds = wind_sums(table, held, early)
    part, half = lon_merge(lanes, sums, got, winds)
    theirs = partner("lon", NLON, 4)(half)
    local = local_sums(table, held, winds, part)
    steps = lat_steps(table, part)
    carry, keep, send = column_sums(table, lanes, part, theirs, edge, local)
    got_core = partner("lat", NLAT, 1)(send)
    chip = chip_merge(steps, keep, got_core)
    pair = partner("lat", NLAT, 2)(chip)
    z2 = local_filter(table, carry, held, 40, 8, chip, early)
    z0 = local_filter(table, carry, held, 0, 16, z2)
    left, *sends = quad_merge(steps, chip, pair, z0)
    gs = [partner("lat", NLAT, 4 * d)(t) for d, t in zip((1, 2, 3), sends)]
    z1 = local_filter(table, carry, held, 16, 24, left)
    own, other = lat_carry(steps, keep, got_core, pair, left, gs, z1)
    got_carry = partner("lat", NLAT, 1)(other)
    done = finish_own(table, own, (z0, z1, z2))
    return finish(table, got_carry, (z0, z1, z2), done)


def solution(mesh):
    in_specs = (P(None, "lat", "lon"), P(), P())
    out_specs = P(None, "lat", "lon")
    return jax.shard_map(shards, mesh=mesh, in_specs=in_specs, out_specs=out_specs, check_vma=False)
```
